128 devices in a mesh: tm: 32 (over z, x, core), llm: 4 (over y).
Axes of the slice: x: 4, y: 4, z: 4, core: 2. Of those that a mesh axis runs over, the one named last changes fastest.
Arguments:
- audio: bfloat16 [4, 4096, 1536], P('llm', 'tm'), may hold values from -6 to 6
- frame_counts: int32 [4], replicated, may hold values from 2048 to 4096
- text_lengths: int32 [32, 4], replicated, may hold values from 0 to 32
- norm_gain: float32 [1536], replicated, may hold values from 0.25 to 1.75
- w_query: bfloat16 [1536, 1536], replicated, may hold values from -4 to 4, as said below
- w_key: bfloat16 [1536, 1536], replicated, may hold values from -1 to 1, as said below
- w_value: bfloat16 [1536, 1536], replicated, may hold values from -0.15625 to 0.15625
- w_out: bfloat16 [1536, 1536], replicated, may hold values from -0.15625 to 0.15625
- conv_gain: float32 [1536], replicated, may hold values from 0.25 to 1.75
- conv_kernel: float32 [32, 1536], replicated, may hold values from -1 to 1
- latent_gain: float32 [1536], replicated, may hold values from 0.25 to 1.75
- llm_grads: bfloat16 [32, 256, 1536], P('tm', 'llm'), may hold values from -6 to 6
Outputs:
- llm_inputs: bfloat16 [32, 256, 1536], P('tm', 'llm')
- d_audio: bfloat16 [4, 4096, 1536], P('llm', 'tm')
The draws below stay inside these ranges and needn't reach their ends.
Inputs may be any that keep to these rules, and one draw needn't show every extreme that they name: `w_query`: a 1536 x 1536 matrix. `w_key`: a 1536 x 1536 matrix.
All inputs are finite; a program needn't handle non-finite values.
Results may differ from the reference program's by a relative error of at most 0.02.
Values may be sent and summed in bfloat16 or wider, within the bound.
No kernel may reach another device: no remote copies, remote signals or barrier semaphores. Data moves between devices by JAX's collectives and lax.ppermute only.
A program may use at most 128 MiB of HBM per device.

```python
import math
import jax
import jax.numpy as jnp
from jax import lax

D = 1536
HEADS = 16
REACH = 64
KERN = 32
F_DEV = 128
FRAMES = 4096
LLM_LEN = 256
N_TM = 32
N_LLM = 4


def shared_map(key):
    return jax.random.normal(key, (D, D), jnp.float32) * D ** (-0.5)


def draw_w_query(key, part):
    common = shared_map(key)
    key = jax.random.fold_in(key, 7)
    jitter = jax.random.normal(key, (D, D), jnp.float32) * D ** (-0.5)
    blended = 0.6 * common + 0.8 * jitter
    return jnp.clip(blended, -4.0, 4.0).astype(jnp.bfloat16)


def draw_w_key(key, part):
    common = shared_map(key)
    key = jax.random.fold_in(key, 13)
    jitter = jax.random.normal(key, (D, D), jnp.float32) * D ** (-0.5)
    blended = 0.6 * common + 0.8 * jitter
    return jnp.clip(blended, -1.0, 1.0).astype(jnp.bfloat16)


def with_ends(drawn, own_key, low, largest):
    dims = drawn.shape
    spot = [jax.random.randint(jax.random.fold_in(own_key, axis), (), 0, dims[axis]) for axis in range(len(dims))]
    drawn = drawn.at[tuple(spot)].set(low)
    longest = dims.index(max(dims))
    spot[longest] = (spot[longest] + 1) % dims[longest]
    return drawn.at[tuple(spot)].set(largest)


def block_scale(rng, shape, split, smallest, largest):
    factor_of = 1.0
    for dim, shards_of in split:
        draws = jax.random.uniform(jax.random.fold_in(jax.random.fold_in(rng, 6), dim), (shards_of,), jnp.float32, smallest / len(split), largest / len(split))
        factor_of = factor_of * jnp.repeat(jnp.exp(draws), shape[dim] // shards_of).reshape((-1,) + (1,) * (len(shape) - 1 - dim))
    return factor_of


def bell_draw(stream_key, shape, scale, most, shards=(), kind=jnp.bfloat16):
    level = block_scale(stream_key, shape, shards, -0.22, 0.18) if shards else 1.0
    values = jax.random.normal(stream_key, shape, jnp.float32) * scale * level
    return jnp.minimum(jnp.maximum(values, -most), most).astype(kind)


def setup_inputs(seed: int = 0) -> dict:
    key_list = jax.random.split(jax.random.key(seed), 13)
    return {
        "audio": bell_draw(key_list[0], (N_LLM, FRAMES, D), 1.0, 6.0, ((0, 4), (1, 32))),
        "frame_counts": with_ends(jax.random.randint(key_list[1], (N_LLM,), F_DEV * N_TM // 2, F_DEV * N_TM + 1), jax.random.fold_in(key_list[1], 1), F_DEV * N_TM // 2, F_DEV * N_TM).astype(jnp.int32),
        "text_lengths": with_ends(jax.random.randint(key_list[2], (N_TM, N_LLM), 0, F_DEV // 4 + 1), jax.random.fold_in(key_list[2], 1), 0, (F_DEV // 4 + 1) - 1).astype(jnp.int32),
        "norm_gain": jnp.clip(1.0 + 0.15 * jax.random.normal(key_list[3], (D,), jnp.float32), 0.25, 1.75),
        "w_query": draw_w_query(jax.random.fold_in(key_list[12], 71), 0),
        "w_key": draw_w_key(jax.random.fold_in(key_list[12], 71), 0),
        "w_value": bell_draw(key_list[6], (D, D), D ** -0.5, 0.15625),
        "w_out": bell_draw(key_list[7], (D, D), D ** -0.5, 0.15625),
        "conv_gain": jnp.clip(1.0 + 0.15 * jax.random.normal(key_list[8], (D,), jnp.float32), 0.25, 1.75),
        "conv_kernel": bell_draw(key_list[9], (KERN, D), KERN ** -0.5, 1.0, (), jnp.float32),
        "latent_gain": jnp.clip(1.0 + 0.15 * jax.random.normal(key_list[10], (D,), jnp.float32), 0.25, 1.75),
        "llm_grads": bell_draw(key_list[11], (N_TM, LLM_LEN, D), 1.0, 6.0, ((0, 32), (1, 4))),
    }


EPSILON = 1e-06

def normalize(values_in, gain):
    widened = values_in.astype(jnp.float32)
    inverse = lax.rsqrt(lax.optimization_barrier(jnp.mean(widened * widened, axis=-1, keepdims=True)) + EPSILON)
    return widened * inverse * gain

def project(normed, w_query, w_key, w_value):
    queries = jnp.dot(normed, w_query, preferred_element_type=jnp.float32).astype(jnp.bfloat16)
    key_rows = jnp.dot(normed, w_key, preferred_element_type=jnp.float32).astype(jnp.bfloat16)
    value_rows = jnp.dot(normed, w_value, preferred_element_type=jnp.float32).astype(jnp.bfloat16)
    return (queries, key_rows, value_rows)

def attend(queries, key_float, value_float, query_pos, key_pos, frame_limit, frame_total, reach, heads):
    query_count, width = queries.shape
    head_size = width // heads
    query_float = queries.astype(jnp.float32).reshape(query_count, heads, head_size)
    key_heads = key_float.reshape(key_float.shape[0], heads, head_size)
    value_heads = value_float.reshape(value_float.shape[0], heads, head_size)
    scores = jnp.einsum('qhd,khd->hqk', query_float, key_heads) * head_size ** (-0.5)
    lower = key_pos[None, :] >= query_pos[:, None] - reach
    upper = key_pos[None, :] < query_pos[:, None] + reach
    inside = (key_pos >= 0) & (key_pos < frame_total)
    spoken = (key_pos[None, :] < frame_limit) | (key_pos[None, :] == query_pos[:, None])
    allowed = lower & upper & inside[None, :] & spoken
    scores = jnp.where(allowed[None, :, :], scores, -1e+30)
    highest = lax.optimization_barrier(jnp.max(scores, axis=-1, keepdims=True))
    powers = jnp.exp(scores - highest)
    weights = (powers / lax.optimization_barrier(jnp.sum(powers, axis=-1, keepdims=True))).astype(jnp.bfloat16)
    mixture = jnp.einsum('hqk,khd->qhd', weights.astype(jnp.float32), value_heads)
    return mixture.reshape(query_count, width).astype(jnp.bfloat16)

def mix_out(signal, attended, w_out):
    return (signal.astype(jnp.float32) + jnp.dot(attended, w_out, preferred_element_type=jnp.float32)).astype(jnp.bfloat16)

def conv_input(hidden, gain, spoken_rows):
    return (normalize(hidden, gain) * spoken_rows).astype(jnp.bfloat16)

def finish(hidden, padded_float, kernel, gain):
    frame_rows = hidden.shape[0]
    summed = jnp.zeros(hidden.shape, jnp.float32)
    for lag_index in range(kernel.shape[0]):
        summed = summed + kernel[lag_index] * padded_float[lag_index:lag_index + frame_rows]
    updated = hidden.astype(jnp.float32) + jax.nn.silu(summed)
    pooled = lax.optimization_barrier(jnp.mean(updated.reshape(frame_rows // 4, 4, updated.shape[1]), axis=1))
    return normalize(pooled, gain).astype(jnp.bfloat16)

def route_positions(frame_counts, text_lengths, pooled_dev):
    slice_index = jnp.arange(text_lengths.shape[0], dtype=jnp.int32)[:, None]
    live_rows = jnp.clip(frame_counts[None, :] // 4 - slice_index * pooled_dev, 0, pooled_dev).astype(jnp.int32)
    starts = (jnp.cumsum(text_lengths + live_rows, axis=1) - live_rows).astype(jnp.int32)
    row_index = jnp.arange(pooled_dev, dtype=jnp.int32)
    placed = starts[:, :, None] + row_index[None, None, :]
    return jnp.where(row_index[None, None, :] < live_rows[:, :, None], placed, -1).astype(jnp.int32)

def reference(audio, frame_counts, text_lengths, norm_gain, w_query, w_key, w_value, w_out, conv_gain, conv_kernel, latent_gain, llm_grads):
    block_rows = math.gcd(FRAMES, 512)
    block_count = FRAMES // block_rows
    pooled_dev = F_DEV // 4
    side = KERN // 2

    def forward_one(signal, frame_limit):
        normed = normalize(signal, norm_gain).astype(jnp.bfloat16)
        queries, key_rows, value_rows = project(normed, w_query, w_key, w_value)
        key_padded = jnp.pad(key_rows.astype(jnp.float32), ((REACH, REACH), (0, 0)))
        value_padded = jnp.pad(value_rows.astype(jnp.float32), ((REACH, REACH), (0, 0)))

        def one_block(block_index):
            offset = block_index * block_rows
            query_pos = offset + jnp.arange(block_rows, dtype=jnp.int32)
            key_pos = offset - REACH + jnp.arange(block_rows + 2 * REACH, dtype=jnp.int32)
            return attend(lax.dynamic_slice_in_dim(queries, offset, block_rows, 0), lax.dynamic_slice_in_dim(key_padded, offset, block_rows + 2 * REACH, 0), lax.dynamic_slice_in_dim(value_padded, offset, block_rows + 2 * REACH, 0), query_pos, key_pos, frame_limit, FRAMES, REACH, HEADS)
        attended = lax.map(one_block, jnp.arange(block_count, dtype=jnp.int32)).reshape(FRAMES, D)
        hidden = mix_out(signal, attended, w_out)
        spoken_rows = (jnp.arange(FRAMES, dtype=jnp.int32) < frame_limit).astype(jnp.float32)[:, None]
        conv_in = conv_input(hidden, conv_gain, spoken_rows)
        padded = jnp.pad(conv_in.astype(jnp.float32), ((side, side), (0, 0)))
        return finish(hidden, padded, conv_kernel, latent_gain)

    def forward(signal):
        return jax.vmap(forward_one)(signal, frame_counts)
    latents, pullback = jax.vjp(forward, audio)
    positions = route_positions(frame_counts, text_lengths, pooled_dev)
    flat = positions.reshape(N_TM, N_LLM * pooled_dev)
    select = (flat[:, None, :] == jnp.arange(LLM_LEN, dtype=jnp.int32)[None, :, None]).astype(jnp.float32)
    by_slice = latents.reshape(N_LLM, N_TM, pooled_dev, D).transpose(1, 0, 2, 3).reshape(N_TM, N_LLM * pooled_dev, D)
    llm_inputs = jnp.einsum('tlr,trd->tld', select, by_slice.astype(jnp.float32)).astype(jnp.bfloat16)
    returned = jnp.einsum('tlr,tld->trd', select, llm_grads.astype(jnp.float32)).astype(jnp.bfloat16)
    returned = returned.reshape(N_TM, N_LLM, pooled_dev, D).transpose(1, 0, 2, 3).reshape(N_LLM, FRAMES // 4, D)
    d_audio = pullback(returned)[0]
    return (llm_inputs, d_audio)
```

```python
import functools

import jax
import jax.numpy as jnp
from jax import lax
from jax.experimental import pallas as pl
from jax.experimental.pallas import tpu as pltpu
from jax.sharding import PartitionSpec as P

D = 1536
REACH = 64
KERN = 32
FR = 128
HALO = 96
EXT = FR + 2 * HALO
QR = FR + 64
SR = FR + 32
PR = SR // 4
LR = FR // 4
SLOTS = 64
NREC = 4
HEAD = 96
LANE = 128
NB = D // LANE
COL = 256
NC = D // COL
GROUP = 4 * HEAD
EPSILON = 1e-06
SCALE = HEAD ** (-0.5)
BF = jnp.bfloat16
F32 = jnp.float32
WINDOWS = ((0, 1), (0, 2), (1, 3), (2, 3))

ANY = pl.BlockSpec(memory_space=pl.ANY)
SMEM = pl.BlockSpec(memory_space=pltpu.SMEM)


def dot(a, b):
    return lax.dot_general(a, b, (((1,), (0,)), ((), ())), preferred_element_type=F32)


def dot_t(a, b):
    return lax.dot_general(a, b, (((1,), (1,)), ((), ())), preferred_element_type=F32)


def t_dot(a, b):
    return lax.dot_general(a, b, (((0,), (0,)), ((), ())), preferred_element_type=F32)


def lanes(c, width=LANE):
    return pl.ds(pl.multiple_of(c * width, width), width)


def routes(fc, tl, slice_index):
    starts, lives = [], []
    total = 0
    for b in range(NREC):
        live = jnp.clip(fc[b] // 4 - slice_index * LR, 0, LR)
        total = total + tl[slice_index, b]
        starts.append(total)
        lives.append(live)
        total = total + live
    return starts, lives


def pick(values, index):
    out = values[0]
    for b in range(1, NREC):
        out = jnp.where(index == b, values[b], out)
    return out


def prepare(fc, tl, audio, grads, send_a, send_b, o0, o1, o2, o3, g_buf, o_buf, sems):
    tm = lax.axis_index("tm")
    llm = lax.axis_index("llm")
    off_a = (1 - tm % 2) * (FR - HALO)
    off_b = (FR - HALO) - off_a
    ca = pltpu.make_async_copy(audio.at[pl.ds(pl.multiple_of(off_a, 32), HALO)], send_a, sems.at[0])
    cb = pltpu.make_async_copy(audio.at[pl.ds(pl.multiple_of(off_b, 32), HALO)], send_b, sems.at[1])
    cg = pltpu.make_async_copy(grads, g_buf, sems.at[2])
    cg.start()
    ca.start()
    cb.start()
    starts, lives = routes(fc, tl, tm)
    row = lax.broadcasted_iota(jnp.int32, (LR, SLOTS), 0)
    slot = lax.broadcasted_iota(jnp.int32, (LR, SLOTS), 1) + llm * SLOTS
    cg.wait()
    copies = []
    for j, out in enumerate((o0, o1, o2, o3)):
        b = llm ^ j
        chosen = (row < pick(lives, b)) & (slot == row + pick(starts, b))
        o_buf[j] = dot(jnp.where(chosen, 1.0, 0.0).astype(BF), g_buf[...]).astype(BF)
        copy = pltpu.make_async_copy(o_buf.at[j], out, sems.at[3 + j])
        copy.start()
        copies.append(copy)
    for copy in [ca, cb] + copies:
        copy.wait()


def main_kernel(
    fc, audio, recv_a, recv_b, lat_grad, edge_a, edge_b, w_query, w_key, w_value, w_out,
    norm_gain, conv_gain, latent_gain, taps,
    latent_out, dhid_out, dn_out, send_a, send_b,
    x_s, n_s, q_s, k_s, v_s, wq_s, wk_s, wv_s, wo_s, ng_s, cg_s, lg_s, tap_s,
    att_s, p_s, bias_s, biasl_s, biasr_s, h_s, ci_s, dsilu_s, up_s, pool_s, g_s, gst_s, norm_t, lat_s,
    ds_s, us_s, dnc_s, dhid_s, datt_s, dq_s, dk_s, dv_s, dn_s, edge_s, w_sems, sems,
):
    tm = lax.axis_index("tm")
    llm = lax.axis_index("llm")
    n_tm = lax.axis_size("tm")
    even = tm % 2 == 0
    parity = tm % 2
    first = tm * FR
    total = n_tm * FR
    limit = fc[llm]

    left_row = pl.multiple_of((1 - parity) * (HALO + FR), 32)
    right_row = pl.multiple_of(parity * (HALO + FR), 32)
    small = [
        pltpu.make_async_copy(audio, x_s.at[pl.ds(HALO, FR)], sems.at[0]),
        pltpu.make_async_copy(recv_a, x_s.at[pl.ds(left_row, HALO)], sems.at[1]),
        pltpu.make_async_copy(recv_b, x_s.at[pl.ds(right_row, HALO)], sems.at[2]),
        pltpu.make_async_copy(norm_gain, ng_s, sems.at[3]),
    ]
    late = [
        pltpu.make_async_copy(conv_gain, cg_s, sems.at[4]),
        pltpu.make_async_copy(latent_gain, lg_s, sems.at[5]),
        pltpu.make_async_copy(taps, tap_s, sems.at[6]),
        pltpu.make_async_copy(lat_grad, gst_s.at[pl.ds(16, LR)], sems.at[7]),
        pltpu.make_async_copy(edge_a, gst_s.at[pl.ds(pl.multiple_of((1 - parity) * 48, 16), 16)], sems.at[8]),
        pltpu.make_async_copy(edge_b, gst_s.at[pl.ds(pl.multiple_of(parity * 48, 16), 16)], sems.at[9]),
    ]
    for copy in small:
        copy.start()

    def w_copy(n, j):
        src = (w_key, w_value, w_query, w_out)[n]
        dst = (wk_s, wv_s, wq_s, wo_s)[n]
        return pltpu.make_async_copy(src.at[:, lanes(j, COL)], dst.at[:, lanes(j, COL)], w_sems.at[n, j])

    for n in range(4):
        for j in range(NC):
            w_copy(n, j).start()
    for copy in late:
        copy.start()

    def bias_of(rows, cols, q_first, k_first):
        qe = lax.broadcasted_iota(jnp.int32, (rows, cols), 0) + q_first
        ke = lax.broadcasted_iota(jnp.int32, (rows, cols), 1) + k_first
        kt = ke + (first - HALO)
        ok = (ke >= qe - REACH) & (ke < qe + REACH) & (kt >= 0) & (kt < total) & ((kt < limit) | (ke == qe))
        return jnp.where(ok, 0.0, -1e30)

    bias_s[...] = bias_of(FR, 256, HALO, 32)
    biasl_s[...] = bias_of(32, 160, 64, 0)
    biasr_s[...] = bias_of(32, 160, 224, 160)

    for copy in small:
        copy.wait()

    @pl.loop(0, EXT // 64)
    def _(r):
        rows = pl.ds(pl.multiple_of(r * 64, 64), 64)
        x = x_s[rows, :].astype(F32)
        inv = lax.rsqrt(jnp.mean(x * x, axis=-1, keepdims=True) + EPSILON)
        n_s[rows, :] = (x * inv * ng_s[...]).astype(BF)

    for n, (w_s, out_s, lo, hi) in enumerate(
        ((wk_s, k_s, 0, EXT), (wv_s, v_s, 0, EXT), (wq_s, q_s, 64, 64 + QR))
    ):
        @pl.loop(0, NC)
        def _(j, n=n, w_s=w_s, out_s=out_s, lo=lo, hi=hi):
            w_copy(n, j).wait()
            out_s[:, lanes(j, COL)] = dot(n_s[lo:hi, :], w_s[:, lanes(j, COL)]).astype(BF)

    lane_of = lax.broadcasted_iota(jnp.int32, (1, GROUP), 1)

    def head_mask(j, lo, hi):
        lane = lane_of[:, : (hi - lo) * LANE] + lo * LANE
        return jnp.where((lane >= j * HEAD) & (lane < (j + 1) * HEAD), 1.0, 0.0).astype(BF)

    def softmax(scores):
        powers = jnp.exp(scores - jnp.max(scores, axis=-1, keepdims=True))
        return powers * (1.0 / jnp.sum(powers, axis=-1, keepdims=True))

    def window(g, lo, hi):
        return pl.ds(pl.multiple_of(g * GROUP + lo * LANE, LANE), (hi - lo) * LANE)

    def add_tiles(tiles, lo, value):
        for t in range(value.shape[1] // LANE):
            part = value[:, t * LANE : (t + 1) * LANE]
            tiles[lo + t] = part if tiles[lo + t] is None else tiles[lo + t] + part

    @pl.loop(0, 4)
    def _(g):
        own, left, right = [None] * 3, [None] * 3, [None] * 3
        for j, (lo, hi) in enumerate(WINDOWS):
            win = window(g, lo, hi)
            mask = head_mask(j, lo, hi)
            q = q_s[:, win] * mask
            k = k_s[:, win]
            v = v_s[:, win] * mask
            p = softmax(dot_t(q[32:160], k[32:288]) * SCALE + bias_s[...]).astype(BF)
            p_s[g * 4 + j] = p
            add_tiles(own, lo, dot(p, v[32:288]))
            p = softmax(dot_t(q[0:32], k[0:160]) * SCALE + biasl_s[...]).astype(BF)
            add_tiles(left, lo, dot(p, v[0:160]))
            p = softmax(dot_t(q[160:192], k[160:320]) * SCALE + biasr_s[...]).astype(BF)
            add_tiles(right, lo, dot(p, v[160:320]))
        for t in range(3):
            at = window(g, t, t + 1)
            att_s[0:32, at] = left[t].astype(BF)
            att_s[32:160, at] = own[t].astype(BF)
            att_s[160:192, at] = right[t].astype(BF)

    def hidden_step(j, squares):
        w_copy(3, j).wait()
        cols = lanes(j, COL)
        h = dot(att_s[...], wo_s[:, cols]) + x_s[64 : 64 + QR, cols].astype(F32)
        h = h.astype(BF).astype(F32)
        h_s[2 * j] = h[:, :LANE]
        h_s[2 * j + 1] = h[:, LANE:]
        return squares + h[:, :LANE] * h[:, :LANE] + h[:, LANE:] * h[:, LANE:]

    squares = lax.fori_loop(0, NC, hidden_step, jnp.zeros((QR, LANE), F32))
    inv_h = lax.rsqrt(jnp.sum(squares, axis=-1, keepdims=True) * (1.0 / D) + EPSILON)
    frame = lax.broadcasted_iota(jnp.int32, (QR, 1), 0) + (first - 32)
    spoken = jnp.where((frame >= 0) & (frame < limit), 1.0, 0.0)
    inv_spoken = inv_h * spoken

    for copy in late:
        copy.wait()

    row = lax.broadcasted_iota(jnp.int32, (PR, 64), 0)
    col = lax.broadcasted_iota(jnp.int32, (PR, 64), 1)
    at = tm * LR + row - 4
    chosen = (col == row + 12) & (at >= 0) & (at < n_tm * LR)
    g_s[...] = dot(jnp.where(chosen, 1.0, 0.0).astype(BF), gst_s[...])

    def conv_step(c, carry):
        squares, along = carry
        cols = lanes(c)
        ci_s[...] = (h_s[c] * inv_spoken * cg_s[:, cols]).astype(BF).astype(F32)
        kern = tap_s[:, cols]
        acc = jnp.zeros((SR, LANE), F32)
        for s in range(8):
            xs = ci_s[s : s + SR + 24, :]
            for u in range(4):
                m = s + 8 * u
                acc = acc + kern[m : m + 1, :] * xs[8 * u : 8 * u + SR]
        sig = 1.0 / (1.0 + jnp.exp(-acc))
        silu = acc * sig
        dsilu_s[c] = sig + silu * (1.0 - sig)
        up_s[...] = h_s[c, 16 : 16 + SR, :] + silu
        pooled = up_s[pl.ds(0, PR, 4), :]
        for u in range(1, 4):
            pooled = pooled + up_s[pl.ds(u, PR, 4), :]
        pooled = pooled * 0.25
        pool_s[c] = pooled
        return squares + pooled * pooled, along + g_s[:, cols] * lg_s[:, cols] * pooled

    zero = jnp.zeros((PR, LANE), F32)
    squares, along = lax.fori_loop(0, NB, conv_step, (zero, zero))
    inv_p = lax.rsqrt(jnp.sum(squares, axis=-1, keepdims=True) * (1.0 / D) + EPSILON)
    back_p = inv_p * inv_p * inv_p * (jnp.sum(along, axis=-1, keepdims=True) * (1.0 / D))

    inv_own = inv_h[32:160]
    spoken_own = spoken[32:160]

    def conv_back(c, along):
        cols = lanes(c)
        pooled = pool_s[c]
        gain = lg_s[:, cols]
        norm_t[...] = pooled * inv_p * gain
        lat_s[:, cols] = norm_t[4:36, :].astype(BF)
        dpool = (g_s[:, cols] * gain * inv_p - pooled * back_p) * 0.25
        for u in range(4):
            up_s[pl.ds(u, PR, 4), :] = dpool
        ds_s[...] = up_s[...] * dsilu_s[c]
        us_s[c] = up_s[16 : 16 + FR, :]
        kern = tap_s[:, cols]
        acc = jnp.zeros((FR, LANE), F32)
        for s in range(8):
            base = 8 if s == 0 else s
            xs = ds_s[base : base + FR + 24, :]
            for u in range(4):
                m = 32 - base - 8 * u
                acc = acc + kern[m : m + 1, :] * xs[8 * u : 8 * u + FR]
        dn = acc.astype(BF).astype(F32) * spoken_own * cg_s[:, cols]
        dnc_s[c] = dn
        return along + dn * h_s[c, 32:160, :]

    along = lax.fori_loop(0, NB, conv_back, jnp.zeros((FR, LANE), F32))
    latent_copy = pltpu.make_async_copy(lat_s, latent_out, sems.at[10])
    latent_copy.start()
    back_h = inv_own * inv_own * inv_own * (jnp.sum(along, axis=-1, keepdims=True) * (1.0 / D))

    @pl.loop(0, NB)
    def _(c):
        dhid_s[:, lanes(c)] = (us_s[c] + dnc_s[c] * inv_own - h_s[c, 32:160, :] * back_h).astype(BF)

    dhid_copy = pltpu.make_async_copy(dhid_s, dhid_out, sems.at[11])
    dhid_copy.start()

    @pl.loop(0, NC)
    def _(j):
        datt_s[:, lanes(j, COL)] = dot_t(dhid_s[...], wo_s[lanes(j, COL), :]).astype(BF)

    @pl.loop(0, 4)
    def _(g):
        dq, dk, dv = [None] * 3, [None] * 3, [None] * 3
        for j, (lo, hi) in enumerate(WINDOWS):
            win = window(g, lo, hi)
            mask = head_mask(j, lo, hi)
            q = q_s[32:160, win] * mask
            k = k_s[32:288, win] * mask
            v = v_s[32:288, win]
            do = datt_s[:, win] * mask
            p = p_s[g * 4 + j]
            dp = dot_t(do, v)
            pf = p.astype(F32)
            pd = pf * dp
            ds = ((pd - pf * jnp.sum(pd, axis=-1, keepdims=True)) * SCALE).astype(BF)
            add_tiles(dq, lo, dot(ds, k))
            add_tiles(dk, lo, t_dot(ds, q))
            add_tiles(dv, lo, t_dot(p, do))
        for t in range(3):
            at = window(g, t, t + 1)
            dq_s[:, at] = dq[t].astype(BF)
            dk_s[:, at] = dk[t].astype(BF)
            dv_s[:, at] = dv[t].astype(BF)

    @pl.loop(0, NC)
    def _(j):
        cols = lanes(j, COL)
        both = dot_t(dk_s[...], wk_s[cols, :]) + dot_t(dv_s[...], wv_s[cols, :])
        dn_s[:, cols] = both[64:192] + dot_t(dq_s[...], wq_s[cols, :])
        edge_s[0:64, cols] = both[0:64].astype(BF)
        edge_s[64:128, cols] = both[192:256].astype(BF)

    row_a = pl.multiple_of((1 - parity) * 64, 64)
    row_b = pl.multiple_of(parity * 64, 64)
    outs = [
        pltpu.make_async_copy(edge_s.at[pl.ds(row_a, 64)], send_a, sems.at[12]),
        pltpu.make_async_copy(edge_s.at[pl.ds(row_b, 64)], send_b, sems.at[13]),
        pltpu.make_async_copy(dn_s, dn_out, sems.at[14]),
    ]
    for copy in outs:
        copy.start()
    for copy in [latent_copy, dhid_copy] + outs:
        copy.wait()


def finish(
    fc, tl, audio, dhid, dn, recv_a, recv_b, l0, l1, l2, l3, norm_gain,
    rows_out, grad_out,
    x_s, dh_s, dn_s, r_s, lat_s, ng_s, out_s, rows_s, sems,
):
    tm = lax.axis_index("tm")
    llm = lax.axis_index("llm")
    parity = tm % 2
    copies = [
        pltpu.make_async_copy(audio, x_s, sems.at[0]),
        pltpu.make_async_copy(dhid, dh_s, sems.at[1]),
        pltpu.make_async_copy(dn, dn_s, sems.at[2]),
        pltpu.make_async_copy(recv_a, r_s.at[pl.ds(pl.multiple_of((1 - parity) * 64, 64), 64)], sems.at[3]),
        pltpu.make_async_copy(recv_b, r_s.at[pl.ds(pl.multiple_of(parity * 64, 64), 64)], sems.at[4]),
        pltpu.make_async_copy(norm_gain, ng_s, sems.at[5]),
    ]
    lat_copies = [
        pltpu.make_async_copy(source, lat_s.at[pl.ds(j * LR, LR)], sems.at[6 + j])
        for j, source in enumerate((l0, l1, l2, l3))
    ]
    for copy in copies + lat_copies:
        copy.start()
    starts, lives = routes(fc, tl, tm)
    slot = lax.broadcasted_iota(jnp.int32, (SLOTS, NREC * LR), 0) + llm * SLOTS
    col = lax.broadcasted_iota(jnp.int32, (SLOTS, NREC * LR), 1)
    chosen = jnp.zeros((SLOTS, NREC * LR), F32)
    for j in range(NREC):
        b = llm ^ j
        r = col - j * LR
        hit = (r >= 0) & (r < pick(lives, b)) & (slot == r + pick(starts, b))
        chosen = jnp.where(hit, 1.0, chosen)
    for copy in copies:
        copy.wait()
    keep_left = jnp.where(tm > 0, 1.0, 0.0)
    keep_right = jnp.where(tm < lax.axis_size("tm") - 1, 1.0, 0.0)
    for half in range(2):
        rows = slice(half * 64, half * 64 + 64)
        keep = keep_left if half == 0 else keep_right
        x = x_s[rows, :].astype(F32)
        inv = lax.rsqrt(jnp.mean(x * x, axis=-1, keepdims=True) + EPSILON)
        g = (dn_s[rows, :] + r_s[rows, :].astype(F32) * keep).astype(BF).astype(F32) * ng_s[...]
        back = inv * inv * inv * jnp.mean(g * x, axis=-1, keepdims=True)
        out_s[rows, :] = (dh_s[rows, :].astype(F32) + g * inv - x * back).astype(BF)
    grad_copy = pltpu.make_async_copy(out_s, grad_out, sems.at[10])
    grad_copy.start()
    for copy in lat_copies:
        copy.wait()
    rows_s[...] = dot(chosen.astype(BF), lat_s[...]).astype(BF)
    rows_copy = pltpu.make_async_copy(rows_s, rows_out, sems.at[11])
    rows_copy.start()
    grad_copy.wait()
    rows_copy.wait()


def swap(count, cells_a, cells_b):
    pairs_a = [(i, i ^ 1) for i in range(count)]
    pairs_b = [(i, min(max(((i + 1) ^ 1) - 1, 0), count - 1)) for i in range(count)]
    return lax.ppermute(cells_a, "tm", pairs_a), lax.ppermute(cells_b, "tm", pairs_b)


def exchange(count, cells):
    return [
        lax.ppermute(cells[j], "llm", [(i, i ^ j) for i in range(count)]) for j in range(1, count)
    ]


def call(kernel, outs, scratch, specs, name, limit, flops):
    return pl.pallas_call(
        kernel,
        out_shape=outs,
        in_specs=specs,
        out_specs=[ANY] * len(outs),
        scratch_shapes=scratch,
        compiler_params=pltpu.CompilerParams(vmem_limit_bytes=limit),
        cost_estimate=pl.CostEstimate(flops=flops, bytes_accessed=4_000_000, transcendentals=0),
        name=name,
    )


def shape(rows, dtype=BF, cols=D):
    return jax.ShapeDtypeStruct((rows, cols), dtype)


MIB = 1024 * 1024


def on_device(
    audio, frame_counts, text_lengths, norm_gain, w_query, w_key, w_value, w_out,
    conv_gain, conv_kernel, latent_gain, llm_grads,
):
    signal = audio[0]
    n_tm = lax.axis_size("tm")
    n_llm = lax.axis_size("llm")
    norm_row, conv_row, latent_row = (g.reshape(1, D) for g in (norm_gain, conv_gain, latent_gain))
    V = pltpu.VMEM
    dma = pltpu.SemaphoreType.DMA

    send_a, send_b, o0, o1, o2, o3 = call(
        prepare,
        [shape(HALO)] * 2 + [shape(LR)] * 4,
        [V((SLOTS, D), BF), V((NREC, LR, D), BF), dma((7,))],
        [SMEM, SMEM, ANY, ANY],
        "prepare", 8 * MIB, 10_000_000,
    )(frame_counts, text_lengths, signal, llm_grads[0])
    recv_a, recv_b = swap(n_tm, send_a, send_b)
    came = exchange(n_llm, [o0, o1, o2, o3])
    lat_grad = o0 + came[0] + came[1] + came[2]
    even = lax.axis_index("tm") % 2 == 0
    edge_a, edge_b = swap(
        n_tm,
        jnp.where(even, lat_grad[16:], lat_grad[:16]),
        jnp.where(even, lat_grad[:16], lat_grad[16:]),
    )

    latent, dhid, dn, back_a, back_b = call(
        main_kernel,
        [shape(LR), shape(FR), shape(FR, F32), shape(64), shape(64)],
        [
            V((EXT, D), BF), V((EXT, D), BF), V((QR, D), BF), V((EXT, D), BF), V((EXT, D), BF),
            V((D, D), BF), V((D, D), BF), V((D, D), BF), V((D, D), BF),
            V((1, D), F32), V((1, D), F32), V((1, D), F32), V((KERN, D), F32),
            V((QR, D), BF), V((16, FR, 256), BF), V((FR, 256), F32), V((32, 160), F32), V((32, 160), F32),
            V((NB, QR, LANE), F32), V((QR, LANE), F32), V((NB, SR, LANE), F32), V((SR, LANE), F32),
            V((NB, PR, LANE), F32), V((PR, D), F32), V((64, D), BF), V((PR, LANE), F32), V((LR, D), BF),
            V((SR, LANE), F32), V((NB, FR, LANE), F32), V((NB, FR, LANE), F32), V((FR, D), BF),
            V((FR, D), BF), V((FR, D), BF), V((256, D), BF), V((256, D), BF), V((FR, D), F32), V((FR, D), BF),
            dma((4, NC)), dma((15,)),
        ],
        [SMEM] + [ANY] * 14,
        "main", 50 * MIB, 10_000_000_000,
    )(
        frame_counts, signal, recv_a, recv_b, lat_grad, edge_a, edge_b,
        w_query, w_key, w_value, w_out, norm_row, conv_row, latent_row, conv_kernel,
    )
    ret_a, ret_b = swap(n_tm, back_a, back_b)
    others = exchange(n_llm, [latent] * n_llm)
    rows, grad = call(
        finish,
        [shape(SLOTS), shape(FR)],
        [
            V((FR, D), BF), V((FR, D), BF), V((FR, D), F32), V((FR, D), BF), V((NREC * LR, D), BF),
            V((1, D), F32), V((FR, D), BF), V((SLOTS, D), BF), dma((12,)),
        ],
        [SMEM, SMEM] + [ANY] * 10,
        "finish", 8 * MIB, 10_000_000,
    )(frame_counts, text_lengths, signal, dhid, dn, ret_a, ret_b, latent, *others, norm_row)
    return (rows[None], grad[None])


def solution(mesh):
    placed = (P("llm", "tm", None),) + (P(),) * 10 + (P("tm", "llm", None),)
    return jax.shard_map(
        on_device,
        mesh=mesh,
        in_specs=placed,
        out_specs=(P("tm", "llm", None), P("llm", "tm", None)),
        check_vma=False,
    )
```

```python
import functools

import jax
import jax.numpy as jnp
from jax import lax
from jax.experimental import pallas as pl
from jax.experimental.pallas import tpu as pltpu
from jax.sharding import PartitionSpec as P

D = 1536
REACH = 64
KERN = 32
FR = 128
HALO = 96
EXT = FR + 2 * HALO
QR = FR + 64
SR = FR + 32
PR = SR // 4
LR = FR // 4
SLOTS = 64
NREC = 4
HEAD = 96
LANE = 128
NB = D // LANE
COL = 768
NC = D // COL
GROUP = 4 * HEAD
EPSILON = 1e-06
SCALE = HEAD ** (-0.5)
BF = jnp.bfloat16
F32 = jnp.float32
WINDOWS = ((0, 1), (0, 2), (1, 3), (2, 3))

ANY = pl.BlockSpec(memory_space=pl.ANY)


def dot(a, b):
    return lax.dot_general(a, b, (((1,), (0,)), ((), ())), preferred_element_type=F32)


def dot_t(a, b):
    return lax.dot_general(a, b, (((1,), (1,)), ((), ())), preferred_element_type=F32)


def t_dot(a, b):
    return lax.dot_general(a, b, (((0,), (0,)), ((), ())), preferred_element_type=F32)


def lanes(c, width=LANE):
    return pl.ds(pl.multiple_of(c * width, width), width)


def routes(fc, tl, slice_index):
    starts, lives = [], []
    total = 0
    for b in range(NREC):
        live = jnp.clip(fc[b] // 4 - slice_index * LR, 0, LR)
        total = total + tl[b, slice_index]
        starts.append(total)
        lives.append(live)
        total = total + live
    return starts, lives


def pick(values, index):
    out = values[0]
    for b in range(1, NREC):
        out = jnp.where(index == b, values[b], out)
    return out


def prepare(fc_in, tl_in, audio, grads, send_a, send_b, o0, o1, o2, o3, fc, tl, g_buf, o_buf, sems):
    cf = pltpu.make_async_copy(fc_in, fc, sems.at[7])
    ct = pltpu.make_async_copy(tl_in, tl, sems.at[8])
    cf.start()
    ct.start()
    tm = lax.axis_index("tm")
    llm = lax.axis_index("llm")
    off_a = (1 - tm % 2) * (FR - HALO)
    off_b = (FR - HALO) - off_a
    ca = pltpu.make_async_copy(audio.at[pl.ds(pl.multiple_of(off_a, 32), HALO)], send_a, sems.at[0])
    cb = pltpu.make_async_copy(audio.at[pl.ds(pl.multiple_of(off_b, 32), HALO)], send_b, sems.at[1])
    cg = pltpu.make_async_copy(grads, g_buf, sems.at[2])
    cg.start()
    ca.start()
    cb.start()
    cf.wait()
    ct.wait()
    starts, lives = routes(fc, tl, tm)
    row = lax.broadcasted_iota(jnp.int32, (LR, SLOTS), 0)
    slot = lax.broadcasted_iota(jnp.int32, (LR, SLOTS), 1) + llm * SLOTS
    cg.wait()
    copies = []
    for j, out in enumerate((o0, o1, o2, o3)):
        b = llm ^ j
        chosen = (row < pick(lives, b)) & (slot == row + pick(starts, b))
        o_buf[j] = dot(jnp.where(chosen, 1.0, 0.0).astype(BF), g_buf[...]).astype(BF)
        copy = pltpu.make_async_copy(o_buf.at[j], out, sems.at[3 + j])
        copy.start()
        copies.append(copy)
    for copy in [ca, cb] + copies:
        copy.wait()


def main_kernel(
    fc_in, audio, recv_a, recv_b, lat_grad, edge_a, edge_b, w_query, w_key, w_value, w_out,
    norm_gain, conv_gain, latent_gain, taps,
    latent_out, dhid_out, dn_out, send_a, send_b,
    fc, x_s, n_s, q_s, k_s, v_s, wq_s, wk_s, wv_s, wo_s, ng_s, cg_s, lg_s, tap_s,
    att_s, p_s, bias_s, h_s, ci_s, dsilu_s, up_s, pool_s, g_s, gst_s, norm_t, lat_s,
    ds_s, us_s, dnc_s, dhid_s, datt_s, dq_s, dk_s, dv_s, dn_s, edge_s, w_sems, sems,
):
    tm = lax.axis_index("tm")
    llm = lax.axis_index("llm")
    n_tm = lax.axis_size("tm")
    even = tm % 2 == 0
    parity = tm % 2
    first = tm * FR
    total = n_tm * FR
    fc_copy = pltpu.make_async_copy(fc_in, fc, sems.at[15])
    fc_copy.start()

    left_row = pl.multiple_of((1 - parity) * (HALO + FR), 32)
    right_row = pl.multiple_of(parity * (HALO + FR), 32)
    small = [
        pltpu.make_async_copy(audio, x_s.at[pl.ds(HALO, FR)], sems.at[0]),
        pltpu.make_async_copy(recv_a, x_s.at[pl.ds(left_row, HALO)], sems.at[1]),
        pltpu.make_async_copy(recv_b, x_s.at[pl.ds(right_row, HALO)], sems.at[2]),
        pltpu.make_async_copy(norm_gain, ng_s, sems.at[3]),
    ]
    late = [
        pltpu.make_async_copy(conv_gain, cg_s, sems.at[4]),
        pltpu.make_async_copy(latent_gain, lg_s, sems.at[5]),
        pltpu.make_async_copy(taps, tap_s, sems.at[6]),
        pltpu.make_async_copy(lat_grad, gst_s.at[pl.ds(16, LR)], sems.at[7]),
        pltpu.make_async_copy(edge_a, gst_s.at[pl.ds(pl.multiple_of((1 - parity) * 48, 16), 16)], sems.at[8]),
        pltpu.make_async_copy(edge_b, gst_s.at[pl.ds(pl.multiple_of(parity * 48, 16), 16)], sems.at[9]),
    ]
    for copy in small:
        copy.start()

    def w_copy(n, j):
        src = (w_key, w_value, w_query, w_out)[n]
        dst = (wk_s, wv_s, wq_s, wo_s)[n]
        return pltpu.make_async_copy(src.at[:, lanes(j, COL)], dst.at[:, lanes(j, COL)], w_sems.at[n, j])

    for n in range(4):
        for j in range(NC):
            w_copy(n, j).start()
    for copy in late:
        copy.start()

    fc_copy.wait()
    limit = fc[llm]

    def bias_of(rows, cols, q_first, k_first):
        qe = lax.broadcasted_iota(jnp.int32, (rows, cols), 0) + q_first
        ke = lax.broadcasted_iota(jnp.int32, (rows, cols), 1) + k_first
        kt = ke + (first - HALO)
        ok = (ke >= qe - REACH) & (ke < qe + REACH) & (kt >= 0) & (kt < total) & ((kt < limit) | (ke == qe))
        return jnp.where(ok, 0.0, -1e30)

    bias_s[0:32, :] = bias_of(32, 256, 64, 0)
    bias_s[32:160, :] = bias_of(FR, 256, HALO, 32)
    bias_s[160:192, :] = bias_of(32, 256, 224, 64)

    for copy in small:
        copy.wait()

    @pl.loop(0, EXT // 64)
    def _(r):
        rows = pl.ds(pl.multiple_of(r * 64, 64), 64)
        x = x_s[rows, :].astype(F32)
        inv = lax.rsqrt(jnp.mean(x * x, axis=-1, keepdims=True) + EPSILON)
        for c in range(NB):
            cols = slice(c * LANE, (c + 1) * LANE)
            n_s[rows, cols] = (x[:, cols] * inv * ng_s[c : c + 1, :]).astype(BF)

    for n, (w_s, out_s, lo, hi) in enumerate(
        ((wk_s, k_s, 0, EXT), (wv_s, v_s, 0, EXT), (wq_s, q_s, 64, 64 + QR))
    ):
        @pl.loop(0, NC)
        def _(j, n=n, w_s=w_s, out_s=out_s, lo=lo, hi=hi):
            w_copy(n, j).wait()
            out_s[:, lanes(j, COL)] = dot(n_s[lo:hi, :], w_s[:, lanes(j, COL)]).astype(BF)

    lane_of = lax.broadcasted_iota(jnp.int32, (1, GROUP), 1)

    def head_mask(j, lo, hi):
        lane = lane_of[:, : (hi - lo) * LANE] + lo * LANE
        return jnp.where((lane >= j * HEAD) & (lane < (j + 1) * HEAD), 1.0, 0.0).astype(BF)

    def window(g, lo, hi):
        return pl.ds(pl.multiple_of(g * GROUP + lo * LANE, LANE), (hi - lo) * LANE)

    def add_tiles(tiles, lo, value):
        for t in range(value.shape[1] // LANE):
            part = value[:, t * LANE : (t + 1) * LANE]
            tiles[lo + t] = part if tiles[lo + t] is None else tiles[lo + t] + part

    @pl.loop(0, 4)
    def _(g):
        heads = []
        for j, (lo, hi) in enumerate(WINDOWS):
            win = window(g, lo, hi)
            q = q_s[:, win] * head_mask(j, lo, hi)
            k = k_s[:, win]
            heads.append(
                jnp.concatenate(
                    [dot_t(q[0:32], k[0:256]), dot_t(q[32:160], k[32:288]), dot_t(q[160:192], k[64:320])], axis=0
                )
            )
        heads = [scores * SCALE + bias_s[...] for scores in heads]
        highest = [jnp.max(scores, axis=-1, keepdims=True) for scores in heads]
        heads = [jnp.exp(scores - top) for scores, top in zip(heads, highest)]
        inverse = [1.0 / jnp.sum(powers, axis=-1, keepdims=True) for powers in heads]
        heads = [(powers * inv).astype(BF) for powers, inv in zip(heads, inverse)]
        parts = [[None] * 3 for _ in range(3)]
        for j, (lo, hi) in enumerate(WINDOWS):
            v = v_s[:, window(g, lo, hi)] * head_mask(j, lo, hi)
            p = heads[j]
            p_s[g * 4 + j] = p[32:160]
            add_tiles(parts[0], lo, dot(p[0:32], v[0:256]))
            add_tiles(parts[1], lo, dot(p[32:160], v[32:288]))
            add_tiles(parts[2], lo, dot(p[160:192], v[64:320]))
        for t in range(3):
            at = window(g, t, t + 1)
            att_s[0:32, at] = parts[0][t].astype(BF)
            att_s[32:160, at] = parts[1][t].astype(BF)
            att_s[160:192, at] = parts[2][t].astype(BF)

    def hidden_step(j, squares):
        w_copy(3, j).wait()
        cols = lanes(j, COL)
        h = dot(att_s[...], wo_s[:, cols]) + x_s[64 : 64 + QR, cols].astype(F32)
        h = h.astype(BF).astype(F32)
        for t in range(COL // LANE):
            part = h[:, t * LANE : (t + 1) * LANE]
            h_s[j * (COL // LANE) + t] = part
            squares = squares + part * part
        return squares

    squares = lax.fori_loop(0, NC, hidden_step, jnp.zeros((QR, LANE), F32))
    inv_h = lax.rsqrt(jnp.sum(squares, axis=-1, keepdims=True) * (1.0 / D) + EPSILON)
    frame = lax.broadcasted_iota(jnp.int32, (QR, 1), 0) + (first - 32)
    spoken = jnp.where((frame >= 0) & (frame < limit), 1.0, 0.0)
    inv_spoken = inv_h * spoken

    for copy in late:
        copy.wait()

    row = lax.broadcasted_iota(jnp.int32, (PR, 64), 0)
    col = lax.broadcasted_iota(jnp.int32, (PR, 64), 1)
    at = tm * LR + row - 4
    chosen = (col == row + 12) & (at >= 0) & (at < n_tm * LR)
    g_s[...] = dot(jnp.where(chosen, 1.0, 0.0).astype(BF), gst_s[...])

    def conv_step(c, carry):
        squares, along = carry
        cols = lanes(c)
        ci_s[...] = (h_s[c] * inv_spoken * cg_s[pl.ds(c, 1), :]).astype(BF).astype(F32)
        kern = tap_s[:, cols]
        acc = jnp.zeros((SR, LANE), F32)
        for s in range(8):
            xs = ci_s[s : s + SR + 24, :]
            for u in range(4):
                m = s + 8 * u
                acc = acc + kern[m : m + 1, :] * xs[8 * u : 8 * u + SR]
        sig = 1.0 / (1.0 + jnp.exp(-acc))
        silu = acc * sig
        dsilu_s[c] = sig + silu * (1.0 - sig)
        up_s[...] = h_s[c, 16 : 16 + SR, :] + silu
        pooled = up_s[pl.ds(0, PR, 4), :]
        for u in range(1, 4):
            pooled = pooled + up_s[pl.ds(u, PR, 4), :]
        pooled = pooled * 0.25
        pool_s[c] = pooled
        return squares + pooled * pooled, along + g_s[:, cols] * lg_s[pl.ds(c, 1), :] * pooled

    zero = jnp.zeros((PR, LANE), F32)
    squares, along = lax.fori_loop(0, NB, conv_step, (zero, zero))
    inv_p = lax.rsqrt(jnp.sum(squares, axis=-1, keepdims=True) * (1.0 / D) + EPSILON)
    back_p = inv_p * inv_p * inv_p * (jnp.sum(along, axis=-1, keepdims=True) * (1.0 / D))

    inv_own = inv_h[32:160]
    spoken_own = spoken[32:160]

    def conv_back(c, along):
        cols = lanes(c)
        pooled = pool_s[c]
        gain = lg_s[pl.ds(c, 1), :]
        norm_t[...] = pooled * inv_p * gain
        lat_s[:, cols] = norm_t[4:36, :].astype(BF)
        dpool = (g_s[:, cols] * gain * inv_p - pooled * back_p) * 0.25
        for u in range(4):
            up_s[pl.ds(u, PR, 4), :] = dpool
        ds_s[...] = up_s[...] * dsilu_s[c]
        us_s[c] = up_s[16 : 16 + FR, :]
        kern = tap_s[:, cols]
        acc = jnp.zeros((FR, LANE), F32)
        for s in range(8):
            base = 8 if s == 0 else s
            xs = ds_s[base : base + FR + 24, :]
            for u in range(4):
                m = 32 - base - 8 * u
                acc = acc + kern[m : m + 1, :] * xs[8 * u : 8 * u + FR]
        dn = acc.astype(BF).astype(F32) * spoken_own * cg_s[pl.ds(c, 1), :]
        dnc_s[c] = dn
        return along + dn * h_s[c, 32:160, :]

    along = lax.fori_loop(0, NB, conv_back, jnp.zeros((FR, LANE), F32))
    latent_copy = pltpu.make_async_copy(lat_s, latent_out, sems.at[10])
    latent_copy.start()
    back_h = inv_own * inv_own * inv_own * (jnp.sum(along, axis=-1, keepdims=True) * (1.0 / D))

    @pl.loop(0, NB)
    def _(c):
        dhid_s[:, lanes(c)] = (us_s[c] + dnc_s[c] * inv_own - h_s[c, 32:160, :] * back_h).astype(BF)

    dhid_copy = pltpu.make_async_copy(dhid_s, dhid_out, sems.at[11])
    dhid_copy.start()

    @pl.loop(0, NC)
    def _(j):
        datt_s[:, lanes(j, COL)] = dot_t(dhid_s[...], wo_s[lanes(j, COL), :]).astype(BF)

    @pl.loop(0, 4)
    def _(g):
        heads = []
        for j, (lo, hi) in enumerate(WINDOWS):
            win = window(g, lo, hi)
            heads.append(dot_t(datt_s[:, win] * head_mask(j, lo, hi), v_s[32:288, win]))
        weights = [p_s[g * 4 + j].astype(F32) for j in range(4)]
        heads = [w * dp for w, dp in zip(weights, heads)]
        sums = [jnp.sum(pd, axis=-1, keepdims=True) for pd in heads]
        heads = [((pd - w * total) * SCALE).astype(BF) for pd, w, total in zip(heads, weights, sums)]
        dq, dk, dv = [None] * 3, [None] * 3, [None] * 3
        for j, (lo, hi) in enumerate(WINDOWS):
            win = window(g, lo, hi)
            mask = head_mask(j, lo, hi)
            add_tiles(dq, lo, dot(heads[j], k_s[32:288, win] * mask))
            add_tiles(dk, lo, t_dot(heads[j], q_s[32:160, win] * mask))
            add_tiles(dv, lo, t_dot(p_s[g * 4 + j], datt_s[:, win] * mask))
        for t in range(3):
            at = window(g, t, t + 1)
            dq_s[:, at] = dq[t].astype(BF)
            dk_s[:, at] = dk[t].astype(BF)
            dv_s[:, at] = dv[t].astype(BF)

    @pl.loop(0, NC)
    def _(j):
        cols = lanes(j, COL)
        both = dot_t(dk_s[...], wk_s[cols, :]) + dot_t(dv_s[...], wv_s[cols, :])
        dn_s[:, cols] = both[64:192] + dot_t(dq_s[...], wq_s[cols, :])
        edge_s[0:64, cols] = both[0:64].astype(BF)
        edge_s[64:128, cols] = both[192:256].astype(BF)

    row_a = pl.multiple_of((1 - parity) * 64, 64)
    row_b = pl.multiple_of(parity * 64, 64)
    outs = [
        pltpu.make_async_copy(edge_s.at[pl.ds(row_a, 64)], send_a, sems.at[12]),
        pltpu.make_async_copy(edge_s.at[pl.ds(row_b, 64)], send_b, sems.at[13]),
        pltpu.make_async_copy(dn_s, dn_out, sems.at[14]),
    ]
    for copy in outs:
        copy.start()
    for copy in [latent_copy, dhid_copy] + outs:
        copy.wait()


def finish(
    fc_in, tl_in, audio, dhid, dn, recv_a, recv_b, l0, l1, l2, l3, norm_gain,
    rows_out, grad_out,
    fc, tl, x_s, dh_s, dn_s, r_s, lat_s, ng_s, out_s, rows_s, sems,
):
    cf = pltpu.make_async_copy(fc_in, fc, sems.at[12])
    ct = pltpu.make_async_copy(tl_in, tl, sems.at[13])
    cf.start()
    ct.start()
    tm = lax.axis_index("tm")
    llm = lax.axis_index("llm")
    parity = tm % 2
    copies = [
        pltpu.make_async_copy(audio, x_s, sems.at[0]),
        pltpu.make_async_copy(dhid, dh_s, sems.at[1]),
        pltpu.make_async_copy(dn, dn_s, sems.at[2]),
        pltpu.make_async_copy(recv_a, r_s.at[pl.ds(pl.multiple_of((1 - parity) * 64, 64), 64)], sems.at[3]),
        pltpu.make_async_copy(recv_b, r_s.at[pl.ds(pl.multiple_of(parity * 64, 64), 64)], sems.at[4]),
        pltpu.make_async_copy(norm_gain, ng_s, sems.at[5]),
    ]
    lat_copies = [
        pltpu.make_async_copy(source, lat_s.at[pl.ds(j * LR, LR)], sems.at[6 + j])
        for j, source in enumerate((l0, l1, l2, l3))
    ]
    for copy in copies + lat_copies:
        copy.start()
    cf.wait()
    ct.wait()
    starts, lives = routes(fc, tl, tm)
    slot = lax.broadcasted_iota(jnp.int32, (SLOTS, NREC * LR), 0) + llm * SLOTS
    col = lax.broadcasted_iota(jnp.int32, (SLOTS, NREC * LR), 1)
    chosen = jnp.zeros((SLOTS, NREC * LR), F32)
    for j in range(NREC):
        b = llm ^ j
        r = col - j * LR
        hit = (r >= 0) & (r < pick(lives, b)) & (slot == r + pick(starts, b))
        chosen = jnp.where(hit, 1.0, chosen)
    for copy in copies:
        copy.wait()
    keep_left = jnp.where(tm > 0, 1.0, 0.0)
    keep_right = jnp.where(tm < lax.axis_size("tm") - 1, 1.0, 0.0)
    for half in range(2):
        rows = slice(half * 64, half * 64 + 64)
        keep = keep_left if half == 0 else keep_right
        x = x_s[rows, :].astype(F32)
        inv = lax.rsqrt(jnp.mean(x * x, axis=-1, keepdims=True) + EPSILON)
        along = jnp.zeros((64, LANE), F32)
        for c in range(NB):
            cols = slice(c * LANE, (c + 1) * LANE)
            g = (dn_s[rows, cols] + r_s[rows, cols].astype(F32) * keep).astype(BF).astype(F32) * ng_s[c : c + 1, :]
            dn_s[rows, cols] = g
            along = along + g * x[:, cols]
        back = inv * inv * inv * (jnp.sum(along, axis=-1, keepdims=True) * (1.0 / D))
        out_s[rows, :] = (dh_s[rows, :].astype(F32) + dn_s[rows, :] * inv - x * back).astype(BF)
    grad_copy = pltpu.make_async_copy(out_s, grad_out, sems.at[10])
    grad_copy.start()
    for copy in lat_copies:
        copy.wait()
    rows_s[...] = dot(chosen.astype(BF), lat_s[...]).astype(BF)
    rows_copy = pltpu.make_async_copy(rows_s, rows_out, sems.at[11])
    rows_copy.start()
    grad_copy.wait()
    rows_copy.wait()


def swap(count, cells_a, cells_b):
    pairs_a = [(i, i ^ 1) for i in range(count)]
    n = lax.axis_size("llm")
    full_b = []
    for i in range(count):
        partner = ((i + 1) ^ 1) - 1
        end = partner < 0 or partner >= count
        full_b += [(i * n + y, i * n + (y ^ 1) if end else partner * n + y) for y in range(n)]
    return lax.ppermute(cells_a, "tm", pairs_a), lax.ppermute(cells_b, ("tm", "llm"), full_b)


def exchange(count, cells):
    return [
        lax.ppermute(cells[j], "llm", [(i, i ^ j) for i in range(count)]) for j in range(1, count)
    ]


def call(kernel, outs, scratch, specs, name, limit, flops):
    return pl.pallas_call(
        kernel,
        out_shape=outs,
        in_specs=specs,
        out_specs=[ANY] * len(outs),
        scratch_shapes=scratch,
        compiler_params=pltpu.CompilerParams(vmem_limit_bytes=limit),
        cost_estimate=pl.CostEstimate(flops=flops, bytes_accessed=4_000_000, transcendentals=0),
        name=name,
    )


def shape(rows, dtype=BF, cols=D):
    return jax.ShapeDtypeStruct((rows, cols), dtype)


MIB = 1024 * 1024


def hbm(array):
    return pltpu.with_memory_space_constraint(array, pltpu.HBM)


def run_main(*operands):
    V = pltpu.VMEM
    S = pltpu.SMEM
    dma = pltpu.SemaphoreType.DMA
    return call(
        main_kernel,
        [shape(LR), shape(FR), shape(FR, F32), shape(64), shape(64)],
        [
            S((NREC,), jnp.int32),
            V((EXT, D), BF), V((EXT, D), BF), V((QR, D), BF), V((EXT, D), BF), V((EXT, D), BF),
            V((D, D), BF), V((D, D), BF), V((D, D), BF), V((D, D), BF),
            V((NB, LANE), F32), V((NB, LANE), F32), V((NB, LANE), F32), V((KERN, D), F32),
            V((QR, D), BF), V((16, FR, 256), BF), V((QR, 256), F32),
            V((NB, QR, LANE), F32), V((QR, LANE), F32), V((NB, SR, LANE), F32), V((SR, LANE), F32),
            V((NB, PR, LANE), F32), V((PR, D), F32), V((64, D), BF), V((PR, LANE), F32), V((LR, D), BF),
            V((SR, LANE), F32), V((NB, FR, LANE), F32), V((NB, FR, LANE), F32), V((FR, D), BF),
            V((FR, D), BF), V((FR, D), BF), V((256, D), BF), V((256, D), BF), V((FR, D), F32), V((FR, D), BF),
            dma((4, NC)), dma((16,)),
        ],
        [ANY] * 15,
        "main", 50 * MIB, 10_000_000_000,
    )(*operands)


def on_device(
    audio, frame_counts, text_lengths, norm_gain, w_query, w_key, w_value, w_out,
    conv_gain, conv_kernel, latent_gain, llm_grads,
):
    signal = hbm(audio[0])
    n_tm = lax.axis_size("tm")
    n_llm = lax.axis_size("llm")
    norm_row, conv_row, latent_row = (hbm(g.reshape(NB, LANE)) for g in (norm_gain, conv_gain, latent_gain))
    fc, tl, taps = hbm(frame_counts), hbm(text_lengths.T), hbm(conv_kernel)
    weights = [hbm(w) for w in (w_query, w_key, w_value, w_out)]
    V = pltpu.VMEM
    S = pltpu.SMEM
    dma = pltpu.SemaphoreType.DMA

    send_a, send_b, o0, o1, o2, o3 = call(
        prepare,
        [shape(HALO)] * 2 + [shape(LR)] * 4,
        [S((NREC,), jnp.int32), S((NREC, n_tm), jnp.int32), V((SLOTS, D), BF), V((NREC, LR, D), BF), dma((9,))],
        [ANY] * 4,
        "prepare", 8 * MIB, 10_000_000,
    )(fc, tl, signal, hbm(llm_grads[0]))
    recv_a, recv_b = swap(n_tm, send_a, send_b)
    came = exchange(n_llm, [o0, o1, o2, o3])
    lat_grad = o0 + came[0] + came[1] + came[2]
    even = lax.axis_index("tm") % 2 == 0
    edge_a, edge_b = swap(
        n_tm,
        jnp.where(even, lat_grad[16:], lat_grad[:16]),
        jnp.where(even, lat_grad[:16], lat_grad[16:]),
    )

    latent, dhid, dn, back_a, back_b = run_main(
        fc, signal, recv_a, recv_b, lat_grad, edge_a, edge_b,
        *weights, norm_row, conv_row, latent_row, taps,
    )
    ret_a, ret_b = swap(n_tm, back_a, back_b)
    others = exchange(n_llm, [latent] * n_llm)
    rows, grad = call(
        finish,
        [shape(SLOTS), shape(FR)],
        [
            S((NREC,), jnp.int32), S((NREC, n_tm), jnp.int32),
            V((FR, D), BF), V((FR, D), BF), V((FR, D), F32), V((FR, D), BF), V((NREC * LR, D), BF),
            V((NB, LANE), F32), V((FR, D), BF), V((SLOTS, D), BF), dma((14,)),
        ],
        [ANY] * 12,
        "finish", 8 * MIB, 10_000_000,
    )(fc, tl, signal, dhid, dn, ret_a, ret_b, latent, *others, norm_row)
    return (rows[None], grad[None])


def solution(mesh):
    placed = (P("llm", "tm", None),) + (P(),) * 10 + (P("tm", "llm", None),)
    return jax.shard_map(
        on_device,
        mesh=mesh,
        in_specs=placed,
        out_specs=(P("tm", "llm", None), P("llm", "tm", None)),
        check_vma=False,
    )
```

```python
import jax
import jax.numpy as jnp
from jax import lax
from jax.experimental import pallas as pl
from jax.experimental.pallas import tpu as pltpu
from jax.sharding import PartitionSpec as P

D = 1536
REACH = 64
KERN = 32
FR = 128
HALO = 96
EXT = FR + 2 * HALO
QR = FR + 64
SR = FR + 32
PR = SR // 4
LR = FR // 4
SLOTS = 64
NREC = 4
HEAD = 96
LANE = 128
NB = D // LANE
COL = 1536
NC = D // COL
GROUP = 4 * HEAD
EPSILON = 1e-06
SCALE = HEAD ** (-0.5)
BF = jnp.bfloat16
F32 = jnp.float32
WINDOWS = ((0, 1), (0, 2), (1, 3), (2, 3))

VMEM = pl.BlockSpec(memory_space=pltpu.VMEM)
ANY = pl.BlockSpec(memory_space=pl.ANY)


def dot(a, b):
    return lax.dot_general(a, b, (((1,), (0,)), ((), ())), preferred_element_type=F32)


def dot_t(a, b):
    return lax.dot_general(a, b, (((1,), (1,)), ((), ())), preferred_element_type=F32)


def t_dot(a, b):
    return lax.dot_general(a, b, (((0,), (0,)), ((), ())), preferred_element_type=F32)


def lanes(c, width=LANE):
    return pl.ds(pl.multiple_of(c * width, width), width)


def routes(fc, tl, slice_index):
    starts, lives = [], []
    total = 0
    for b in range(NREC):
        live = jnp.clip(fc[b] // 4 - slice_index * LR, 0, LR)
        total = total + tl[b, slice_index]
        starts.append(total)
        lives.append(live)
        total = total + live
    return starts, lives


def pick(values, index):
    out = values[0]
    for b in range(1, NREC):
        out = jnp.where(index == b, values[b], out)
    return out


def prepare(fc_in, tl_in, audio, grads, send_a, send_b, own, pair, mate, fc, tl, g_buf, sems):
    cf = pltpu.make_async_copy(fc_in, fc, sems.at[0])
    ct = pltpu.make_async_copy(tl_in, tl, sems.at[1])
    cf.start()
    ct.start()
    tm = lax.axis_index("tm")
    llm = lax.axis_index("llm")
    off_a = (1 - tm % 2) * (FR - HALO)
    off_b = (FR - HALO) - off_a
    cg = pltpu.make_async_copy(grads, g_buf, sems.at[2])
    ca = pltpu.make_async_copy(audio.at[pl.ds(pl.multiple_of(off_a, 32), HALO)], send_a, sems.at[3])
    cb = pltpu.make_async_copy(audio.at[pl.ds(pl.multiple_of(off_b, 32), HALO)], send_b, sems.at[4])
    cg.start()
    ca.start()
    cb.start()
    cf.wait()
    ct.wait()
    starts, lives = routes(fc, tl, tm)
    row = lax.broadcasted_iota(jnp.int32, (LR, SLOTS), 0)
    slot = lax.broadcasted_iota(jnp.int32, (LR, SLOTS), 1) + llm * SLOTS
    picked = []
    for j in range(NREC):
        b = llm ^ j
        chosen = (row < pick(lives, b)) & (slot == row + pick(starts, b))
        picked.append(jnp.where(chosen, 1.0, 0.0).astype(BF))
    cg.wait()
    moved = dot(jnp.concatenate(picked, axis=0), g_buf[...]).astype(BF)
    own[...] = moved[:LR]
    pair[...] = moved[LR : 3 * LR]
    mate[...] = moved[3 * LR :]
    ca.wait()
    cb.wait()


def norm_rows(x, gains, out, rows):
    inv = lax.rsqrt(jnp.mean(x * x, axis=-1, keepdims=True) + EPSILON)
    for c in range(NB):
        cols = slice(c * LANE, (c + 1) * LANE)
        out[rows, cols] = (x[:, cols] * inv * gains[c : c + 1, :]).astype(BF)


def project_own(
    after, audio, gains_in, w_key, w_value, w_query, w_out,
    x_o, gain_o, k_o, v_o, q_o, wk_o, wv_o, wq_o, wo_o, n_s, w_sems, sems,
):
    cx = pltpu.make_async_copy(audio, x_o, sems.at[0])
    cg = pltpu.make_async_copy(gains_in, gain_o, sems.at[1])
    cx.start()
    cg.start()

    def w_copy(n, j):
        src = (w_key, w_value, w_query, w_out)[n]
        dst = (wk_o, wv_o, wq_o, wo_o)[n]
        return pltpu.make_async_copy(src.at[:, lanes(j, COL)], dst.at[:, lanes(j, COL)], w_sems.at[n, j])

    for n in range(4):
        for j in range(NC):
            w_copy(n, j).start()
    cx.wait()
    cg.wait()
    for r in range(2):
        rows = slice(r * 64, r * 64 + 64)
        norm_rows(x_o[rows, :].astype(F32), gain_o, n_s, rows)
    for n, (w_s, out_s) in enumerate(((wk_o, k_o), (wv_o, v_o), (wq_o, q_o))):
        for j in range(NC):
            w_copy(n, j).wait()
            cols = slice(j * COL, (j + 1) * COL)
            out_s[:, cols] = dot(n_s[...], w_s[:, cols]).astype(BF)
    for j in range(NC):
        w_copy(3, j).wait()


def combine(after, mate, got_pair, out):
    out[...] = mate[...] + got_pair[LR:, :]


def split_edges(after, own, got_pair, got_mate, grad_o, send_a, send_b):
    grads = own[...] + got_pair[:LR, :] + got_mate[...]
    grad_o[...] = grads
    even = lax.axis_index("tm") % 2 == 0

    @pl.when(even)
    def _():
        send_a[...] = grads[16:]
        send_b[...] = grads[:16]

    @pl.when(jnp.logical_not(even))
    def _():
        send_a[...] = grads[:16]
        send_b[...] = grads[16:]


def head_mask(j, lo, hi):
    lane = lax.broadcasted_iota(jnp.int32, (1, (hi - lo) * LANE), 1) + lo * LANE
    return jnp.where((lane >= j * HEAD) & (lane < (j + 1) * HEAD), 1.0, 0.0).astype(BF)


def window(g, lo, hi):
    return pl.ds(pl.multiple_of(g * GROUP + lo * LANE, LANE), (hi - lo) * LANE)


def add_tiles(tiles, lo, value):
    for t in range(value.shape[1] // LANE):
        part = value[:, t * LANE : (t + 1) * LANE]
        tiles[lo + t] = part if tiles[lo + t] is None else tiles[lo + t] + part


def attend(
    fc_in, recv_a, recv_b, x_own, gains, k_own, v_own, q_own, wk_s, wv_s, wq_s,
    xq_o, q_s, k_s, v_s, p_s, att_s, fc, n_s, bias_s, sems,
):
    fc_copy = pltpu.make_async_copy(fc_in, fc, sems.at[0])
    fc_copy.start()
    tm = lax.axis_index("tm")
    llm = lax.axis_index("llm")
    even = tm % 2 == 0
    first = tm * FR
    total = lax.axis_size("tm") * FR

    @pl.when(even)
    def _():
        norm_rows(recv_b[...].astype(F32), gains, n_s, slice(0, HALO))
        norm_rows(recv_a[...].astype(F32), gains, n_s, slice(HALO, 2 * HALO))
        xq_o[0:32, :] = recv_b[64:96, :]
        xq_o[160:192, :] = recv_a[0:32, :]

    @pl.when(jnp.logical_not(even))
    def _():
        norm_rows(recv_a[...].astype(F32), gains, n_s, slice(0, HALO))
        norm_rows(recv_b[...].astype(F32), gains, n_s, slice(HALO, 2 * HALO))
        xq_o[0:32, :] = recv_a[64:96, :]
        xq_o[160:192, :] = recv_b[0:32, :]

    xq_o[32:160, :] = x_own[...]
    k_s[96:224, :] = k_own[...]
    v_s[96:224, :] = v_own[...]
    q_s[32:160, :] = q_own[...]
    for w_s, out_s in ((wk_s, k_s), (wv_s, v_s)):
        @pl.loop(0, NC)
        def _(j, w_s=w_s, out_s=out_s):
            cols = lanes(j, COL)
            new = dot(n_s[...], w_s[:, cols]).astype(BF)
            out_s[0:96, cols] = new[0:96]
            out_s[224:320, cols] = new[96:192]

    @pl.loop(0, NC)
    def _(j):
        cols = lanes(j, COL)
        new = dot(n_s[64:128, :], wq_s[:, cols]).astype(BF)
        q_s[0:32, cols] = new[0:32]
        q_s[160:192, cols] = new[32:64]

    fc_copy.wait()
    limit = fc[llm]

    def bias_of(rows, q_first, k_first):
        qe = lax.broadcasted_iota(jnp.int32, (rows, 256), 0) + q_first
        ke = lax.broadcasted_iota(jnp.int32, (rows, 256), 1) + k_first
        kt = ke + (first - HALO)
        ok = (ke >= qe - REACH) & (ke < qe + REACH) & (kt >= 0) & (kt < total) & ((kt < limit) | (ke == qe))
        return jnp.where(ok, 0.0, -1e30)

    bias_s[0:32, :] = bias_of(32, 64, 0)
    bias_s[32:160, :] = bias_of(FR, HALO, 32)
    bias_s[160:192, :] = bias_of(32, 224, 64)

    @pl.loop(0, 4)
    def _(g):
        heads = []
        for j, (lo, hi) in enumerate(WINDOWS):
            win = window(g, lo, hi)
            q = q_s[:, win] * head_mask(j, lo, hi)
            k = k_s[:, win]
            heads.append(
                jnp.concatenate(
                    [dot_t(q[0:32], k[0:256]), dot_t(q[32:160], k[32:288]), dot_t(q[160:192], k[64:320])], axis=0
                )
            )
        heads = [scores * SCALE + bias_s[...] for scores in heads]
        highest = [jnp.max(scores, axis=-1, keepdims=True) for scores in heads]
        heads = [jnp.exp(scores - top) for scores, top in zip(heads, highest)]
        inverse = [1.0 / jnp.sum(powers, axis=-1, keepdims=True) for powers in heads]
        heads = [(powers * inv).astype(BF) for powers, inv in zip(heads, inverse)]
        parts = [[None] * 3 for _ in range(3)]
        for j, (lo, hi) in enumerate(WINDOWS):
            v = v_s[:, window(g, lo, hi)] * head_mask(j, lo, hi)
            p = heads[j]
            p_s[g * 4 + j] = p[32:160]
            add_tiles(parts[0], lo, dot(p[0:32], v[0:256]))
            add_tiles(parts[1], lo, dot(p[32:160], v[32:288]))
            add_tiles(parts[2], lo, dot(p[160:192], v[64:320]))
        for t in range(3):
            at = window(g, t, t + 1)
            att_s[0:32, at] = parts[0][t].astype(BF)
            att_s[32:160, at] = parts[1][t].astype(BF)
            att_s[160:192, at] = parts[2][t].astype(BF)


def spoken_rows(fc, tm, llm):
    frame = lax.broadcasted_iota(jnp.int32, (QR, 1), 0) + (tm * FR - 32)
    return jnp.where((frame >= 0) & (frame < fc[llm]), 1.0, 0.0)


def convolve(
    fc_in, xq, att_s, wo_s, cg_in, lg_in, taps_in,
    lat_o, h_s, dsilu_s, pool_s, inv_o, cg_s, lg_s, tap_s, fc, ci_s, up_s, norm_t, sems,
):
    copies = [
        pltpu.make_async_copy(source, into, sems.at[i])
        for i, (source, into) in enumerate(((fc_in, fc), (cg_in, cg_s), (lg_in, lg_s), (taps_in, tap_s)))
    ]
    for copy in copies:
        copy.start()
    tm = lax.axis_index("tm")
    llm = lax.axis_index("llm")

    def hidden_step(j, squares):
        cols = lanes(j, COL)
        h = dot(att_s[...], wo_s[:, cols]) + xq[:, cols].astype(F32)
        h = h.astype(BF).astype(F32)
        for t in range(COL // LANE):
            part = h[:, t * LANE : (t + 1) * LANE]
            h_s[j * (COL // LANE) + t] = part
            squares = squares + part * part
        return squares

    squares = lax.fori_loop(0, NC, hidden_step, jnp.zeros((QR, LANE), F32))
    inv_h = lax.rsqrt(jnp.sum(squares, axis=-1, keepdims=True) * (1.0 / D) + EPSILON)
    inv_o[...] = jnp.broadcast_to(inv_h, (QR, LANE))
    for copy in copies:
        copy.wait()
    inv_spoken = inv_h * spoken_rows(fc, tm, llm)

    def conv_step(c, squares):
        cols = lanes(c)
        ci_s[...] = (h_s[c] * inv_spoken * cg_s[pl.ds(c, 1), :]).astype(BF).astype(F32)
        kern = tap_s[:, cols]
        acc = jnp.zeros((SR, LANE), F32)
        for s in range(8):
            xs = ci_s[s : s + SR + 24, :]
            for u in range(4):
                m = s + 8 * u
                acc = acc + kern[m : m + 1, :] * xs[8 * u : 8 * u + SR]
        sig = 1.0 / (1.0 + jnp.exp(-acc))
        silu = acc * sig
        dsilu_s[c] = sig + silu * (1.0 - sig)
        up_s[...] = h_s[c, 16 : 16 + SR, :] + silu
        pooled = up_s[pl.ds(0, PR, 4), :]
        for u in range(1, 4):
            pooled = pooled + up_s[pl.ds(u, PR, 4), :]
        pooled = pooled * 0.25
        pool_s[c] = pooled
        return squares + pooled * pooled

    squares = lax.fori_loop(0, NB, conv_step, jnp.zeros((PR, LANE), F32))
    inv_p = lax.rsqrt(jnp.sum(squares, axis=-1, keepdims=True) * (1.0 / D) + EPSILON)
    for c in range(NB):
        norm_t[...] = pool_s[c] * inv_p * lg_s[c : c + 1, :]
        lat_o[:, c * LANE : (c + 1) * LANE] = norm_t[4:36, :].astype(BF)


def convolve_back(
    fc_in, lat_grad, edge_a, edge_b, h_s, dsilu_s, pool_s, inv_s, cg_s, lg_s, tap_s, wo_s,
    dhid_s, datt_s, fc, g_s, up_s, ds_s, us_s, dnc_s, sems,
):
    copy = pltpu.make_async_copy(fc_in, fc, sems.at[0])
    copy.start()
    tm = lax.axis_index("tm")
    llm = lax.axis_index("llm")
    even = tm % 2 == 0

    row = lax.broadcasted_iota(jnp.int32, (PR, 64), 0)
    col = lax.broadcasted_iota(jnp.int32, (PR, 64), 1)
    at = tm * LR + row - 4
    chosen = (col == row + 12) & (at >= 0) & (at < lax.axis_size("tm") * LR)
    chosen = jnp.where(chosen, 1.0, 0.0).astype(BF)
    left = jnp.where(even, 0.0, 1.0).astype(BF)
    right = jnp.where(even, 1.0, 0.0).astype(BF)
    stacked = jnp.concatenate(
        [
            edge_a[...] * left + edge_b[...] * right,
            lat_grad[...],
            edge_a[...] * right + edge_b[...] * left,
        ],
        axis=0,
    )
    g_s[...] = dot(chosen, stacked)

    def sums(c, carry):
        squares, along = carry
        pooled = pool_s[c]
        return squares + pooled * pooled, along + g_s[:, lanes(c)] * lg_s[pl.ds(c, 1), :] * pooled

    zero = jnp.zeros((PR, LANE), F32)
    squares, along = lax.fori_loop(0, NB, sums, (zero, zero))
    inv_p = lax.rsqrt(jnp.sum(squares, axis=-1, keepdims=True) * (1.0 / D) + EPSILON)
    back_p = inv_p * inv_p * inv_p * (jnp.sum(along, axis=-1, keepdims=True) * (1.0 / D))
    inv_own = inv_s[32:160, :]
    copy.wait()
    spoken_own = spoken_rows(fc, tm, llm)[32:160]

    def conv_back(c, along):
        cols = lanes(c)
        gain = lg_s[pl.ds(c, 1), :]
        dpool = (g_s[:, cols] * gain * inv_p - pool_s[c] * back_p) * 0.25
        for u in range(4):
            up_s[pl.ds(u, PR, 4), :] = dpool
        ds_s[...] = up_s[...] * dsilu_s[c]
        us_s[c] = up_s[16 : 16 + FR, :]
        kern = tap_s[:, cols]
        acc = jnp.zeros((FR, LANE), F32)
        for s in range(8):
            base = 8 if s == 0 else s
            xs = ds_s[base : base + FR + 24, :]
            for u in range(4):
                m = 32 - base - 8 * u
                acc = acc + kern[m : m + 1, :] * xs[8 * u : 8 * u + FR]
        dn = acc.astype(BF).astype(F32) * spoken_own * cg_s[pl.ds(c, 1), :]
        dnc_s[c] = dn
        return along + dn * h_s[c, 32:160, :]

    along = lax.fori_loop(0, NB, conv_back, jnp.zeros((FR, LANE), F32))
    back_h = inv_own * inv_own * inv_own * (jnp.sum(along, axis=-1, keepdims=True) * (1.0 / D))

    @pl.loop(0, NB)
    def _(c):
        dhid_s[:, lanes(c)] = (us_s[c] + dnc_s[c] * inv_own - h_s[c, 32:160, :] * back_h).astype(BF)

    @pl.loop(0, NC)
    def _(j):
        datt_s[:, lanes(j, COL)] = dot_t(dhid_s[...], wo_s[lanes(j, COL), :]).astype(BF)


def attend_back(q_s, k_s, v_s, p_s, datt_s, wk_s, wv_s, send_a, send_b, dq_s, dk_s, dv_s, ek_s, ev_s):
    @pl.loop(0, 4)
    def _(g):
        heads = []
        for j, (lo, hi) in enumerate(WINDOWS):
            win = window(g, lo, hi)
            heads.append(dot_t(datt_s[:, win] * head_mask(j, lo, hi), v_s[32:288, win]))
        weights = [p_s[g * 4 + j].astype(F32) for j in range(4)]
        heads = [w * dp for w, dp in zip(weights, heads)]
        sums = [jnp.sum(pd, axis=-1, keepdims=True) for pd in heads]
        heads = [((pd - w * total) * SCALE).astype(BF) for pd, w, total in zip(heads, weights, sums)]
        dq, dk, dv = [None] * 3, [None] * 3, [None] * 3
        for j, (lo, hi) in enumerate(WINDOWS):
            win = window(g, lo, hi)
            mask = head_mask(j, lo, hi)
            add_tiles(dq, lo, dot(heads[j], k_s[32:288, win] * mask))
            add_tiles(dk, lo, t_dot(heads[j], q_s[32:160, win] * mask))
            add_tiles(dv, lo, t_dot(p_s[g * 4 + j], datt_s[:, win] * mask))
        for t in range(3):
            at = window(g, t, t + 1)
            dq_s[:, at] = dq[t].astype(BF)
            for out, edge, tiles in ((dk_s, ek_s, dk), (dv_s, ev_s, dv)):
                new = tiles[t].astype(BF)
                edge[0:64, at] = new[0:64]
                out[:, at] = new[64:192]
                edge[64:128, at] = new[192:256]

    even = lax.axis_index("tm") % 2 == 0

    @pl.loop(0, NC)
    def _(j):
        cols = lanes(j, COL)
        both = (dot_t(ek_s[...], wk_s[cols, :]) + dot_t(ev_s[...], wv_s[cols, :])).astype(BF)

        @pl.when(even)
        def _():
            send_a[:, cols] = both[64:128]
            send_b[:, cols] = both[0:64]

        @pl.when(jnp.logical_not(even))
        def _():
            send_a[:, cols] = both[0:64]
            send_b[:, cols] = both[64:128]


def project_back(after, dq, dk, dv, wq_s, wk_s, wv_s, dn_o):
    @pl.loop(0, NC)
    def _(j):
        cols = lanes(j, COL)
        dn_o[:, cols] = (
            dot_t(dk[...], wk_s[cols, :]) + dot_t(dv[...], wv_s[cols, :]) + dot_t(dq[...], wq_s[cols, :])
        )


def finish(
    fc_in, tl_in, x_s, dh_s, dn_s, recv_a, recv_b, l0, l1, l23, gains,
    rows_out, grad_out, fc, tl, r_s, g_s, out_s, rows_s, sems,
):
    cf = pltpu.make_async_copy(fc_in, fc, sems.at[0])
    ct = pltpu.make_async_copy(tl_in, tl, sems.at[1])
    cf.start()
    ct.start()
    tm = lax.axis_index("tm")
    llm = lax.axis_index("llm")
    even = tm % 2 == 0

    @pl.when(even)
    def _():
        r_s[0:64, :] = recv_b[...]
        r_s[64:128, :] = recv_a[...]

    @pl.when(jnp.logical_not(even))
    def _():
        r_s[0:64, :] = recv_a[...]
        r_s[64:128, :] = recv_b[...]

    copies = []
    for half in range(2):
        rows = slice(half * 64, half * 64 + 64)
        inside = (tm > 0) if half == 0 else (tm < lax.axis_size("tm") - 1)
        keep = jnp.where(inside, 1.0, 0.0)
        x = x_s[rows, :].astype(F32)
        inv = lax.rsqrt(jnp.mean(x * x, axis=-1, keepdims=True) + EPSILON)
        along = jnp.zeros((64, LANE), F32)
        for c in range(NB):
            cols = slice(c * LANE, (c + 1) * LANE)
            g = (dn_s[rows, cols] + r_s[rows, cols].astype(F32) * keep).astype(BF).astype(F32) * gains[c : c + 1, :]
            g_s[rows, cols] = g
            along = along + g * x[:, cols]
        back = inv * inv * inv * (jnp.sum(along, axis=-1, keepdims=True) * (1.0 / D))
        out_s[rows, :] = (dh_s[rows, :].astype(F32) + g_s[rows, :] * inv - x * back).astype(BF)
        copy = pltpu.make_async_copy(out_s.at[rows], grad_out.at[rows], sems.at[2 + half])
        copy.start()
        copies.append(copy)
    cf.wait()
    ct.wait()
    starts, lives = routes(fc, tl, tm)
    slot = lax.broadcasted_iota(jnp.int32, (SLOTS, NREC * LR), 0) + llm * SLOTS
    col = lax.broadcasted_iota(jnp.int32, (SLOTS, NREC * LR), 1)
    chosen = jnp.zeros((SLOTS, NREC * LR), F32)
    for j, apart in enumerate((0, 1, 3, 2)):
        b = llm ^ apart
        r = col - j * LR
        hit = (r >= 0) & (r < pick(lives, b)) & (slot == r + pick(starts, b))
        chosen = jnp.where(hit, 1.0, chosen)
    latents = jnp.concatenate([l0[...], l1[...], l23[...]], axis=0)
    rows_s[...] = dot(chosen.astype(BF), latents).astype(BF)
    copy = pltpu.make_async_copy(rows_s, rows_out, sems.at[4])
    copy.start()
    for copy in copies + [copy]:
        copy.wait()


def swap(count, cells_a, cells_b):
    pairs_a = [(i, i ^ 1) for i in range(count)]
    n = lax.axis_size("llm")
    full_b = []
    for i in range(count):
        partner = ((i + 1) ^ 1) - 1
        end = partner < 0 or partner >= count
        full_b += [(i * n + y, i * n + (y ^ 1) if end else partner * n + y) for y in range(n)]
    return lax.ppermute(cells_a, "tm", pairs_a), lax.ppermute(cells_b, ("tm", "llm"), full_b)


def trade(cells, apart):
    n = lax.axis_size("llm")
    return lax.ppermute(cells, "llm", [(i, i ^ apart) for i in range(n)])


def hbm(array):
    return pltpu.with_memory_space_constraint(array, pltpu.HBM)


def vmem(array):
    return pltpu.with_memory_space_constraint(array, pltpu.VMEM)


def call(kernel, ins, outs, scratch, flops, outs_in_hbm=False):
    place = {"h": hbm, "v": vmem, "n": lambda array: array}
    spec = {"h": ANY, "v": VMEM, "n": ANY}
    if outs_in_hbm:
        shapes = [jax.ShapeDtypeStruct(s, d) for s, d in outs]
    else:
        shapes = [pltpu.VMEM(s, d) for s, d in outs]
    return pl.pallas_call(
        kernel,
        out_shape=shapes,
        in_specs=[spec[kind] for kind, _ in ins],
        out_specs=[ANY if outs_in_hbm else VMEM] * len(outs),
        scratch_shapes=scratch,
        compiler_params=pltpu.CompilerParams(vmem_limit_bytes=12 * 1024 * 1024),
        cost_estimate=pl.CostEstimate(flops=flops, bytes_accessed=1_000_000, transcendentals=0),
        name=kernel.__name__,
    )(*[place[kind](array) for kind, array in ins])


def mark(kind, *arrays):
    return [(kind, array) for array in arrays]


def on_device(
    audio, frame_counts, text_lengths, norm_gain, w_query, w_key, w_value, w_out,
    conv_gain, conv_kernel, latent_gain, llm_grads,
):
    signal = audio[0]
    n_tm = lax.axis_size("tm")
    norm_row, conv_row, latent_row = (g.reshape(NB, LANE) for g in (norm_gain, conv_gain, latent_gain))
    tl_in = text_lengths.T
    V = pltpu.VMEM
    fc = pltpu.SMEM((NREC,), jnp.int32)
    tl = pltpu.SMEM((NREC, n_tm), jnp.int32)
    gain = ((NB, LANE), F32)
    weight = ((D, D), BF)

    def rows(n, dtype=BF):
        return ((n, D), dtype)

    def sems(*dims):
        return pltpu.SemaphoreType.DMA(dims)

    send_a, send_b, own, pair, mate = call(
        prepare,
        mark("h", frame_counts, tl_in, signal, llm_grads[0]),
        [rows(HALO), rows(HALO), rows(LR), rows(2 * LR), rows(LR)],
        [fc, tl, V((SLOTS, D), BF), sems(5)],
        100_000_000,
    )
    got_pair = trade(pair, 1)
    recv_a, recv_b = swap(n_tm, send_a, send_b)
    x, gains, k_own, v_own, q_own, wk, wv, wq, wo = call(
        project_own,
        mark("v", own) + mark("h", signal, norm_row, w_key, w_value, w_query, w_out),
        [rows(FR), gain, rows(FR), rows(FR), rows(FR), weight, weight, weight, weight],
        [V((FR, D), BF), sems(4, NC), sems(2)],
        6_000_000_000,
    )
    (both,) = call(combine, mark("v", gains, mate, got_pair), [rows(LR)], [], 1_000_000)
    got_mate = trade(both, 3)
    xq, q, k, v, p, att = call(
        attend,
        mark("h", frame_counts) + mark("v", recv_a, recv_b, x, gains, k_own, v_own, q_own, wk, wv, wq),
        [rows(QR), rows(QR), rows(EXT), rows(EXT), ((16, FR, 256), BF), rows(QR)],
        [fc, V((2 * HALO, D), BF), V((QR, 256), F32), sems(1)],
        8_000_000_000,
    )
    lat_grad, first_a, first_b = call(
        split_edges, mark("v", xq, own, got_pair, got_mate), [rows(LR), rows(16), rows(16)], [], 1_000_000
    )
    edge_a, edge_b = swap(n_tm, first_a, first_b)
    latent, h, dsilu, pool, inv, cgain, lgain, taps = call(
        convolve,
        mark("h", frame_counts) + mark("v", xq, att, wo) + mark("h", conv_row, latent_row, conv_kernel),
        [
            rows(LR), ((NB, QR, LANE), F32), ((NB, SR, LANE), F32), ((NB, PR, LANE), F32), ((QR, LANE), F32),
            gain, gain, rows(KERN, F32),
        ],
        [fc, V((QR, LANE), F32), V((SR, LANE), F32), V((PR, LANE), F32), sems(4)],
        5_000_000_000,
    )
    latent_1 = trade(latent, 1)
    dhid, datt = call(
        convolve_back,
        mark("h", frame_counts)
        + mark("v", lat_grad, edge_a, edge_b, h, dsilu, pool, inv, cgain, lgain, taps, wo),
        [rows(FR), rows(FR)],
        [
            fc, V((PR, D), F32), V((SR, LANE), F32), V((SR, LANE), F32), V((NB, FR, LANE), F32),
            V((NB, FR, LANE), F32), sems(1),
        ],
        5_000_000_000,
    )
    latent_23 = trade(jnp.concatenate([latent, latent_1], axis=0), 3)
    back_a, back_b, dq, dk, dv = call(
        attend_back,
        mark("v", q, k, v, p, datt, wk, wv),
        [rows(64), rows(64), rows(FR), rows(FR), rows(FR)],
        [V((FR, D), BF), V((FR, D), BF)],
        6_000_000_000,
    )
    ret_a, ret_b = swap(n_tm, back_a, back_b)
    (dn,) = call(
        project_back,
        mark("v", back_a, dq, dk, dv, wq, wk, wv),
        [rows(FR, F32)],
        [],
        3_000_000_000,
    )
    out_rows, grad = call(
        finish,
        mark("h", frame_counts, tl_in)
        + mark("v", x, dhid, dn, ret_a, ret_b, latent, latent_1, latent_23, gains),
        [rows(SLOTS), rows(FR)],
        [fc, tl, V((FR, D), BF), V((FR, D), F32), V((FR, D), BF), V((SLOTS, D), BF), sems(5)],
        1_000_000_000,
        outs_in_hbm=True,
    )
    return (out_rows[None], grad[None])


def solution(mesh):
    placed = (P("llm", "tm", None),) + (P(),) * 10 + (P("tm", "llm", None),)
    return jax.shard_map(
        on_device,
        mesh=mesh,
        in_specs=placed,
        out_specs=(P("tm", "llm", None), P("llm", "tm", None)),
        check_vma=False,
    )
```

```python
import jax
import jax.numpy as jnp
from jax import lax
from jax.experimental import pallas as pl
from jax.experimental.pallas import tpu as pltpu
from jax.sharding import PartitionSpec as P

D = 1536
REACH = 64
KERN = 32
FR = 128
HALO = 96
EXT = FR + 2 * HALO
QR = FR + 64
SR = FR + 32
PR = SR // 4
LR = FR // 4
SLOTS = 64
NREC = 4
HEAD = 96
LANE = 128
NB = D // LANE
COL = 1536
NC = D // COL
GROUP = 4 * HEAD
EPSILON = 1e-06
SCALE = HEAD ** (-0.5)
BF = jnp.bfloat16
F32 = jnp.float32
WINDOWS = ((0, 1), (0, 2), (1, 3), (2, 3))

VMEM = pl.BlockSpec(memory_space=pltpu.VMEM)
ANY = pl.BlockSpec(memory_space=pl.ANY)


def dot(a, b):
    return lax.dot_general(a, b, (((1,), (0,)), ((), ())), preferred_element_type=F32)


def dot_t(a, b):
    return lax.dot_general(a, b, (((1,), (1,)), ((), ())), preferred_element_type=F32)


def t_dot(a, b):
    return lax.dot_general(a, b, (((0,), (0,)), ((), ())), preferred_element_type=F32)


def lanes(c, width=LANE):
    return pl.ds(pl.multiple_of(c * width, width), width)


def routes(fc, tl, slice_index):
    starts, lives = [], []
    total = 0
    for b in range(NREC):
        live = jnp.clip(fc[b] // 4 - slice_index * LR, 0, LR)
        total = total + tl[b, slice_index]
        starts.append(total)
        lives.append(live)
        total = total + live
    return starts, lives


def pick(values, index):
    out = values[0]
    for b in range(1, NREC):
        out = jnp.where(index == b, values[b], out)
    return out


def prepare(fc_in, tl_in, audio, grads, send_a, send_b, own, pair, mate, fc, tl, g_buf, sems):
    cf = pltpu.make_async_copy(fc_in, fc, sems.at[0])
    ct = pltpu.make_async_copy(tl_in, tl, sems.at[1])
    cf.start()
    ct.start()
    tm = lax.axis_index("tm")
    llm = lax.axis_index("llm")
    off_a = (1 - tm % 2) * (FR - HALO)
    off_b = (FR - HALO) - off_a
    cg = pltpu.make_async_copy(grads, g_buf, sems.at[2])
    ca = pltpu.make_async_copy(
        audio.at[pl.ds(pl.multiple_of(off_a, 32), HALO)], send_a.at[pl.ds(0, HALO)], sems.at[3]
    )
    cb = pltpu.make_async_copy(
        audio.at[pl.ds(pl.multiple_of(off_b, 32), HALO)], send_b.at[pl.ds(0, HALO)], sems.at[4]
    )
    cg.start()
    ca.start()
    cb.start()
    cf.wait()
    ct.wait()
    starts, lives = routes(fc, tl, tm)
    row = lax.broadcasted_iota(jnp.int32, (LR, SLOTS), 0)
    slot = lax.broadcasted_iota(jnp.int32, (LR, SLOTS), 1) + llm * SLOTS
    starts = [pick(starts, llm ^ j) for j in range(NREC)]
    lives = [pick(lives, llm ^ j) for j in range(NREC)]
    picked = []
    for j in range(NREC):
        chosen = (row < lives[j]) & (slot == row + starts[j])
        picked.append(jnp.where(chosen, 1.0, 0.0).astype(BF))
    place = lax.broadcasted_iota(jnp.int32, (16, SLOTS), 0)
    slot = lax.broadcasted_iota(jnp.int32, (16, SLOTS), 1) + llm * SLOTS
    for offset in ((1 - tm % 2) * (LR - 4), (tm % 2) * (LR - 4)):
        r = place % 4 + offset
        chosen = jnp.zeros((16, SLOTS), F32)
        for j in range(NREC):
            hit = (place // 4 == (j + 3) % 4) & (r < lives[j]) & (slot == r + starts[j])
            chosen = jnp.where(hit, 1.0, chosen)
        picked.append(chosen.astype(BF))
    cg.wait()
    moved = dot(jnp.concatenate(picked, axis=0), g_buf[...]).astype(BF)
    own[...] = moved[:LR]
    pair[...] = moved[LR : 3 * LR]
    mate[...] = moved[3 * LR : 4 * LR]
    send_a[HALO:, :] = moved[4 * LR : 4 * LR + 16]
    send_b[HALO:, :] = moved[4 * LR + 16 :]
    ca.wait()
    cb.wait()


def norm_rows(x, gains, out, rows):
    inv = lax.rsqrt(jnp.mean(x * x, axis=-1, keepdims=True) + EPSILON)
    for c in range(NB):
        cols = slice(c * LANE, (c + 1) * LANE)
        out[rows, cols] = (x[:, cols] * inv * gains[c : c + 1, :]).astype(BF)


def project_own(
    after, audio, gains_in, w_key, w_value, x_o, gain_o, n_s, k_o, v_o, wk_o, wv_o, wkt_o, wvt_o, sems
):
    cx = pltpu.make_async_copy(audio, x_o, sems.at[0])
    cg = pltpu.make_async_copy(gains_in, gain_o, sems.at[1])
    loads = [
        pltpu.make_async_copy(w_key, wk_o, sems.at[2]),
        pltpu.make_async_copy(w_value, wv_o, sems.at[3]),
    ]
    for copy in [cx, cg] + loads:
        copy.start()
    cx.wait()
    cg.wait()
    for r in range(2):
        rows = slice(r * 64, r * 64 + 64)
        norm_rows(x_o[rows, :].astype(F32), gain_o, n_s, rows)
    for load, w_s, wt_s, out_s in zip(loads, (wk_o, wv_o), (wkt_o, wvt_o), (k_o, v_o)):
        load.wait()
        out_s[...] = dot(n_s[...], w_s[...]).astype(BF)
        wt_s[...] = w_s[...].T


def halves(first, second, lo):
    pair = [part.astype(F32)[lo : lo + 8] for part in (first, second)]
    return jnp.concatenate(pair, axis=0).astype(BF)


def stack_pair(after, pair, recv_a, recv_b, out):
    out[: 2 * LR, :] = pair[...]
    out[2 * LR :, :] = halves(recv_a[HALO:, :], recv_b[HALO:, :], 0)


def stack_mate(after, mate, got_pair, recv_a, recv_b, out):
    out[:LR, :] = mate[...] + got_pair[LR : 2 * LR, :]
    out[LR : LR + 16, :] = halves(recv_a[HALO:, :], recv_b[HALO:, :], 8)
    out[LR + 16 :, :] = got_pair[2 * LR :, :]


def stack_latents(after, first, second, out):
    out[:LR, :] = first[...]
    out[LR:, :] = second[...]


def head_mask(j, lo, hi):
    lane = lax.broadcasted_iota(jnp.int32, (1, (hi - lo) * LANE), 1) + lo * LANE
    return jnp.where((lane >= j * HEAD) & (lane < (j + 1) * HEAD), 1.0, 0.0).astype(BF)


def window(g, lo, hi):
    start = g * GROUP + lo * LANE
    return pl.ds(start if isinstance(start, int) else pl.multiple_of(start, LANE), (hi - lo) * LANE)


def add_tiles(tiles, lo, value):
    for t in range(value.shape[1] // LANE):
        part = value[:, t * LANE : (t + 1) * LANE]
        tiles[lo + t] = part if tiles[lo + t] is None else tiles[lo + t] + part


def attend(
    fc_in, w_query, w_out, recv_a, recv_b, x_own, n_own, gains, k_own, v_own, wk_s, wv_s,
    xq_o, q_s, k_s, v_s, p_s, att_s, wq_s, wo_s, fc, n_s, bias_s, sems,
):
    fc_copy = pltpu.make_async_copy(fc_in, fc, sems.at[0])
    fc_copy.start()
    load_q = pltpu.make_async_copy(w_query, wq_s, sems.at[1])
    load_q.start()
    load_o = pltpu.make_async_copy(w_out, wo_s, sems.at[2])
    load_o.start()
    tm = lax.axis_index("tm")
    llm = lax.axis_index("llm")
    even = tm % 2 == 0
    first = tm * FR
    total = lax.axis_size("tm") * FR

    @pl.when(even)
    def _():
        norm_rows(recv_b[:HALO, :].astype(F32), gains, n_s, slice(0, HALO))
        norm_rows(recv_a[:HALO, :].astype(F32), gains, n_s, slice(HALO, 2 * HALO))
        xq_o[0:32, :] = recv_b[64:96, :]
        xq_o[160:192, :] = recv_a[0:32, :]

    @pl.when(jnp.logical_not(even))
    def _():
        norm_rows(recv_a[:HALO, :].astype(F32), gains, n_s, slice(0, HALO))
        norm_rows(recv_b[:HALO, :].astype(F32), gains, n_s, slice(HALO, 2 * HALO))
        xq_o[0:32, :] = recv_a[64:96, :]
        xq_o[160:192, :] = recv_b[0:32, :]

    xq_o[32:160, :] = x_own[...]
    k_s[96:224, :] = k_own[...]
    v_s[96:224, :] = v_own[...]
    for w_s, out_s in ((wk_s, k_s), (wv_s, v_s)):
        @pl.loop(0, NC)
        def _(j, w_s=w_s, out_s=out_s):
            cols = lanes(j, COL)
            new = dot(n_s[...], w_s[:, cols]).astype(BF)
            out_s[0:96, cols] = new[0:96]
            out_s[224:320, cols] = new[96:192]

    queried = jnp.concatenate([n_s[64:96, :], n_own[...], n_s[96:128, :]], axis=0)
    load_q.wait()
    q_s[...] = dot(queried, wq_s[...]).astype(BF)

    fc_copy.wait()
    limit = fc[llm]

    def bias_of(rows, q_first, k_first):
        qe = lax.broadcasted_iota(jnp.int32, (rows, 256), 0) + q_first
        ke = lax.broadcasted_iota(jnp.int32, (rows, 256), 1) + k_first
        kt = ke + (first - HALO)
        ok = (ke >= qe - REACH) & (ke < qe + REACH) & (kt >= 0) & (kt < total) & ((kt < limit) | (ke == qe))
        return jnp.where(ok, 0.0, -1e30)

    bias_s[0:32, :] = bias_of(32, 64, 0)
    bias_s[32:160, :] = bias_of(FR, HALO, 32)
    bias_s[160:192, :] = bias_of(32, 224, 64)

    @pl.loop(0, 4)
    def _(g):
        heads = []
        for j, (lo, hi) in enumerate(WINDOWS):
            win = window(g, lo, hi)
            q = q_s[:, win] * head_mask(j, lo, hi)
            k = k_s[:, win]
            heads.append(
                jnp.concatenate(
                    [dot_t(q[0:32], k[0:256]), dot_t(q[32:160], k[32:288]), dot_t(q[160:192], k[64:320])], axis=0
                )
            )
        heads = [scores * SCALE + bias_s[...] for scores in heads]
        highest = [jnp.max(scores, axis=-1, keepdims=True) for scores in heads]
        heads = [jnp.exp(scores - top) for scores, top in zip(heads, highest)]
        inverse = [1.0 / jnp.sum(powers, axis=-1, keepdims=True) for powers in heads]
        heads = [(powers * inv).astype(BF) for powers, inv in zip(heads, inverse)]
        parts = [[None] * 3 for _ in range(3)]
        for j, (lo, hi) in enumerate(WINDOWS):
            v = v_s[:, window(g, lo, hi)] * head_mask(j, lo, hi)
            p = heads[j]
            p_s[g * 4 + j] = p[32:160]
            add_tiles(parts[0], lo, dot(p[0:32], v[0:256]))
            add_tiles(parts[1], lo, dot(p[32:160], v[32:288]))
            add_tiles(parts[2], lo, dot(p[160:192], v[64:320]))
        for t in range(3):
            at = window(g, t, t + 1)
            att_s[0:32, at] = parts[0][t].astype(BF)
            att_s[32:160, at] = parts[1][t].astype(BF)
            att_s[160:192, at] = parts[2][t].astype(BF)

    load_o.wait()


def spoken_rows(fc, tm, llm):
    frame = lax.broadcasted_iota(jnp.int32, (QR, 1), 0) + (tm * FR - 32)
    return jnp.where((frame >= 0) & (frame < fc[llm]), 1.0, 0.0)


def convolve(
    fc_in, xq, att_s, wo_s, cg_in, lg_in, taps_in,
    lat_o, h_s, dsilu_s, pool_s, inv_o, cg_s, lg_s, tap_s, wot_s, fc, ci_s, up_s, norm_t, sems,
):
    copies = [
        pltpu.make_async_copy(source, into, sems.at[i])
        for i, (source, into) in enumerate(((fc_in, fc), (cg_in, cg_s), (lg_in, lg_s), (taps_in, tap_s)))
    ]
    for copy in copies:
        copy.start()
    tm = lax.axis_index("tm")
    llm = lax.axis_index("llm")

    def hidden_step(j, squares):
        cols = lanes(j, COL)
        h = dot(att_s[...], wo_s[:, cols]) + xq[:, cols].astype(F32)
        h = h.astype(BF).astype(F32)
        for t in range(COL // LANE):
            part = h[:, t * LANE : (t + 1) * LANE]
            h_s[j * (COL // LANE) + t] = part
            squares = squares + part * part
        return squares

    squares = lax.fori_loop(0, NC, hidden_step, jnp.zeros((QR, LANE), F32))
    inv_h = lax.rsqrt(jnp.sum(squares, axis=-1, keepdims=True) * (1.0 / D) + EPSILON)
    inv_o[...] = jnp.broadcast_to(inv_h, (QR, LANE))
    for copy in copies:
        copy.wait()
    inv_spoken = inv_h * spoken_rows(fc, tm, llm)

    def conv_step(c, squares):
        cols = lanes(c)
        wot_s[cols, :] = wo_s[:, cols].T
        ci_s[...] = (h_s[c] * inv_spoken * cg_s[pl.ds(c, 1), :]).astype(BF).astype(F32)
        kern = tap_s[:, cols]
        part = SR // 4
        for at in range(0, SR, part):
            acc = jnp.zeros((part, LANE), F32)
            for s in range(8):
                xs = ci_s[at + s : at + s + part + 24, :]
                for u in range(4):
                    m = s + 8 * u
                    acc = acc + kern[m : m + 1, :] * xs[8 * u : 8 * u + part]
            sig = 0.5 * jnp.tanh(0.5 * acc) + 0.5
            silu = acc * sig
            dsilu_s[c, at : at + part, :] = sig + silu * (1.0 - sig)
            up_s[at : at + part, :] = h_s[c, 16 + at : 16 + at + part, :] + silu
        pooled = up_s[pl.ds(0, PR, 4), :]
        for u in range(1, 4):
            pooled = pooled + up_s[pl.ds(u, PR, 4), :]
        pooled = pooled * 0.25
        pool_s[c] = pooled
        return squares + pooled * pooled

    squares = lax.fori_loop(0, NB, conv_step, jnp.zeros((PR, LANE), F32))
    inv_p = lax.rsqrt(jnp.sum(squares, axis=-1, keepdims=True) * (1.0 / D) + EPSILON)
    for c in range(NB):
        norm_t[...] = pool_s[c] * inv_p * lg_s[c : c + 1, :]
        lat_o[:, c * LANE : (c + 1) * LANE] = norm_t[4:36, :].astype(BF)


def convolve_back(
    fc_in, own, got_pair, got_mate, recv_a, recv_b, h_s, dsilu_s, pool_s, inv_s, cg_s, lg_s, tap_s, wot_s,
    dhid_s, datt_s, fc, g_s, up_s, ds_s, us_s, dnc_s, sems,
):
    copy = pltpu.make_async_copy(fc_in, fc, sems.at[0])
    copy.start()
    tm = lax.axis_index("tm")
    llm = lax.axis_index("llm")
    even = tm % 2 == 0

    row = lax.broadcasted_iota(jnp.int32, (PR, LR + 80), 0)
    col = lax.broadcasted_iota(jnp.int32, (PR, LR + 80), 1)
    is_left = row < 4
    is_right = row >= PR - 4
    r = jnp.where(is_left, row, row - (PR - 4))
    label = jnp.where(is_left, 1 - tm % 2, tm % 2)
    side = (
        (col == 44 + 16 * label + r) | (col == 64 + 8 * label + r)
        | (col == 80 + 8 * label + r) | (col == 100 + 8 * label + r)
    ) & (is_left | is_right)
    middle = (col < LR) & (col == row - 4)
    at = tm * LR + row - 4
    chosen = (side | middle) & (at >= 0) & (at < lax.axis_size("tm") * LR)
    chosen = jnp.where(chosen, 1.0, 0.0).astype(BF)
    stacked = jnp.concatenate(
        [
            own[...] + got_pair[:LR, :] + got_mate[:LR, :],
            recv_a[HALO:, :],
            recv_b[HALO:, :],
            got_pair[2 * LR :, :],
            got_mate[LR:, :],
        ],
        axis=0,
    )
    g_s[...] = dot(chosen, stacked)

    def sums(c, carry):
        squares, along = carry
        pooled = pool_s[c]
        return squares + pooled * pooled, along + g_s[:, lanes(c)] * lg_s[pl.ds(c, 1), :] * pooled

    zero = jnp.zeros((PR, LANE), F32)
    squares, along = lax.fori_loop(0, NB, sums, (zero, zero))
    inv_p = lax.rsqrt(jnp.sum(squares, axis=-1, keepdims=True) * (1.0 / D) + EPSILON)
    back_p = inv_p * inv_p * inv_p * (jnp.sum(along, axis=-1, keepdims=True) * (1.0 / D))
    inv_own = inv_s[32:160, :]
    copy.wait()
    spoken_own = spoken_rows(fc, tm, llm)[32:160]

    def conv_back(c, along):
        cols = lanes(c)
        gain = lg_s[pl.ds(c, 1), :]
        dpool = (g_s[:, cols] * gain * inv_p - pool_s[c] * back_p) * 0.25
        for u in range(4):
            up_s[pl.ds(u, PR, 4), :] = dpool
        ds_s[...] = up_s[...] * dsilu_s[c]
        us_s[c] = up_s[16 : 16 + FR, :]
        kern = tap_s[:, cols]
        part = FR // 4
        sums = []
        for at in range(0, FR, part):
            acc = jnp.zeros((part, LANE), F32)
            for s in range(8):
                base = 8 if s == 0 else s
                xs = ds_s[at + base : at + base + part + 24, :]
                for u in range(4):
                    m = 32 - base - 8 * u
                    acc = acc + kern[m : m + 1, :] * xs[8 * u : 8 * u + part]
            dn = acc.astype(BF).astype(F32) * spoken_own[at : at + part] * cg_s[pl.ds(c, 1), :]
            dnc_s[c, at : at + part, :] = dn
            sums.append(along[at : at + part] + dn * h_s[c, 32 + at : 32 + at + part, :])
        return jnp.concatenate(sums, axis=0)

    along = lax.fori_loop(0, NB, conv_back, jnp.zeros((FR, LANE), F32))
    back_h = inv_own * inv_own * inv_own * (jnp.sum(along, axis=-1, keepdims=True) * (1.0 / D))

    @pl.loop(0, NB)
    def _(c):
        dhid_s[:, lanes(c)] = (us_s[c] + dnc_s[c] * inv_own - h_s[c, 32:160, :] * back_h).astype(BF)

    @pl.loop(0, NC)
    def _(j):
        datt_s[:, lanes(j, COL)] = dot(dhid_s[...], wot_s[:, lanes(j, COL)]).astype(BF)


def attend_back(after, q_s, v_s, p_s, datt_s, wkt_s, wvt_s, send_a, send_b, ds_o, dk_s, dv_s, ek_s, ev_s):
    @pl.loop(0, 4)
    def _(g):
        heads = []
        for j, (lo, hi) in enumerate(WINDOWS):
            win = window(g, lo, hi)
            heads.append(dot_t(datt_s[:, win] * head_mask(j, lo, hi), v_s[32:288, win]))
        weights = [p_s[g * 4 + j].astype(F32) for j in range(4)]
        heads = [w * dp for w, dp in zip(weights, heads)]
        sums = [jnp.sum(pd, axis=-1, keepdims=True) for pd in heads]
        heads = [((pd - w * total) * SCALE).astype(BF) for pd, w, total in zip(heads, weights, sums)]
        dk, dv = [None] * 3, [None] * 3
        for j, (lo, hi) in enumerate(WINDOWS):
            win = window(g, lo, hi)
            mask = head_mask(j, lo, hi)
            ds_o[g * 4 + j] = heads[j]
            add_tiles(dk, lo, t_dot(heads[j], q_s[32:160, win] * mask))
            add_tiles(dv, lo, t_dot(p_s[g * 4 + j], datt_s[:, win] * mask))
        for t in range(3):
            at = window(g, t, t + 1)
            for out, edge, tiles in ((dk_s, ek_s, dk), (dv_s, ev_s, dv)):
                new = tiles[t].astype(BF)
                edge[0:64, at] = new[0:64]
                out[:, at] = new[64:192]
                edge[64:128, at] = new[192:256]

    even = lax.axis_index("tm") % 2 == 0

    @pl.loop(0, NC)
    def _(j):
        cols = lanes(j, COL)
        both = (dot(ek_s[...], wkt_s[:, cols]) + dot(ev_s[...], wvt_s[:, cols])).astype(BF)

        @pl.when(even)
        def _():
            send_a[:, cols] = both[64:128]
            send_b[:, cols] = both[0:64]

        @pl.when(jnp.logical_not(even))
        def _():
            send_a[:, cols] = both[0:64]
            send_b[:, cols] = both[64:128]


def project_back(after, ds_s, k_s, dk, dv, wq_s, wkt_s, wvt_s, dn_o, dq_s):
    for g in range(4):
        dq = [None] * 3
        for j, (lo, hi) in enumerate(WINDOWS):
            add_tiles(dq, lo, dot(ds_s[g * 4 + j], k_s[32:288, window(g, lo, hi)] * head_mask(j, lo, hi)))
        for t in range(3):
            dq_s[:, window(g, t, t + 1)] = dq[t].astype(BF)
    dn_o[...] = dot(dk[...], wkt_s[...]) + dot(dv[...], wvt_s[...]) + dot_t(dq_s[...], wq_s[...])


def finish(
    fc_in, tl_in, x_s, dh_s, dn_s, recv_a, recv_b, l0, l1, l23, gains,
    rows_out, grad_out, fc, tl, r_s, g_s, out_s, rows_s, sems,
):
    cf = pltpu.make_async_copy(fc_in, fc, sems.at[0])
    ct = pltpu.make_async_copy(tl_in, tl, sems.at[1])
    cf.start()
    ct.start()
    tm = lax.axis_index("tm")
    llm = lax.axis_index("llm")
    even = tm % 2 == 0

    @pl.when(even)
    def _():
        r_s[0:64, :] = recv_b[...]
        r_s[64:128, :] = recv_a[...]

    @pl.when(jnp.logical_not(even))
    def _():
        r_s[0:64, :] = recv_a[...]
        r_s[64:128, :] = recv_b[...]

    copies = []
    for half in range(2):
        rows = slice(half * 64, half * 64 + 64)
        inside = (tm > 0) if half == 0 else (tm < lax.axis_size("tm") - 1)
        keep = jnp.where(inside, 1.0, 0.0)
        x = x_s[rows, :].astype(F32)
        inv = lax.rsqrt(jnp.mean(x * x, axis=-1, keepdims=True) + EPSILON)
        along = jnp.zeros((64, LANE), F32)
        for c in range(NB):
            cols = slice(c * LANE, (c + 1) * LANE)
            g = (dn_s[rows, cols] + r_s[rows, cols].astype(F32) * keep).astype(BF).astype(F32) * gains[c : c + 1, :]
            g_s[rows, cols] = g
            along = along + g * x[:, cols]
        back = inv * inv * inv * (jnp.sum(along, axis=-1, keepdims=True) * (1.0 / D))
        out_s[rows, :] = (dh_s[rows, :].astype(F32) + g_s[rows, :] * inv - x * back).astype(BF)
        copy = pltpu.make_async_copy(out_s.at[rows], grad_out.at[rows], sems.at[2 + half])
        copy.start()
        copies.append(copy)
    cf.wait()
    ct.wait()
    starts, lives = routes(fc, tl, tm)
    slot = lax.broadcasted_iota(jnp.int32, (SLOTS, NREC * LR), 0) + llm * SLOTS
    col = lax.broadcasted_iota(jnp.int32, (SLOTS, NREC * LR), 1)
    chosen = jnp.zeros((SLOTS, NREC * LR), F32)
    for j, apart in enumerate((0, 1, 3, 2)):
        b = llm ^ apart
        r = col - j * LR
        hit = (r >= 0) & (r < pick(lives, b)) & (slot == r + pick(starts, b))
        chosen = jnp.where(hit, 1.0, chosen)
    latents = jnp.concatenate([l0[...], l1[...], l23[...]], axis=0)
    rows_s[...] = dot(chosen.astype(BF), latents).astype(BF)
    copy = pltpu.make_async_copy(rows_s, rows_out, sems.at[4])
    copy.start()
    for copy in copies + [copy]:
        copy.wait()


def swap(count, cells_a, cells_b):
    pairs_a = [(i, i ^ 1) for i in range(count)]
    n = lax.axis_size("llm")
    full_b = []
    for i in range(count):
        partner = ((i + 1) ^ 1) - 1
        end = partner < 0 or partner >= count
        full_b += [(i * n + y, i * n + (y ^ 1) if end else partner * n + y) for y in range(n)]
    return lax.ppermute(cells_a, "tm", pairs_a), lax.ppermute(cells_b, ("tm", "llm"), full_b)


def trade(cells, apart):
    n = lax.axis_size("llm")
    return lax.ppermute(cells, "llm", [(i, i ^ apart) for i in range(n)])


def hbm(array):
    return pltpu.with_memory_space_constraint(array, pltpu.HBM)


def vmem(array):
    return pltpu.with_memory_space_constraint(array, pltpu.VMEM)


def call(kernel, ins, outs, scratch, flops, outs_in_hbm=False):
    place = {"h": hbm, "v": vmem, "n": lambda array: array}
    spec = {"h": ANY, "v": VMEM, "n": ANY}
    if outs_in_hbm:
        shapes = [jax.ShapeDtypeStruct(s, d) for s, d in outs]
    else:
        shapes = [pltpu.VMEM(s, d) for s, d in outs]
    return pl.pallas_call(
        kernel,
        out_shape=shapes,
        in_specs=[spec[kind] for kind, _ in ins],
        out_specs=[ANY if outs_in_hbm else VMEM] * len(outs),
        scratch_shapes=scratch,
        compiler_params=pltpu.CompilerParams(vmem_limit_bytes=12 * 1024 * 1024),
        cost_estimate=pl.CostEstimate(flops=flops, bytes_accessed=1_000_000, transcendentals=0),
        name=kernel.__name__,
    )(*[place[kind](array) for kind, array in ins])


def mark(kind, *arrays):
    return [(kind, array) for array in arrays]


def on_device(
    audio, frame_counts, text_lengths, norm_gain, w_query, w_key, w_value, w_out,
    conv_gain, conv_kernel, latent_gain, llm_grads,
):
    signal = audio[0]
    n_tm = lax.axis_size("tm")
    norm_row, conv_row, latent_row = (g.reshape(NB, LANE) for g in (norm_gain, conv_gain, latent_gain))
    tl_in = text_lengths.T
    V = pltpu.VMEM
    fc = pltpu.SMEM((NREC,), jnp.int32)
    tl = pltpu.SMEM((NREC, n_tm), jnp.int32)
    gain = ((NB, LANE), F32)
    weight = ((D, D), BF)

    def rows(n, dtype=BF):
        return ((n, D), dtype)

    def sems(*dims):
        return pltpu.SemaphoreType.DMA(dims)

    send_a, send_b, own, pair, mate = call(
        prepare,
        mark("h", frame_counts, tl_in, signal, llm_grads[0]),
        [rows(HALO + 16), rows(HALO + 16), rows(LR), rows(2 * LR), rows(LR)],
        [fc, tl, V((SLOTS, D), BF), sems(5)],
        100_000_000,
    )
    recv_a, recv_b = swap(n_tm, send_a, send_b)
    x, gains, normed, k_own, v_own, wk, wv, wkt, wvt = call(
        project_own,
        mark("v", own) + mark("h", signal, norm_row, w_key, w_value),
        [rows(FR), gain, rows(FR), rows(FR), rows(FR), weight, weight, weight, weight],
        [sems(4)],
        6_000_000_000,
    )
    (pairs,) = call(stack_pair, mark("v", gains, pair, recv_a, recv_b), [rows(2 * LR + 16)], [], 1_000_000)
    got_pair = trade(pairs, 1)
    xq, q, k, v, p, att, wq, wo = call(
        attend,
        mark("h", frame_counts, w_query, w_out)
        + mark("v", recv_a, recv_b, x, normed, gains, k_own, v_own, wk, wv),
        [rows(QR), rows(QR), rows(EXT), rows(EXT), ((16, FR, 256), BF), rows(QR), weight, weight],
        [fc, V((2 * HALO, D), BF), V((QR, 256), F32), sems(3)],
        8_000_000_000,
    )
    (mates,) = call(stack_mate, mark("v", xq, mate, got_pair, recv_a, recv_b), [rows(LR + 32)], [], 1_000_000)
    got_mate = trade(mates, 3)
    latent, h, dsilu, pool, inv, cgain, lgain, taps, wot = call(
        convolve,
        mark("h", frame_counts) + mark("v", xq, att, wo) + mark("h", conv_row, latent_row, conv_kernel),
        [
            rows(LR), ((NB, QR, LANE), F32), ((NB, SR, LANE), F32), ((NB, PR, LANE), F32), ((QR, LANE), F32),
            gain, gain, rows(KERN, F32), weight,
        ],
        [fc, V((QR, LANE), F32), V((SR, LANE), F32), V((PR, LANE), F32), sems(4)],
        5_000_000_000,
    )
    latent_1 = trade(latent, 1)
    dhid, datt = call(
        convolve_back,
        mark("h", frame_counts)
        + mark("v", own, got_pair, got_mate, recv_a, recv_b, h, dsilu, pool, inv, cgain, lgain, taps, wot),
        [rows(FR), rows(FR)],
        [
            fc, V((PR, D), F32), V((SR, LANE), F32), V((SR, LANE), F32), V((NB, FR, LANE), F32),
            V((NB, FR, LANE), F32), sems(1),
        ],
        5_000_000_000,
    )
    (latents,) = call(stack_latents, mark("v", dhid, latent, latent_1), [rows(2 * LR)], [], 1_000_000)
    latent_23 = trade(latents, 3)
    back_a, back_b, ds, dk, dv = call(
        attend_back,
        mark("v", latents, q, v, p, datt, wkt, wvt),
        [rows(64), rows(64), ((16, FR, 256), BF), rows(FR), rows(FR)],
        [V((FR, D), BF), V((FR, D), BF)],
        6_000_000_000,
    )
    ret_a, ret_b = swap(n_tm, back_a, back_b)
    (dn,) = call(
        project_back,
        mark("v", back_a, ds, k, dk, dv, wq, wkt, wvt),
        [rows(FR, F32)],
        [V((FR, D), BF)],
        3_000_000_000,
    )
    out_rows, grad = call(
        finish,
        mark("h", frame_counts, tl_in)
        + mark("v", x, dhid, dn, ret_a, ret_b, latent, latent_1, latent_23, gains),
        [rows(SLOTS), rows(FR)],
        [fc, tl, V((FR, D), BF), V((FR, D), F32), V((FR, D), BF), V((SLOTS, D), BF), sems(5)],
        1_000_000_000,
        outs_in_hbm=True,
    )
    return (out_rows[None], grad[None])


def solution(mesh):
    placed = (P("llm", "tm", None),) + (P(),) * 10 + (P("tm", "llm", None),)
    return jax.shard_map(
        on_device,
        mesh=mesh,
        in_specs=placed,
        out_specs=(P("tm", "llm", None), P("llm", "tm", None)),
        check_vma=False,
    )
```

```python
import jax
import jax.numpy as jnp
from jax import lax
from jax.experimental import pallas as pl
from jax.experimental.pallas import tpu as pltpu
from jax.sharding import PartitionSpec as P

D = 1536
REACH = 64
KERN = 32
FR = 128
HALO = 96
EXT = FR + 2 * HALO
QR = FR + 64
SR = FR + 32
PR = SR // 4
LR = FR // 4
SLOTS = 64
NREC = 4
HEAD = 96
HEADS = 16
LANE = 128
NB = D // LANE
COL = 1536
NC = D // COL
GROUP = 4 * HEAD
EPSILON = 1e-06
SCALE = HEAD ** (-0.5)
BF = jnp.bfloat16
F32 = jnp.float32
WINDOWS = ((0, 1), (0, 2), (1, 3), (2, 3))

VMEM = pl.BlockSpec(memory_space=pltpu.VMEM)
ANY = pl.BlockSpec(memory_space=pl.ANY)


def dot(a, b):
    return lax.dot_general(a, b, (((1,), (0,)), ((), ())), preferred_element_type=F32)


def dot_t(a, b):
    return lax.dot_general(a, b, (((1,), (1,)), ((), ())), preferred_element_type=F32)


def t_dot(a, b):
    return lax.dot_general(a, b, (((0,), (0,)), ((), ())), preferred_element_type=F32)


def lanes(c, width=LANE):
    return pl.ds(pl.multiple_of(c * width, width), width)


def routes(fc, tl, slice_index):
    starts, lives = [], []
    total = 0
    for b in range(NREC):
        live = jnp.clip(fc[b] // 4 - slice_index * LR, 0, LR)
        total = total + tl[b, slice_index]
        starts.append(total)
        lives.append(live)
        total = total + live
    return starts, lives


def pick(values, index):
    out = values[0]
    for b in range(1, NREC):
        out = jnp.where(index == b, values[b], out)
    return out


def prepare(fc_in, tl_in, audio, grads, send_a, send_b, own, pair, mate, fc, tl, g_buf, sems):
    cf = pltpu.make_async_copy(fc_in, fc, sems.at[0])
    ct = pltpu.make_async_copy(tl_in, tl, sems.at[1])
    cf.start()
    ct.start()
    tm = lax.axis_index("tm")
    llm = lax.axis_index("llm")
    off_a = (1 - tm % 2) * (FR - HALO)
    off_b = (FR - HALO) - off_a
    cg = pltpu.make_async_copy(grads, g_buf, sems.at[2])
    ca = pltpu.make_async_copy(
        audio.at[pl.ds(pl.multiple_of(off_a, 32), HALO)], send_a.at[pl.ds(0, HALO)], sems.at[3]
    )
    cb = pltpu.make_async_copy(
        audio.at[pl.ds(pl.multiple_of(off_b, 32), HALO)], send_b.at[pl.ds(0, HALO)], sems.at[4]
    )
    cg.start()
    ca.start()
    cb.start()
    cf.wait()
    ct.wait()
    starts, lives = routes(fc, tl, tm)
    row = lax.broadcasted_iota(jnp.int32, (LR, SLOTS), 0)
    slot = lax.broadcasted_iota(jnp.int32, (LR, SLOTS), 1) + llm * SLOTS
    starts = [pick(starts, llm ^ j) for j in range(NREC)]
    lives = [pick(lives, llm ^ j) for j in range(NREC)]
    picked = []
    for j in range(NREC):
        chosen = (row < lives[j]) & (slot == row + starts[j])
        picked.append(jnp.where(chosen, 1.0, 0.0).astype(BF))
    place = lax.broadcasted_iota(jnp.int32, (16, SLOTS), 0)
    slot = lax.broadcasted_iota(jnp.int32, (16, SLOTS), 1) + llm * SLOTS
    for offset in ((1 - tm % 2) * (LR - 4), (tm % 2) * (LR - 4)):
        r = place % 4 + offset
        chosen = jnp.zeros((16, SLOTS), F32)
        for j in range(NREC):
            hit = (place // 4 == (j + 3) % 4) & (r < lives[j]) & (slot == r + starts[j])
            chosen = jnp.where(hit, 1.0, chosen)
        picked.append(chosen.astype(BF))
    cg.wait()
    moved = dot(jnp.concatenate(picked, axis=0), g_buf[...]).astype(BF)
    own[...] = moved[:LR]
    pair[...] = moved[LR : 3 * LR]
    mate[...] = moved[3 * LR : 4 * LR]
    send_a[HALO:, :] = moved[4 * LR : 4 * LR + 16]
    send_b[HALO:, :] = moved[4 * LR + 16 :]
    ca.wait()
    cb.wait()


def norm_rows(x, gains, out, rows):
    inv = lax.rsqrt(jnp.mean(x * x, axis=-1, keepdims=True) + EPSILON)
    for c in range(NB):
        cols = slice(c * LANE, (c + 1) * LANE)
        out[rows, cols] = (x[:, cols] * inv * gains[c : c + 1, :]).astype(BF)


def project_own(
    after, audio, gains_in, w_key, w_value, x_o, gain_o, n_s, k_o, v_o, wk_o, wv_o, wkt_o, wvt_o, sems
):
    cx = pltpu.make_async_copy(audio, x_o, sems.at[0])
    cg = pltpu.make_async_copy(gains_in, gain_o, sems.at[1])
    loads = [
        pltpu.make_async_copy(w_key, wk_o, sems.at[2]),
        pltpu.make_async_copy(w_value, wv_o, sems.at[3]),
    ]
    for copy in [cx, cg] + loads:
        copy.start()
    cx.wait()
    cg.wait()
    for r in range(2):
        rows = slice(r * 64, r * 64 + 64)
        norm_rows(x_o[rows, :].astype(F32), gain_o, n_s, rows)
    for load, w_s, wt_s, out_s in zip(loads, (wk_o, wv_o), (wkt_o, wvt_o), (k_o, v_o)):
        load.wait()
        out_s[...] = dot(n_s[...], w_s[...]).astype(BF)
        wt_s[...] = w_s[...].T


def halves(first, second, lo):
    pair = [part.astype(F32)[lo : lo + 8] for part in (first, second)]
    return jnp.concatenate(pair, axis=0).astype(BF)


def stack_pair(after, pair, recv_a, recv_b, out):
    out[: 2 * LR, :] = pair[...]
    out[2 * LR :, :] = halves(recv_a[HALO:, :], recv_b[HALO:, :], 0)


def stack_mate(after, mate, got_pair, recv_a, recv_b, out):
    out[:LR, :] = mate[...] + got_pair[LR : 2 * LR, :]
    out[LR : LR + 16, :] = halves(recv_a[HALO:, :], recv_b[HALO:, :], 8)
    out[LR + 16 :, :] = got_pair[2 * LR :, :]


def stack_latents(after, first, second, out):
    out[:LR, :] = first[...]
    out[LR:, :] = second[...]


def head_mask(j, lo, hi):
    lane = lax.broadcasted_iota(jnp.int32, (1, (hi - lo) * LANE), 1) + lo * LANE
    return jnp.where((lane >= j * HEAD) & (lane < (j + 1) * HEAD), 1.0, 0.0).astype(BF)


def window(g, lo, hi):
    start = g * GROUP + lo * LANE
    return pl.ds(start if isinstance(start, int) else pl.multiple_of(start, LANE), (hi - lo) * LANE)


def add_tiles(tiles, lo, value):
    for t in range(value.shape[1] // LANE):
        part = value[:, t * LANE : (t + 1) * LANE]
        tiles[lo + t] = part if tiles[lo + t] is None else tiles[lo + t] + part


def attend(
    fc_in, w_query, w_out, recv_a, recv_b, x_own, n_own, gains, k_own, v_own, wk_s, wv_s,
    xq_o, q_s, k_s, v_s, p_s, att_s, wq_s, wo_s, fc, n_s, bias_s, sems,
):
    fc_copy = pltpu.make_async_copy(fc_in, fc, sems.at[0])
    fc_copy.start()
    load_q = pltpu.make_async_copy(w_query, wq_s, sems.at[1])
    load_q.start()
    load_o = pltpu.make_async_copy(w_out, wo_s, sems.at[2])
    tm = lax.axis_index("tm")
    llm = lax.axis_index("llm")
    even = tm % 2 == 0
    first = tm * FR
    total = lax.axis_size("tm") * FR

    @pl.when(even)
    def _():
        norm_rows(recv_b[:HALO, :].astype(F32), gains, n_s, slice(0, HALO))
        norm_rows(recv_a[:HALO, :].astype(F32), gains, n_s, slice(HALO, 2 * HALO))
        xq_o[0:32, :] = recv_b[64:96, :]
        xq_o[160:192, :] = recv_a[0:32, :]

    @pl.when(jnp.logical_not(even))
    def _():
        norm_rows(recv_a[:HALO, :].astype(F32), gains, n_s, slice(0, HALO))
        norm_rows(recv_b[:HALO, :].astype(F32), gains, n_s, slice(HALO, 2 * HALO))
        xq_o[0:32, :] = recv_a[64:96, :]
        xq_o[160:192, :] = recv_b[0:32, :]

    xq_o[32:160, :] = x_own[...]
    k_s[96:224, :] = k_own[...]
    v_s[96:224, :] = v_own[...]
    for w_s, out_s in ((wk_s, k_s), (wv_s, v_s)):
        @pl.loop(0, NC)
        def _(j, w_s=w_s, out_s=out_s):
            cols = lanes(j, COL)
            new = dot(n_s[...], w_s[:, cols]).astype(BF)
            out_s[0:96, cols] = new[0:96]
            out_s[224:320, cols] = new[96:192]

    queried = jnp.concatenate([n_s[64:96, :], n_own[...], n_s[96:128, :]], axis=0)
    load_q.wait()
    load_o.start()
    q_s[...] = dot(queried, wq_s[...]).astype(BF)

    fc_copy.wait()
    limit = fc[llm]

    def bias_of(rows, q_first, k_first):
        qe = lax.broadcasted_iota(jnp.int32, (rows, 256), 0) + q_first
        ke = lax.broadcasted_iota(jnp.int32, (rows, 256), 1) + k_first
        kt = ke + (first - HALO)
        ok = (ke >= qe - REACH) & (ke < qe + REACH) & (kt >= 0) & (kt < total) & ((kt < limit) | (ke == qe))
        return jnp.where(ok, 0.0, -1e30)

    bias_s[0:32, :] = bias_of(32, 64, 0)
    bias_s[32:160, :] = bias_of(FR, HALO, 32)
    bias_s[160:192, :] = bias_of(32, 224, 64)

    for base in range(0, HEADS, 16):
        some = [(h, h // 4, WINDOWS[h % 4]) for h in range(base, base + 16)]
        heads = []
        for h, g, (lo, hi) in some:
            q = q_s[:, window(g, lo, hi)] * head_mask(h % 4, lo, hi)
            k = k_s[:, window(g, lo, hi)]
            heads.append(
                jnp.concatenate(
                    [dot_t(q[0:32], k[0:256]), dot_t(q[32:160], k[32:288]), dot_t(q[160:192], k[64:320])], axis=0
                )
            )
        heads = [scores * SCALE + bias_s[...] for scores in heads]
        highest = [jnp.max(scores, axis=-1, keepdims=True) for scores in heads]
        heads = [jnp.exp(scores - top) for scores, top in zip(heads, highest)]
        inverse = [1.0 / jnp.sum(powers, axis=-1, keepdims=True) for powers in heads]
        heads = [(powers * inv).astype(BF) for powers, inv in zip(heads, inverse)]
        for g in range(base // 4, (base + 16) // 4):
            parts = [[None] * 3 for _ in range(3)]
            for (h, of, (lo, hi)), p in zip(some, heads):
                if of != g:
                    continue
                v = v_s[:, window(g, lo, hi)] * head_mask(h % 4, lo, hi)
                p_s[h] = p[32:160]
                add_tiles(parts[0], lo, dot(p[0:32], v[0:256]))
                add_tiles(parts[1], lo, dot(p[32:160], v[32:288]))
                add_tiles(parts[2], lo, dot(p[160:192], v[64:320]))
            for t in range(3):
                at = window(g, t, t + 1)
                att_s[0:32, at] = parts[0][t].astype(BF)
                att_s[32:160, at] = parts[1][t].astype(BF)
                att_s[160:192, at] = parts[2][t].astype(BF)

    load_o.wait()


def spoken_rows(fc, tm, llm):
    frame = lax.broadcasted_iota(jnp.int32, (QR, 1), 0) + (tm * FR - 32)
    return jnp.where((frame >= 0) & (frame < fc[llm]), 1.0, 0.0)


def convolve(
    fc_in, xq, att_s, wo_s, cg_in, lg_in, taps_in,
    lat_o, h_s, dsilu_s, pool_s, inv_o, cg_s, lg_s, tap_s, wot_s, fc, ci_s, up_s, norm_t, sems,
):
    copies = [
        pltpu.make_async_copy(source, into, sems.at[i])
        for i, (source, into) in enumerate(((fc_in, fc), (cg_in, cg_s), (lg_in, lg_s), (taps_in, tap_s)))
    ]
    for copy in copies:
        copy.start()
    tm = lax.axis_index("tm")
    llm = lax.axis_index("llm")

    def hidden_step(j, squares):
        cols = lanes(j, COL)
        h = dot(att_s[...], wo_s[:, cols]) + xq[:, cols].astype(F32)
        h = h.astype(BF).astype(F32)
        for t in range(COL // LANE):
            part = h[:, t * LANE : (t + 1) * LANE]
            h_s[j * (COL // LANE) + t] = part
            squares = squares + part * part
        return squares

    squares = lax.fori_loop(0, NC, hidden_step, jnp.zeros((QR, LANE), F32))
    inv_h = lax.rsqrt(jnp.sum(squares, axis=-1, keepdims=True) * (1.0 / D) + EPSILON)
    inv_o[...] = jnp.broadcast_to(inv_h, (QR, LANE))
    for copy in copies:
        copy.wait()
    inv_spoken = inv_h * spoken_rows(fc, tm, llm)

    def conv_step(c, squares):
        cols = lanes(c)
        wot_s[cols, :] = wo_s[:, cols].T
        ci_s[...] = (h_s[c] * inv_spoken * cg_s[pl.ds(c, 1), :]).astype(BF).astype(F32)
        kern = tap_s[:, cols]
        part = SR // 4
        for at in range(0, SR, part):
            acc = jnp.zeros((part, LANE), F32)
            for s in range(8):
                xs = ci_s[at + s : at + s + part + 24, :]
                for u in range(4):
                    m = s + 8 * u
                    acc = acc + kern[m : m + 1, :] * xs[8 * u : 8 * u + part]
            sig = 0.5 * jnp.tanh(0.5 * acc) + 0.5
            silu = acc * sig
            dsilu_s[c, at : at + part, :] = sig + silu * (1.0 - sig)
            up_s[at : at + part, :] = h_s[c, 16 + at : 16 + at + part, :] + silu
        pooled = up_s[pl.ds(0, PR, 4), :]
        for u in range(1, 4):
            pooled = pooled + up_s[pl.ds(u, PR, 4), :]
        pooled = pooled * 0.25
        pool_s[c] = pooled
        return squares + pooled * pooled

    squares = lax.fori_loop(0, NB, conv_step, jnp.zeros((PR, LANE), F32))
    inv_p = lax.rsqrt(jnp.sum(squares, axis=-1, keepdims=True) * (1.0 / D) + EPSILON)
    for c in range(NB):
        norm_t[...] = pool_s[c] * inv_p * lg_s[c : c + 1, :]
        lat_o[:, c * LANE : (c + 1) * LANE] = norm_t[4:36, :].astype(BF)


def convolve_back(
    fc_in, own, got_pair, got_mate, recv_a, recv_b, h_s, dsilu_s, pool_s, inv_s, cg_s, lg_s, tap_s, wot_s,
    dhid_s, datt_s, fc, g_s, up_s, ds_s, us_s, dnc_s, sems,
):
    copy = pltpu.make_async_copy(fc_in, fc, sems.at[0])
    copy.start()
    tm = lax.axis_index("tm")
    llm = lax.axis_index("llm")
    even = tm % 2 == 0

    row = lax.broadcasted_iota(jnp.int32, (PR, LR + 80), 0)
    col = lax.broadcasted_iota(jnp.int32, (PR, LR + 80), 1)
    is_left = row < 4
    is_right = row >= PR - 4
    r = jnp.where(is_left, row, row - (PR - 4))
    label = jnp.where(is_left, 1 - tm % 2, tm % 2)
    side = (
        (col == 44 + 16 * label + r) | (col == 64 + 8 * label + r)
        | (col == 80 + 8 * label + r) | (col == 100 + 8 * label + r)
    ) & (is_left | is_right)
    middle = (col < LR) & (col == row - 4)
    at = tm * LR + row - 4
    chosen = (side | middle) & (at >= 0) & (at < lax.axis_size("tm") * LR)
    chosen = jnp.where(chosen, 1.0, 0.0).astype(BF)
    stacked = jnp.concatenate(
        [
            own[...] + got_pair[:LR, :] + got_mate[:LR, :],
            recv_a[HALO:, :],
            recv_b[HALO:, :],
            got_pair[2 * LR :, :],
            got_mate[LR:, :],
        ],
        axis=0,
    )
    g_s[...] = dot(chosen, stacked)

    def sums(c, carry):
        squares, along = carry
        pooled = pool_s[c]
        return squares + pooled * pooled, along + g_s[:, lanes(c)] * lg_s[pl.ds(c, 1), :] * pooled

    zero = jnp.zeros((PR, LANE), F32)
    squares, along = lax.fori_loop(0, NB, sums, (zero, zero))
    inv_p = lax.rsqrt(jnp.sum(squares, axis=-1, keepdims=True) * (1.0 / D) + EPSILON)
    back_p = inv_p * inv_p * inv_p * (jnp.sum(along, axis=-1, keepdims=True) * (1.0 / D))
    inv_own = inv_s[32:160, :]
    copy.wait()
    spoken_own = spoken_rows(fc, tm, llm)[32:160]

    def conv_back(c, along):
        cols = lanes(c)
        gain = lg_s[pl.ds(c, 1), :]
        dpool = (g_s[:, cols] * gain * inv_p - pool_s[c] * back_p) * 0.25
        for u in range(4):
            up_s[pl.ds(u, PR, 4), :] = dpool
        ds_s[...] = up_s[...] * dsilu_s[c]
        us_s[c] = up_s[16 : 16 + FR, :]
        kern = tap_s[:, cols]
        part = FR // 4
        sums = []
        for at in range(0, FR, part):
            acc = jnp.zeros((part, LANE), F32)
            for s in range(8):
                base = 8 if s == 0 else s
                xs = ds_s[at + base : at + base + part + 24, :]
                for u in range(4):
                    m = 32 - base - 8 * u
                    acc = acc + kern[m : m + 1, :] * xs[8 * u : 8 * u + part]
            dn = acc.astype(BF).astype(F32) * spoken_own[at : at + part] * cg_s[pl.ds(c, 1), :]
            dnc_s[c, at : at + part, :] = dn
            sums.append(along[at : at + part] + dn * h_s[c, 32 + at : 32 + at + part, :])
        return jnp.concatenate(sums, axis=0)

    along = lax.fori_loop(0, NB, conv_back, jnp.zeros((FR, LANE), F32), unroll=2)
    back_h = inv_own * inv_own * inv_own * (jnp.sum(along, axis=-1, keepdims=True) * (1.0 / D))

    @pl.loop(0, NB)
    def _(c):
        dhid_s[:, lanes(c)] = (us_s[c] + dnc_s[c] * inv_own - h_s[c, 32:160, :] * back_h).astype(BF)

    @pl.loop(0, NC)
    def _(j):
        datt_s[:, lanes(j, COL)] = dot(dhid_s[...], wot_s[:, lanes(j, COL)]).astype(BF)


def attend_back(after, q_s, v_s, p_s, datt_s, wkt_s, wvt_s, send_a, send_b, ds_o, dk_s, dv_s, ek_s, ev_s):
    for base in range(0, HEADS, 16):
        some = [(h, h // 4, WINDOWS[h % 4]) for h in range(base, base + 16)]
        heads = []
        for h, g, (lo, hi) in some:
            win = window(g, lo, hi)
            heads.append(dot_t(datt_s[:, win] * head_mask(h % 4, lo, hi), v_s[32:288, win]))
        weights = [p_s[h].astype(F32) for h, _, _ in some]
        heads = [w * dp for w, dp in zip(weights, heads)]
        sums = [jnp.sum(pd, axis=-1, keepdims=True) for pd in heads]
        heads = [((pd - w * total) * SCALE).astype(BF) for pd, w, total in zip(heads, weights, sums)]
        for g in range(base // 4, (base + 16) // 4):
            dk, dv = [None] * 3, [None] * 3
            for (h, of, (lo, hi)), ds in zip(some, heads):
                if of != g:
                    continue
                win = window(g, lo, hi)
                mask = head_mask(h % 4, lo, hi)
                ds_o[h] = ds
                add_tiles(dk, lo, t_dot(ds, q_s[32:160, win] * mask))
                add_tiles(dv, lo, t_dot(p_s[h], datt_s[:, win] * mask))
            for t in range(3):
                at = window(g, t, t + 1)
                for out, edge, tiles in ((dk_s, ek_s, dk), (dv_s, ev_s, dv)):
                    new = tiles[t].astype(BF)
                    edge[0:64, at] = new[0:64]
                    out[:, at] = new[64:192]
                    edge[64:128, at] = new[192:256]

    even = lax.axis_index("tm") % 2 == 0

    @pl.loop(0, NC)
    def _(j):
        cols = lanes(j, COL)
        both = (dot(ek_s[...], wkt_s[:, cols]) + dot(ev_s[...], wvt_s[:, cols])).astype(BF)

        @pl.when(even)
        def _():
            send_a[:, cols] = both[64:128]
            send_b[:, cols] = both[0:64]

        @pl.when(jnp.logical_not(even))
        def _():
            send_a[:, cols] = both[0:64]
            send_b[:, cols] = both[64:128]


def project_back(
    fc_in, tl_in, after, ds_s, k_s, dk, dv, wq_s, wkt_s, wvt_s, x_s, gains, l0, l1, l23,
    g_o, along_o, inv_o, rows_o, fc, tl, dq_s, sems,
):
    cf = pltpu.make_async_copy(fc_in, fc, sems.at[0])
    ct = pltpu.make_async_copy(tl_in, tl, sems.at[1])
    cf.start()
    ct.start()
    for g in range(4):
        dq = [None] * 3
        for j, (lo, hi) in enumerate(WINDOWS):
            add_tiles(dq, lo, dot(ds_s[g * 4 + j], k_s[32:288, window(g, lo, hi)] * head_mask(j, lo, hi)))
        for t in range(3):
            dq_s[:, window(g, t, t + 1)] = dq[t].astype(BF)
    dn = dot(dk[...], wkt_s[...]) + dot(dv[...], wvt_s[...]) + dot_t(dq_s[...], wq_s[...])
    squares = jnp.zeros((FR, LANE), F32)
    along = jnp.zeros((FR, LANE), F32)
    for c in range(NB):
        cols = slice(c * LANE, (c + 1) * LANE)
        x = x_s[:, cols].astype(F32)
        g = dn[:, cols] * gains[c : c + 1, :]
        g_o[:, cols] = g
        squares = squares + x * x
        along = along + g * x
    along_o[...] = along
    inv = lax.rsqrt(jnp.sum(squares, axis=-1, keepdims=True) * (1.0 / D) + EPSILON)
    inv_o[...] = jnp.broadcast_to(inv, (FR, LANE))

    tm = lax.axis_index("tm")
    llm = lax.axis_index("llm")
    cf.wait()
    ct.wait()
    starts, lives = routes(fc, tl, tm)
    slot = lax.broadcasted_iota(jnp.int32, (SLOTS, NREC * LR), 0) + llm * SLOTS
    col = lax.broadcasted_iota(jnp.int32, (SLOTS, NREC * LR), 1)
    chosen = jnp.zeros((SLOTS, NREC * LR), F32)
    for j, apart in enumerate((0, 1, 3, 2)):
        b = llm ^ apart
        r = col - j * LR
        hit = (r >= 0) & (r < LR) & (r < pick(lives, b)) & (slot == r + pick(starts, b))
        chosen = jnp.where(hit, 1.0, chosen)
    latents = jnp.concatenate([l0[...], l1[...], l23[...]], axis=0)
    rows_o[...] = dot(chosen.astype(BF), latents).astype(BF)


def finish(
    rows, x_s, dh_s, g_own, along_own, inv_s, recv_a, recv_b, gains, rows_out, grad_out, g_s, out_s, sems
):
    rows_copy = pltpu.make_async_copy(rows, rows_out, sems.at[2])
    rows_copy.start()
    tm = lax.axis_index("tm")
    odd = tm % 2
    one, none = jnp.float32(1.0), jnp.float32(0.0)
    copies = []
    for half in range(2):
        at = slice(half * 64, half * 64 + 64)
        keep_a = jnp.where(odd == 1 - half, one, none)
        inside = (tm > 0) & (tm < lax.axis_size("tm") - 1)
        keep_b = jnp.where((odd == half) & inside, one, none)
        along = along_own[at, :]
        for c in range(NB):
            cols = slice(c * LANE, (c + 1) * LANE)
            new = recv_a[:, cols].astype(F32) * keep_a + recv_b[:, cols].astype(F32) * keep_b
            new = new * gains[c : c + 1, :]
            g_s[at, cols] = g_own[at, cols] + new
            along = along + new * x_s[at, cols].astype(F32)
        inv = inv_s[at, :]
        back = inv * inv * inv * (jnp.sum(along, axis=-1, keepdims=True) * (1.0 / D))
        for c in range(NB):
            cols = slice(c * LANE, (c + 1) * LANE)
            x = x_s[at, cols].astype(F32)
            out_s[at, cols] = (dh_s[at, cols].astype(F32) + g_s[at, cols] * inv - x * back).astype(BF)
        copy = pltpu.make_async_copy(out_s.at[at], grad_out.at[at], sems.at[half])
        copy.start()
        copies.append(copy)
    for copy in copies + [rows_copy]:
        copy.wait()


def swap(count, cells_a, cells_b):
    pairs_a = [(i, i ^ 1) for i in range(count)]
    n = lax.axis_size("llm")
    full_b = []
    for i in range(count):
        partner = ((i + 1) ^ 1) - 1
        end = partner < 0 or partner >= count
        full_b += [(i * n + y, i * n + (y ^ 1) if end else partner * n + y) for y in range(n)]
    return lax.ppermute(cells_a, "tm", pairs_a), lax.ppermute(cells_b, ("tm", "llm"), full_b)


def trade(cells, apart):
    n = lax.axis_size("llm")
    return lax.ppermute(cells, "llm", [(i, i ^ apart) for i in range(n)])


def hbm(array):
    return pltpu.with_memory_space_constraint(array, pltpu.HBM)


def vmem(array):
    return pltpu.with_memory_space_constraint(array, pltpu.VMEM)


def call(kernel, ins, outs, scratch, flops, outs_in_hbm=False):
    place = {"h": hbm, "v": vmem, "n": lambda array: array}
    spec = {"h": ANY, "v": VMEM, "n": ANY}
    if outs_in_hbm:
        shapes = [jax.ShapeDtypeStruct(s, d) for s, d in outs]
    else:
        shapes = [pltpu.VMEM(s, d) for s, d in outs]
    return pl.pallas_call(
        kernel,
        out_shape=shapes,
        in_specs=[spec[kind] for kind, _ in ins],
        out_specs=[ANY if outs_in_hbm else VMEM] * len(outs),
        scratch_shapes=scratch,
        compiler_params=pltpu.CompilerParams(vmem_limit_bytes=12 * 1024 * 1024),
        cost_estimate=pl.CostEstimate(flops=flops, bytes_accessed=1_000_000, transcendentals=0),
        name=kernel.__name__,
    )(*[place[kind](array) for kind, array in ins])


def mark(kind, *arrays):
    return [(kind, array) for array in arrays]


def on_device(
    audio, frame_counts, text_lengths, norm_gain, w_query, w_key, w_value, w_out,
    conv_gain, conv_kernel, latent_gain, llm_grads,
):
    signal = audio[0]
    n_tm = lax.axis_size("tm")
    norm_row, conv_row, latent_row = (g.reshape(NB, LANE) for g in (norm_gain, conv_gain, latent_gain))
    tl_in = text_lengths.T
    V = pltpu.VMEM
    fc = pltpu.SMEM((NREC,), jnp.int32)
    tl = pltpu.SMEM((NREC, n_tm), jnp.int32)
    gain = ((NB, LANE), F32)
    weight = ((D, D), BF)

    def rows(n, dtype=BF):
        return ((n, D), dtype)

    def sems(*dims):
        return pltpu.SemaphoreType.DMA(dims)

    send_a, send_b, own, pair, mate = call(
        prepare,
        mark("h", frame_counts, tl_in, signal, llm_grads[0]),
        [rows(HALO + 16), rows(HALO + 16), rows(LR), rows(2 * LR), rows(LR)],
        [fc, tl, V((SLOTS, D), BF), sems(5)],
        100_000_000,
    )
    recv_a, recv_b = swap(n_tm, send_a, send_b)
    x, gains, normed, k_own, v_own, wk, wv, wkt, wvt = call(
        project_own,
        mark("v", own) + mark("h", signal, norm_row, w_key, w_value),
        [rows(FR), gain, rows(FR), rows(FR), rows(FR), weight, weight, weight, weight],
        [sems(4)],
        6_000_000_000,
    )
    (pairs,) = call(stack_pair, mark("v", gains, pair, recv_a, recv_b), [rows(2 * LR + 16)], [], 1_000_000)
    got_pair = trade(pairs, 1)
    xq, q, k, v, p, att, wq, wo = call(
        attend,
        mark("h", frame_counts, w_query, w_out)
        + mark("v", recv_a, recv_b, x, normed, gains, k_own, v_own, wk, wv),
        [rows(QR), rows(QR), rows(EXT), rows(EXT), ((16, FR, 256), BF), rows(QR), weight, weight],
        [fc, V((2 * HALO, D), BF), V((QR, 256), F32), sems(3)],
        8_000_000_000,
    )
    (mates,) = call(stack_mate, mark("v", xq, mate, got_pair, recv_a, recv_b), [rows(LR + 32)], [], 1_000_000)
    got_mate = trade(mates, 3)
    latent, h, dsilu, pool, inv, cgain, lgain, taps, wot = call(
        convolve,
        mark("h", frame_counts) + mark("v", xq, att, wo) + mark("h", conv_row, latent_row, conv_kernel),
        [
            rows(LR), ((NB, QR, LANE), F32), ((NB, SR, LANE), F32), ((NB, PR, LANE), F32), ((QR, LANE), F32),
            gain, gain, rows(KERN, F32), weight,
        ],
        [fc, V((QR, LANE), F32), V((SR, LANE), F32), V((PR, LANE), F32), sems(4)],
        5_000_000_000,
    )
    latent_1 = trade(latent, 1)
    dhid, datt = call(
        convolve_back,
        mark("h", frame_counts)
        + mark("v", own, got_pair, got_mate, recv_a, recv_b, h, dsilu, pool, inv, cgain, lgain, taps, wot),
        [rows(FR), rows(FR)],
        [
            fc, V((PR, D), F32), V((SR, LANE), F32), V((SR, LANE), F32), V((NB, FR, LANE), F32),
            V((NB, FR, LANE), F32), sems(1),
        ],
        5_000_000_000,
    )
    (latents,) = call(stack_latents, mark("v", dhid, latent, latent_1), [rows(2 * LR)], [], 1_000_000)
    latent_23 = trade(latents, 3)
    back_a, back_b, ds, dk, dv = call(
        attend_back,
        mark("v", latents, q, v, p, datt, wkt, wvt),
        [rows(64), rows(64), ((16, FR, 256), BF), rows(FR), rows(FR)],
        [V((FR, D), BF), V((FR, D), BF)],
        6_000_000_000,
    )
    ret_a, ret_b = swap(n_tm, back_a, back_b)
    g_own, along, inv_x, placed = call(
        project_back,
        mark("h", frame_counts, tl_in)
        + mark("v", back_a, ds, k, dk, dv, wq, wkt, wvt, x, gains, latent, latent_1, latent_23),
        [rows(FR, F32), ((FR, LANE), F32), ((FR, LANE), F32), rows(SLOTS)],
        [fc, tl, V((FR, D), BF), sems(2)],
        3_000_000_000,
    )
    out_rows, grad = call(
        finish,
        mark("v", placed, x, dhid, g_own, along, inv_x, ret_a, ret_b, gains),
        [rows(SLOTS), rows(FR)],
        [V((FR, D), F32), V((FR, D), BF), sems(3)],
        1_000_000_000,
        outs_in_hbm=True,
    )
    return (out_rows[None], grad[None])


def solution(mesh):
    placed = (P("llm", "tm", None),) + (P(),) * 10 + (P("tm", "llm", None),)
    return jax.shard_map(
        on_device,
        mesh=mesh,
        in_specs=placed,
        out_specs=(P("tm", "llm", None), P("llm", "tm", None)),
        check_vma=False,
    )
```

```python
import jax
import jax.numpy as jnp
from jax import lax
from jax.experimental import pallas as pl
from jax.experimental.pallas import tpu as pltpu
from jax.sharding import PartitionSpec as P

D = 1536
REACH = 64
KERN = 32
FR = 128
HALO = 96
EXT = FR + 2 * HALO
QR = FR + 64
SR = FR + 32
PR = SR // 4
LR = FR // 4
SLOTS = 64
NREC = 4
HEAD = 96
HEADS = 16
LANE = 128
NB = D // LANE
COL = 1536
NC = D // COL
GROUP = 4 * HEAD
EPSILON = 1e-06
SCALE = HEAD ** (-0.5)
BF = jnp.bfloat16
F32 = jnp.float32
WINDOWS = ((0, 1), (0, 2), (1, 3), (2, 3))

VMEM = pl.BlockSpec(memory_space=pltpu.VMEM)
ANY = pl.BlockSpec(memory_space=pl.ANY)


def dot(a, b):
    return lax.dot_general(a, b, (((1,), (0,)), ((), ())), preferred_element_type=F32)


def dot_t(a, b):
    return lax.dot_general(a, b, (((1,), (1,)), ((), ())), preferred_element_type=F32)


def t_dot(a, b):
    return lax.dot_general(a, b, (((0,), (0,)), ((), ())), preferred_element_type=F32)


def lanes(c, width=LANE):
    return pl.ds(pl.multiple_of(c * width, width), width)


def routes(fc, tl, slice_index):
    starts, lives = [], []
    total = 0
    for b in range(NREC):
        live = jnp.clip(fc[b] // 4 - slice_index * LR, 0, LR)
        total = total + tl[b, slice_index]
        starts.append(total)
        lives.append(live)
        total = total + live
    return starts, lives


def pick(values, index):
    out = values[0]
    for b in range(1, NREC):
        out = jnp.where(index == b, values[b], out)
    return out


def prepare(fc_in, tl_in, audio, grads, send_b, send_a, own, pair, mate, placing, fc, tl, g_buf, sems):
    cf = pltpu.make_async_copy(fc_in, fc, sems.at[0])
    ct = pltpu.make_async_copy(tl_in, tl, sems.at[1])
    cf.start()
    ct.start()
    tm = lax.axis_index("tm")
    llm = lax.axis_index("llm")
    off_a = (1 - tm % 2) * (FR - HALO)
    off_b = (FR - HALO) - off_a
    cg = pltpu.make_async_copy(grads, g_buf, sems.at[2])
    ca = pltpu.make_async_copy(
        audio.at[pl.ds(pl.multiple_of(off_a, 32), HALO)], send_a.at[pl.ds(0, HALO)], sems.at[3]
    )
    cb = pltpu.make_async_copy(
        audio.at[pl.ds(pl.multiple_of(off_b, 32), HALO)], send_b.at[pl.ds(0, HALO)], sems.at[4]
    )
    cg.start()
    ca.start()
    cb.start()
    cf.wait()
    ct.wait()
    starts, lives = routes(fc, tl, tm)
    row = lax.broadcasted_iota(jnp.int32, (LR, SLOTS), 0)
    slot = lax.broadcasted_iota(jnp.int32, (LR, SLOTS), 1) + llm * SLOTS
    starts = [pick(starts, llm ^ j) for j in range(NREC)]
    lives = [pick(lives, llm ^ j) for j in range(NREC)]
    picked = []
    for j in range(NREC):
        chosen = (row < lives[j]) & (slot == row + starts[j])
        picked.append(jnp.where(chosen, 1.0, 0.0).astype(BF))
    place = lax.broadcasted_iota(jnp.int32, (16, SLOTS), 0)
    slot = lax.broadcasted_iota(jnp.int32, (16, SLOTS), 1) + llm * SLOTS
    for offset in ((1 - tm % 2) * (LR - 4), (tm % 2) * (LR - 4)):
        r = place % 4 + offset
        chosen = jnp.zeros((16, SLOTS), F32)
        for j in range(NREC):
            hit = (place // 4 == (j + 3) % 4) & (r < lives[j]) & (slot == r + starts[j])
            chosen = jnp.where(hit, 1.0, chosen)
        picked.append(chosen.astype(BF))
    slot = lax.broadcasted_iota(jnp.int32, (SLOTS, NREC * LR), 0) + llm * SLOTS
    col = lax.broadcasted_iota(jnp.int32, (SLOTS, NREC * LR), 1)
    chosen = jnp.zeros((SLOTS, NREC * LR), F32)
    for j, apart in enumerate((0, 1, 3, 2)):
        r = col - j * LR
        hit = (r >= 0) & (r < LR) & (r < lives[apart]) & (slot == r + starts[apart])
        chosen = jnp.where(hit, 1.0, chosen)
    placing[...] = chosen.astype(BF)
    cg.wait()
    moved = dot(jnp.concatenate(picked, axis=0), g_buf[...]).astype(BF)
    own[...] = moved[:LR]
    pair[...] = moved[LR : 3 * LR]
    mate[...] = moved[3 * LR : 4 * LR]
    send_a[HALO:, :] = moved[4 * LR : 4 * LR + 16]
    send_b[HALO:, :] = moved[4 * LR + 16 :]
    ca.wait()
    cb.wait()


def norm_rows(x, gains, out, rows):
    inv = lax.rsqrt(jnp.mean(x * x, axis=-1, keepdims=True) + EPSILON)
    for c in range(NB):
        cols = slice(c * LANE, (c + 1) * LANE)
        out[rows, cols] = (x[:, cols] * inv * gains[c : c + 1, :]).astype(BF)


def project_own(
    after, audio, gains_in, w_key, w_value, x_o, gain_o, n_s, k_o, v_o, wk_o, wv_o, wkt_o, wvt_o, sems
):
    cx = pltpu.make_async_copy(audio, x_o, sems.at[0])
    cg = pltpu.make_async_copy(gains_in, gain_o, sems.at[1])
    loads = [
        pltpu.make_async_copy(w_key, wk_o, sems.at[2]),
        pltpu.make_async_copy(w_value, wv_o, sems.at[3]),
    ]
    for copy in [cx, cg] + loads:
        copy.start()
    cx.wait()
    cg.wait()
    for r in range(2):
        rows = slice(r * 64, r * 64 + 64)
        norm_rows(x_o[rows, :].astype(F32), gain_o, n_s, rows)
    for load, w_s, wt_s, out_s in zip(loads, (wk_o, wv_o), (wkt_o, wvt_o), (k_o, v_o)):
        load.wait()
        out_s[...] = dot(n_s[...], w_s[...]).astype(BF)
        wt_s[...] = w_s[...].T


def halves(first, second, lo):
    pair = [part.astype(F32)[lo : lo + 8] for part in (first, second)]
    return jnp.concatenate(pair, axis=0).astype(BF)


def stack_pair(after, pair, recv_b, recv_a, out):
    out[: 2 * LR, :] = pair[...]
    out[2 * LR :, :] = halves(recv_a[HALO:, :], recv_b[HALO:, :], 0)


def stack_mate(after, mate, got_pair, recv_a, recv_b, out):
    out[:LR, :] = mate[...] + got_pair[LR : 2 * LR, :]
    out[LR : LR + 16, :] = halves(recv_a[HALO:, :], recv_b[HALO:, :], 8)
    out[LR + 16 :, :] = got_pair[2 * LR :, :]


def stack_latents(after, first, second, out):
    out[:LR, :] = first[...]
    out[LR:, :] = second[...]


def head_mask(j, lo, hi):
    lane = lax.broadcasted_iota(jnp.int32, (1, (hi - lo) * LANE), 1) + lo * LANE
    return jnp.where((lane >= j * HEAD) & (lane < (j + 1) * HEAD), 1.0, 0.0).astype(BF)


def window(g, lo, hi):
    start = g * GROUP + lo * LANE
    return pl.ds(start if isinstance(start, int) else pl.multiple_of(start, LANE), (hi - lo) * LANE)


def add_tiles(tiles, lo, value):
    for t in range(value.shape[1] // LANE):
        part = value[:, t * LANE : (t + 1) * LANE]
        tiles[lo + t] = part if tiles[lo + t] is None else tiles[lo + t] + part


def attend(
    fc_in, w_query, w_out, recv_a, recv_b, x_own, n_own, gains, k_own, v_own, wk_s, wv_s,
    h_s, inv_o, q_s, k_s, v_s, p_s, wq_s, wo_s, fc, n_s, xq_o, att_s, bias_s, sems,
):
    fc_copy = pltpu.make_async_copy(fc_in, fc, sems.at[0])
    fc_copy.start()
    load_q = pltpu.make_async_copy(w_query, wq_s, sems.at[1])
    load_q.start()
    load_o = pltpu.make_async_copy(w_out, wo_s, sems.at[2])
    tm = lax.axis_index("tm")
    llm = lax.axis_index("llm")
    even = tm % 2 == 0
    first = tm * FR
    total = lax.axis_size("tm") * FR

    @pl.when(even)
    def _():
        norm_rows(recv_b[:HALO, :].astype(F32), gains, n_s, slice(0, HALO))
        norm_rows(recv_a[:HALO, :].astype(F32), gains, n_s, slice(HALO, 2 * HALO))
        xq_o[0:32, :] = recv_b[64:96, :]
        xq_o[160:192, :] = recv_a[0:32, :]

    @pl.when(jnp.logical_not(even))
    def _():
        norm_rows(recv_a[:HALO, :].astype(F32), gains, n_s, slice(0, HALO))
        norm_rows(recv_b[:HALO, :].astype(F32), gains, n_s, slice(HALO, 2 * HALO))
        xq_o[0:32, :] = recv_a[64:96, :]
        xq_o[160:192, :] = recv_b[0:32, :]

    xq_o[32:160, :] = x_own[...]
    k_s[96:224, :] = k_own[...]
    v_s[96:224, :] = v_own[...]
    for w_s, out_s in ((wk_s, k_s), (wv_s, v_s)):
        @pl.loop(0, NC)
        def _(j, w_s=w_s, out_s=out_s):
            cols = lanes(j, COL)
            new = dot(n_s[...], w_s[:, cols]).astype(BF)
            out_s[0:96, cols] = new[0:96]
            out_s[224:320, cols] = new[96:192]

    queried = jnp.concatenate([n_s[64:96, :], n_own[...], n_s[96:128, :]], axis=0)
    load_q.wait()
    load_o.start()
    q_s[...] = dot(queried, wq_s[...]).astype(BF)

    fc_copy.wait()
    limit = fc[llm]

    def bias_of(rows, q_first, k_first):
        qe = lax.broadcasted_iota(jnp.int32, (rows, 256), 0) + q_first
        ke = lax.broadcasted_iota(jnp.int32, (rows, 256), 1) + k_first
        kt = ke + (first - HALO)
        ok = (ke >= qe - REACH) & (ke < qe + REACH) & (kt >= 0) & (kt < total) & ((kt < limit) | (ke == qe))
        return jnp.where(ok, 0.0, -1e30)

    bias_s[0:32, :] = bias_of(32, 64, 0)
    bias_s[32:160, :] = bias_of(FR, HALO, 32)
    bias_s[160:192, :] = bias_of(32, 224, 64)

    for base in range(0, HEADS, 16):
        some = [(h, h // 4, WINDOWS[h % 4]) for h in range(base, base + 16)]
        heads = []
        for h, g, (lo, hi) in some:
            q = q_s[:, window(g, lo, hi)] * head_mask(h % 4, lo, hi)
            k = k_s[:, window(g, lo, hi)]
            heads.append(
                jnp.concatenate(
                    [dot_t(q[0:32], k[0:256]), dot_t(q[32:160], k[32:288]), dot_t(q[160:192], k[64:320])], axis=0
                )
            )
        heads = [scores * SCALE + bias_s[...] for scores in heads]
        highest = [jnp.max(scores, axis=-1, keepdims=True) for scores in heads]
        heads = [jnp.exp(scores - top) for scores, top in zip(heads, highest)]
        inverse = [1.0 / jnp.sum(powers, axis=-1, keepdims=True) for powers in heads]
        heads = [(powers * inv).astype(BF) for powers, inv in zip(heads, inverse)]
        for g in range(base // 4, (base + 16) // 4):
            parts = [[None] * 3 for _ in range(3)]
            for (h, of, (lo, hi)), p in zip(some, heads):
                if of != g:
                    continue
                v = v_s[:, window(g, lo, hi)] * head_mask(h % 4, lo, hi)
                p_s[h] = p[32:160]
                add_tiles(parts[0], lo, dot(p[0:32], v[0:256]))
                add_tiles(parts[1], lo, dot(p[32:160], v[32:288]))
                add_tiles(parts[2], lo, dot(p[160:192], v[64:320]))
            for t in range(3):
                at = window(g, t, t + 1)
                att_s[0:32, at] = parts[0][t].astype(BF)
                att_s[32:160, at] = parts[1][t].astype(BF)
                att_s[160:192, at] = parts[2][t].astype(BF)

    load_o.wait()

    def hidden_step(j, squares):
        cols = lanes(j, COL)
        h = dot(att_s[...], wo_s[:, cols]) + xq_o[:, cols].astype(F32)
        h = h.astype(BF).astype(F32)
        for t in range(COL // LANE):
            part = h[:, t * LANE : (t + 1) * LANE]
            h_s[j * (COL // LANE) + t] = part
            squares = squares + part * part
        return squares

    squares = lax.fori_loop(0, NC, hidden_step, jnp.zeros((QR, LANE), F32))
    inv_h = lax.rsqrt(jnp.sum(squares, axis=-1, keepdims=True) * (1.0 / D) + EPSILON)
    inv_o[...] = jnp.broadcast_to(inv_h, (QR, LANE))


def spoken_rows(fc, tm, llm):
    frame = lax.broadcasted_iota(jnp.int32, (QR, 1), 0) + (tm * FR - 32)
    return jnp.where((frame >= 0) & (frame < fc[llm]), 1.0, 0.0)


def convolve(
    fc_in, h_s, inv_s, wo_s, cg_in, lg_in, taps_in,
    lat_o, dsilu_s, pool_s, cg_s, lg_s, tap_s, wot_s, fc, ci_s, up_s, norm_t, sems,
):
    copies = [
        pltpu.make_async_copy(source, into, sems.at[i])
        for i, (source, into) in enumerate(((fc_in, fc), (cg_in, cg_s), (lg_in, lg_s), (taps_in, tap_s)))
    ]
    for copy in copies:
        copy.start()
    tm = lax.axis_index("tm")
    llm = lax.axis_index("llm")

    for copy in copies:
        copy.wait()
    inv_spoken = inv_s[...] * spoken_rows(fc, tm, llm)

    def conv_step(c, squares):
        cols = lanes(c)
        wot_s[cols, :] = wo_s[:, cols].T
        ci_s[...] = (h_s[c] * inv_spoken * cg_s[pl.ds(c, 1), :]).astype(BF).astype(F32)
        kern = tap_s[:, cols]
        part = SR // 4
        for at in range(0, SR, part):
            acc = jnp.zeros((part, LANE), F32)
            for s in range(8):
                xs = ci_s[at + s : at + s + part + 24, :]
                for u in range(4):
                    m = s + 8 * u
                    acc = acc + kern[m : m + 1, :] * xs[8 * u : 8 * u + part]
            sig = 0.5 * jnp.tanh(0.5 * acc) + 0.5
            silu = acc * sig
            dsilu_s[c, at : at + part, :] = sig + silu * (1.0 - sig)
            up_s[at : at + part, :] = h_s[c, 16 + at : 16 + at + part, :] + silu
        pooled = up_s[pl.ds(0, PR, 4), :]
        for u in range(1, 4):
            pooled = pooled + up_s[pl.ds(u, PR, 4), :]
        pooled = pooled * 0.25
        pool_s[c] = pooled
        return squares + pooled * pooled

    squares = lax.fori_loop(0, NB, conv_step, jnp.zeros((PR, LANE), F32))
    inv_p = lax.rsqrt(jnp.sum(squares, axis=-1, keepdims=True) * (1.0 / D) + EPSILON)
    for c in range(NB):
        norm_t[...] = pool_s[c] * inv_p * lg_s[c : c + 1, :]
        lat_o[:, c * LANE : (c + 1) * LANE] = norm_t[4:36, :].astype(BF)


def convolve_back(
    fc_in, own, got_pair, got_mate, recv_a, recv_b, h_s, dsilu_s, pool_s, inv_s, cg_s, lg_s, tap_s, wot_s,
    dhid_s, datt_s, fc, g_s, up_s, ds_s, us_s, dnc_s, sems,
):
    copy = pltpu.make_async_copy(fc_in, fc, sems.at[0])
    copy.start()
    tm = lax.axis_index("tm")
    llm = lax.axis_index("llm")
    even = tm % 2 == 0

    row = lax.broadcasted_iota(jnp.int32, (PR, LR + 80), 0)
    col = lax.broadcasted_iota(jnp.int32, (PR, LR + 80), 1)
    is_left = row < 4
    is_right = row >= PR - 4
    r = jnp.where(is_left, row, row - (PR - 4))
    label = jnp.where(is_left, 1 - tm % 2, tm % 2)
    side = (
        (col == 44 + 16 * label + r) | (col == 64 + 8 * label + r)
        | (col == 80 + 8 * label + r) | (col == 100 + 8 * label + r)
    ) & (is_left | is_right)
    middle = (col < LR) & (col == row - 4)
    at = tm * LR + row - 4
    chosen = (side | middle) & (at >= 0) & (at < lax.axis_size("tm") * LR)
    chosen = jnp.where(chosen, 1.0, 0.0).astype(BF)
    stacked = jnp.concatenate(
        [
            own[...] + got_pair[:LR, :] + got_mate[:LR, :],
            recv_a[HALO:, :],
            recv_b[HALO:, :],
            got_pair[2 * LR :, :],
            got_mate[LR:, :],
        ],
        axis=0,
    )
    g_s[...] = dot(chosen, stacked)

    def sums(c, carry):
        squares, along = carry
        pooled = pool_s[c]
        return squares + pooled * pooled, along + g_s[:, lanes(c)] * lg_s[pl.ds(c, 1), :] * pooled

    zero = jnp.zeros((PR, LANE), F32)
    squares, along = lax.fori_loop(0, NB, sums, (zero, zero))
    inv_p = lax.rsqrt(jnp.sum(squares, axis=-1, keepdims=True) * (1.0 / D) + EPSILON)
    back_p = inv_p * inv_p * inv_p * (jnp.sum(along, axis=-1, keepdims=True) * (1.0 / D))
    inv_own = inv_s[32:160, :]
    copy.wait()
    spoken_own = spoken_rows(fc, tm, llm)[32:160]

    def conv_back(c, along):
        cols = lanes(c)
        gain = lg_s[pl.ds(c, 1), :]
        dpool = (g_s[:, cols] * gain * inv_p - pool_s[c] * back_p) * 0.25
        for u in range(4):
            up_s[pl.ds(u, PR, 4), :] = dpool
        ds_s[...] = up_s[...] * dsilu_s[c]
        us_s[c] = up_s[16 : 16 + FR, :]
        kern = tap_s[:, cols]
        part = FR // 4
        sums = []
        for at in range(0, FR, part):
            acc = jnp.zeros((part, LANE), F32)
            for s in range(8):
                base = 8 if s == 0 else s
                xs = ds_s[at + base : at + base + part + 24, :]
                for u in range(4):
                    m = 32 - base - 8 * u
                    acc = acc + kern[m : m + 1, :] * xs[8 * u : 8 * u + part]
            dn = acc.astype(BF).astype(F32) * spoken_own[at : at + part] * cg_s[pl.ds(c, 1), :]
            dnc_s[c, at : at + part, :] = dn
            sums.append(along[at : at + part] + dn * h_s[c, 32 + at : 32 + at + part, :])
        return jnp.concatenate(sums, axis=0)

    along = lax.fori_loop(0, NB, conv_back, jnp.zeros((FR, LANE), F32), unroll=2)
    back_h = inv_own * inv_own * inv_own * (jnp.sum(along, axis=-1, keepdims=True) * (1.0 / D))

    @pl.loop(0, NB)
    def _(c):
        dhid_s[:, lanes(c)] = (us_s[c] + dnc_s[c] * inv_own - h_s[c, 32:160, :] * back_h).astype(BF)

    @pl.loop(0, NC)
    def _(j):
        datt_s[:, lanes(j, COL)] = dot(dhid_s[...], wot_s[:, lanes(j, COL)]).astype(BF)


def attend_back(after, q_s, v_s, p_s, datt_s, wkt_s, wvt_s, send_a, send_b, ds_o, dk_s, dv_s, ek_s, ev_s):
    for base in range(0, HEADS, 16):
        some = [(h, h // 4, WINDOWS[h % 4]) for h in range(base, base + 16)]
        heads = []
        for h, g, (lo, hi) in some:
            win = window(g, lo, hi)
            heads.append(dot_t(datt_s[:, win] * head_mask(h % 4, lo, hi), v_s[32:288, win]))
        weights = [p_s[h].astype(F32) for h, _, _ in some]
        heads = [w * dp for w, dp in zip(weights, heads)]
        sums = [jnp.sum(pd, axis=-1, keepdims=True) for pd in heads]
        heads = [((pd - w * total) * SCALE).astype(BF) for pd, w, total in zip(heads, weights, sums)]
        for g in range(base // 4, (base + 16) // 4):
            dk, dv = [None] * 3, [None] * 3
            for (h, of, (lo, hi)), ds in zip(some, heads):
                if of != g:
                    continue
                win = window(g, lo, hi)
                mask = head_mask(h % 4, lo, hi)
                ds_o[h] = ds
                add_tiles(dk, lo, t_dot(ds, q_s[32:160, win] * mask))
                add_tiles(dv, lo, t_dot(p_s[h], datt_s[:, win] * mask))
            for t in range(3):
                at = window(g, t, t + 1)
                for out, edge, tiles in ((dk_s, ek_s, dk), (dv_s, ev_s, dv)):
                    new = tiles[t].astype(BF)
                    edge[0:64, at] = new[0:64]
                    out[:, at] = new[64:192]
                    edge[64:128, at] = new[192:256]

    even = lax.axis_index("tm") % 2 == 0

    @pl.loop(0, NC)
    def _(j):
        cols = lanes(j, COL)
        both = (dot(ek_s[...], wkt_s[:, cols]) + dot(ev_s[...], wvt_s[:, cols])).astype(BF)

        @pl.when(even)
        def _():
            send_a[:, cols] = both[64:128]
            send_b[:, cols] = both[0:64]

        @pl.when(jnp.logical_not(even))
        def _():
            send_a[:, cols] = both[0:64]
            send_b[:, cols] = both[64:128]


def project_back(
    after, ds_s, k_s, dk, dv, wq_s, wkt_s, wvt_s, x_s, gains, g_o, along_o, inv_o, dq_s,
):
    for g in range(4):
        dq = [None] * 3
        for j, (lo, hi) in enumerate(WINDOWS):
            add_tiles(dq, lo, dot(ds_s[g * 4 + j], k_s[32:288, window(g, lo, hi)] * head_mask(j, lo, hi)))
        for t in range(3):
            dq_s[:, window(g, t, t + 1)] = dq[t].astype(BF)
    dn = dot(dk[...], wkt_s[...]) + dot(dv[...], wvt_s[...]) + dot_t(dq_s[...], wq_s[...])
    squares = jnp.zeros((FR, LANE), F32)
    along = jnp.zeros((FR, LANE), F32)
    for c in range(NB):
        cols = slice(c * LANE, (c + 1) * LANE)
        x = x_s[:, cols].astype(F32)
        g = dn[:, cols] * gains[c : c + 1, :]
        g_o[:, cols] = g
        squares = squares + x * x
        along = along + g * x
    along_o[...] = along
    inv = lax.rsqrt(jnp.sum(squares, axis=-1, keepdims=True) * (1.0 / D) + EPSILON)
    inv_o[...] = jnp.broadcast_to(inv, (FR, LANE))


def place_rows(after, chosen, l0, l1, l23, rows_o):
    latents = jnp.concatenate([l0[...], l1[...], l23[...]], axis=0)
    rows_o[...] = dot(chosen[...], latents).astype(BF)


def finish(
    rows, x_s, dh_s, g_own, along_own, inv_s, recv_a, recv_b, gains, rows_out, grad_out, g_s, out_s, sems
):
    rows_copy = pltpu.make_async_copy(rows, rows_out, sems.at[2])
    rows_copy.start()
    tm = lax.axis_index("tm")
    odd = tm % 2
    one, none = jnp.float32(1.0), jnp.float32(0.0)
    copies = []
    for half in range(2):
        at = slice(half * 64, half * 64 + 64)
        keep_a = jnp.where(odd == 1 - half, one, none)
        inside = (tm > 0) & (tm < lax.axis_size("tm") - 1)
        keep_b = jnp.where((odd == half) & inside, one, none)
        along = along_own[at, :]
        for c in range(NB):
            cols = slice(c * LANE, (c + 1) * LANE)
            new = recv_a[:, cols].astype(F32) * keep_a + recv_b[:, cols].astype(F32) * keep_b
            new = new * gains[c : c + 1, :]
            g_s[at, cols] = g_own[at, cols] + new
            along = along + new * x_s[at, cols].astype(F32)
        inv = inv_s[at, :]
        back = inv * inv * inv * (jnp.sum(along, axis=-1, keepdims=True) * (1.0 / D))
        for c in range(NB):
            cols = slice(c * LANE, (c + 1) * LANE)
            x = x_s[at, cols].astype(F32)
            out_s[at, cols] = (dh_s[at, cols].astype(F32) + g_s[at, cols] * inv - x * back).astype(BF)
        copy = pltpu.make_async_copy(out_s.at[at], grad_out.at[at], sems.at[half])
        copy.start()
        copies.append(copy)
    for copy in copies + [rows_copy]:
        copy.wait()


def swap(count, cells_a, cells_b):
    pairs_a = [(i, i ^ 1) for i in range(count)]
    n = lax.axis_size("llm")
    full_b = []
    for i in range(count):
        partner = ((i + 1) ^ 1) - 1
        end = partner < 0 or partner >= count
        full_b += [(i * n + y, i * n + (y ^ 1) if end else partner * n + y) for y in range(n)]
    got_b = lax.ppermute(cells_b, ("tm", "llm"), full_b)
    return lax.ppermute(cells_a, "tm", pairs_a), got_b


def trade(cells, apart):
    n = lax.axis_size("llm")
    return lax.ppermute(cells, "llm", [(i, i ^ apart) for i in range(n)])


def hbm(array):
    return pltpu.with_memory_space_constraint(array, pltpu.HBM)


def vmem(array):
    return pltpu.with_memory_space_constraint(array, pltpu.VMEM)


def call(kernel, ins, outs, scratch, flops, outs_in_hbm=False):
    place = {"h": hbm, "v": vmem, "n": lambda array: array}
    spec = {"h": ANY, "v": VMEM, "n": ANY}
    if outs_in_hbm:
        shapes = [jax.ShapeDtypeStruct(s, d) for s, d in outs]
    else:
        shapes = [pltpu.VMEM(s, d) for s, d in outs]
    return pl.pallas_call(
        kernel,
        out_shape=shapes,
        in_specs=[spec[kind] for kind, _ in ins],
        out_specs=[ANY if outs_in_hbm else VMEM] * len(outs),
        scratch_shapes=scratch,
        compiler_params=pltpu.CompilerParams(vmem_limit_bytes=14 * 1024 * 1024),
        cost_estimate=pl.CostEstimate(flops=flops, bytes_accessed=1_000_000, transcendentals=0),
        name=kernel.__name__,
    )(*[place[kind](array) for kind, array in ins])


def mark(kind, *arrays):
    return [(kind, array) for array in arrays]


def on_device(
    audio, frame_counts, text_lengths, norm_gain, w_query, w_key, w_value, w_out,
    conv_gain, conv_kernel, latent_gain, llm_grads,
):
    signal = audio[0]
    n_tm = lax.axis_size("tm")
    norm_row, conv_row, latent_row = (g.reshape(NB, LANE) for g in (norm_gain, conv_gain, latent_gain))
    tl_in = text_lengths.T
    V = pltpu.VMEM
    fc = pltpu.SMEM((NREC,), jnp.int32)
    tl = pltpu.SMEM((NREC, n_tm), jnp.int32)
    gain = ((NB, LANE), F32)
    weight = ((D, D), BF)

    def rows(n, dtype=BF):
        return ((n, D), dtype)

    def sems(*dims):
        return pltpu.SemaphoreType.DMA(dims)

    send_b, send_a, own, pair, mate, placing = call(
        prepare,
        mark("h", frame_counts, tl_in, signal, llm_grads[0]),
        [rows(HALO + 16), rows(HALO + 16), rows(LR), rows(2 * LR), rows(LR), ((SLOTS, NREC * LR), BF)],
        [fc, tl, V((SLOTS, D), BF), sems(5)],
        100_000_000,
    )
    recv_a, recv_b = swap(n_tm, send_a, send_b)
    x, gains, normed, k_own, v_own, wk, wv, wkt, wvt = call(
        project_own,
        mark("v", own) + mark("h", signal, norm_row, w_key, w_value),
        [rows(FR), gain, rows(FR), rows(FR), rows(FR), weight, weight, weight, weight],
        [sems(4)],
        6_000_000_000,
    )
    (pairs,) = call(stack_pair, mark("v", gains, pair, recv_b, recv_a), [rows(2 * LR + 16)], [], 1_000_000)
    got_pair = trade(pairs, 1)
    h, inv, q, k, v, p, wq, wo = call(
        attend,
        mark("h", frame_counts, w_query, w_out)
        + mark("v", recv_a, recv_b, x, normed, gains, k_own, v_own, wk, wv),
        [
            ((NB, QR, LANE), F32), ((QR, LANE), F32), rows(QR), rows(EXT), rows(EXT), ((16, FR, 256), BF),
            weight, weight,
        ],
        [fc, V((2 * HALO, D), BF), V((QR, D), BF), V((QR, D), BF), V((QR, 256), F32), sems(3)],
        8_000_000_000,
    )
    (mates,) = call(stack_mate, mark("v", inv, mate, got_pair, recv_a, recv_b), [rows(LR + 32)], [], 1_000_000)
    got_mate = trade(mates, 3)
    latent, dsilu, pool, cgain, lgain, taps, wot = call(
        convolve,
        mark("h", frame_counts) + mark("v", h, inv, wo) + mark("h", conv_row, latent_row, conv_kernel),
        [
            rows(LR), ((NB, SR, LANE), F32), ((NB, PR, LANE), F32),
            gain, gain, rows(KERN, F32), weight,
        ],
        [fc, V((QR, LANE), F32), V((SR, LANE), F32), V((PR, LANE), F32), sems(4)],
        5_000_000_000,
    )
    latent_1 = trade(latent, 1)
    dhid, datt = call(
        convolve_back,
        mark("h", frame_counts)
        + mark("v", own, got_pair, got_mate, recv_a, recv_b, h, dsilu, pool, inv, cgain, lgain, taps, wot),
        [rows(FR), rows(FR)],
        [
            fc, V((PR, D), F32), V((SR, LANE), F32), V((SR, LANE), F32), V((NB, FR, LANE), F32),
            V((NB, FR, LANE), F32), sems(1),
        ],
        5_000_000_000,
    )
    (latents,) = call(stack_latents, mark("v", dhid, latent, latent_1), [rows(2 * LR)], [], 1_000_000)
    latent_23 = trade(latents, 3)
    back_a, back_b, ds, dk, dv = call(
        attend_back,
        mark("v", latents, q, v, p, datt, wkt, wvt),
        [rows(64), rows(64), ((16, FR, 256), BF), rows(FR), rows(FR)],
        [V((FR, D), BF), V((FR, D), BF)],
        6_000_000_000,
    )
    ret_a, ret_b = swap(n_tm, back_a, back_b)
    g_own, along, inv_x = call(
        project_back,
        mark("v", back_a, ds, k, dk, dv, wq, wkt, wvt, x, gains),
        [rows(FR, F32), ((FR, LANE), F32), ((FR, LANE), F32)],
        [V((FR, D), BF)],
        3_000_000_000,
    )
    (placed,) = call(
        place_rows,
        mark("v", along, placing, latent, latent_1, latent_23),
        [rows(SLOTS)],
        [],
        50_000_000,
    )
    out_rows, grad = call(
        finish,
        mark("v", placed, x, dhid, g_own, along, inv_x, ret_a, ret_b, gains),
        [rows(SLOTS), rows(FR)],
        [V((FR, D), F32), V((FR, D), BF), sems(3)],
        1_000_000_000,
        outs_in_hbm=True,
    )
    return (out_rows[None], grad[None])


def solution(mesh):
    placed = (P("llm", "tm", None),) + (P(),) * 10 + (P("tm", "llm", None),)
    return jax.shard_map(
        on_device,
        mesh=mesh,
        in_specs=placed,
        out_specs=(P("tm", "llm", None), P("llm", "tm", None)),
        check_vma=False,
    )
```

```python
import jax
import jax.numpy as jnp
from jax import lax
from jax.experimental import pallas as pl
from jax.experimental.pallas import tpu as pltpu
from jax.sharding import PartitionSpec as P

D = 1536
REACH = 64
KERN = 32
FR = 128
HALO = 96
EXT = FR + 2 * HALO
QR = FR + 64
SR = FR + 32
PR = SR // 4
LR = FR // 4
SLOTS = 64
NREC = 4
HEAD = 96
HEADS = 16
LANE = 128
NB = D // LANE
COL = 1536
NC = D // COL
GROUP = 4 * HEAD
EPSILON = 1e-06
SCALE = HEAD ** (-0.5)
BF = jnp.bfloat16
F32 = jnp.float32
WINDOWS = ((0, 1), (0, 2), (1, 3), (2, 3))

VMEM = pl.BlockSpec(memory_space=pltpu.VMEM)
ANY = pl.BlockSpec(memory_space=pl.ANY)


def dot(a, b):
    return lax.dot_general(a, b, (((1,), (0,)), ((), ())), preferred_element_type=F32)


def dot_t(a, b):
    return lax.dot_general(a, b, (((1,), (1,)), ((), ())), preferred_element_type=F32)


def t_dot(a, b):
    return lax.dot_general(a, b, (((0,), (0,)), ((), ())), preferred_element_type=F32)


def lanes(c, width=LANE):
    return pl.ds(pl.multiple_of(c * width, width), width)


def routes(fc, tl, slice_index):
    starts, lives = [], []
    total = 0
    for b in range(NREC):
        live = jnp.clip(fc[b] // 4 - slice_index * LR, 0, LR)
        total = total + tl[b, slice_index]
        starts.append(total)
        lives.append(live)
        total = total + live
    return starts, lives


def pick(values, index):
    out = values[0]
    for b in range(1, NREC):
        out = jnp.where(index == b, values[b], out)
    return out


def prepare(fc_in, tl_in, audio, grads, send_a, send_b, own, pair, mate, placing, fc, tl, g_buf, sems):
    cf = pltpu.make_async_copy(fc_in, fc, sems.at[0])
    ct = pltpu.make_async_copy(tl_in, tl, sems.at[1])
    cf.start()
    ct.start()
    tm = lax.axis_index("tm")
    llm = lax.axis_index("llm")
    off_a = (1 - tm % 2) * (FR - HALO)
    off_b = (FR - HALO) - off_a
    cg = pltpu.make_async_copy(grads, g_buf, sems.at[2])
    ca = pltpu.make_async_copy(
        audio.at[pl.ds(pl.multiple_of(off_a, 32), HALO)], send_a.at[pl.ds(0, HALO)], sems.at[3]
    )
    cb = pltpu.make_async_copy(
        audio.at[pl.ds(pl.multiple_of(off_b, 32), HALO)], send_b.at[pl.ds(0, HALO)], sems.at[4]
    )
    cg.start()
    ca.start()
    cb.start()
    cf.wait()
    ct.wait()
    starts, lives = routes(fc, tl, tm)
    row = lax.broadcasted_iota(jnp.int32, (LR, SLOTS), 0)
    slot = lax.broadcasted_iota(jnp.int32, (LR, SLOTS), 1) + llm * SLOTS
    starts = [pick(starts, llm ^ j) for j in range(NREC)]
    lives = [pick(lives, llm ^ j) for j in range(NREC)]
    picked = []
    for j in range(NREC):
        chosen = (row < lives[j]) & (slot == row + starts[j])
        picked.append(jnp.where(chosen, 1.0, 0.0).astype(BF))
    place = lax.broadcasted_iota(jnp.int32, (16, SLOTS), 0)
    slot = lax.broadcasted_iota(jnp.int32, (16, SLOTS), 1) + llm * SLOTS
    for offset in ((1 - tm % 2) * (LR - 4), (tm % 2) * (LR - 4)):
        r = place % 4 + offset
        chosen = jnp.zeros((16, SLOTS), F32)
        for j in range(NREC):
            hit = (place // 4 == (j + 3) % 4) & (r < lives[j]) & (slot == r + starts[j])
            chosen = jnp.where(hit, 1.0, chosen)
        picked.append(chosen.astype(BF))
    slot = lax.broadcasted_iota(jnp.int32, (SLOTS, NREC * LR), 0) + llm * SLOTS
    col = lax.broadcasted_iota(jnp.int32, (SLOTS, NREC * LR), 1)
    chosen = jnp.zeros((SLOTS, NREC * LR), F32)
    for j, apart in enumerate((0, 1, 3, 2)):
        r = col - j * LR
        hit = (r >= 0) & (r < LR) & (r < lives[apart]) & (slot == r + starts[apart])
        chosen = jnp.where(hit, 1.0, chosen)
    placing[...] = chosen.astype(BF)
    cg.wait()
    moved = dot(jnp.concatenate(picked, axis=0), g_buf[...]).astype(BF)
    own[...] = moved[:LR]
    pair[...] = moved[LR : 3 * LR]
    mate[...] = moved[3 * LR : 4 * LR]
    send_a[HALO:, :] = moved[4 * LR : 4 * LR + 16]
    send_b[HALO:, :] = moved[4 * LR + 16 :]
    ca.wait()
    cb.wait()


def norm_rows(x, gains, out, rows):
    inv = lax.rsqrt(jnp.mean(x * x, axis=-1, keepdims=True) + EPSILON)
    for c in range(NB):
        cols = slice(c * LANE, (c + 1) * LANE)
        out[rows, cols] = (x[:, cols] * inv * gains[c : c + 1, :]).astype(BF)


def project_own(
    after, audio, gains_in, w_key, w_value, x_o, gain_o, n_s, k_o, v_o, wk_o, wv_o, wkt_o, wvt_o, sems
):
    cx = pltpu.make_async_copy(audio, x_o, sems.at[0])
    cg = pltpu.make_async_copy(gains_in, gain_o, sems.at[1])
    loads = [
        pltpu.make_async_copy(w_key, wk_o, sems.at[2]),
        pltpu.make_async_copy(w_value, wv_o, sems.at[3]),
    ]
    for copy in [cx, cg] + loads:
        copy.start()
    cx.wait()
    cg.wait()
    for r in range(2):
        rows = slice(r * 64, r * 64 + 64)
        norm_rows(x_o[rows, :].astype(F32), gain_o, n_s, rows)
    for load, w_s, wt_s, out_s in zip(loads, (wk_o, wv_o), (wkt_o, wvt_o), (k_o, v_o)):
        load.wait()
        out_s[...] = dot(n_s[...], w_s[...]).astype(BF)
        wt_s[...] = w_s[...].T


def halves(first, second, lo):
    pair = [part.astype(F32)[lo : lo + 8] for part in (first, second)]
    return jnp.concatenate(pair, axis=0).astype(BF)


def stack_pair(after, pair, recv_a, recv_b, out):
    out[: 2 * LR, :] = pair[...]
    out[2 * LR :, :] = halves(recv_a[HALO:, :], recv_b[HALO:, :], 0)


def stack_mate(after, mate, got_pair, recv_a, recv_b, out):
    out[:LR, :] = mate[...] + got_pair[LR : 2 * LR, :]
    out[LR : LR + 16, :] = halves(recv_a[HALO:, :], recv_b[HALO:, :], 8)
    out[LR + 16 :, :] = got_pair[2 * LR :, :]


def stack_latents(after, first, second, out):
    out[:LR, :] = first[...]
    out[LR:, :] = second[...]


def head_mask(j, lo, hi):
    lane = lax.broadcasted_iota(jnp.int32, (1, (hi - lo) * LANE), 1) + lo * LANE
    return jnp.where((lane >= j * HEAD) & (lane < (j + 1) * HEAD), 1.0, 0.0).astype(BF)


def window(g, lo, hi):
    start = g * GROUP + lo * LANE
    return pl.ds(start if isinstance(start, int) else pl.multiple_of(start, LANE), (hi - lo) * LANE)


def add_tiles(tiles, lo, value):
    for t in range(value.shape[1] // LANE):
        part = value[:, t * LANE : (t + 1) * LANE]
        tiles[lo + t] = part if tiles[lo + t] is None else tiles[lo + t] + part


def attend(
    fc_in, w_query, w_out, recv_a, recv_b, x_own, n_own, gains, k_own, v_own, wk_s, wv_s,
    xq_o, q_s, k_s, v_s, p_s, att_s, wq_s, wo_s, fc, n_s, bias_s, sems,
):
    fc_copy = pltpu.make_async_copy(fc_in, fc, sems.at[0])
    fc_copy.start()
    load_q = pltpu.make_async_copy(w_query, wq_s, sems.at[1])
    load_q.start()
    load_o = pltpu.make_async_copy(w_out, wo_s, sems.at[2])
    tm = lax.axis_index("tm")
    llm = lax.axis_index("llm")
    even = tm % 2 == 0
    first = tm * FR
    total = lax.axis_size("tm") * FR

    @pl.when(even)
    def _():
        norm_rows(recv_b[:HALO, :].astype(F32), gains, n_s, slice(0, HALO))
        norm_rows(recv_a[:HALO, :].astype(F32), gains, n_s, slice(HALO, 2 * HALO))
        xq_o[0:32, :] = recv_b[64:96, :]
        xq_o[160:192, :] = recv_a[0:32, :]

    @pl.when(jnp.logical_not(even))
    def _():
        norm_rows(recv_a[:HALO, :].astype(F32), gains, n_s, slice(0, HALO))
        norm_rows(recv_b[:HALO, :].astype(F32), gains, n_s, slice(HALO, 2 * HALO))
        xq_o[0:32, :] = recv_a[64:96, :]
        xq_o[160:192, :] = recv_b[0:32, :]

    xq_o[32:160, :] = x_own[...]
    k_s[96:224, :] = k_own[...]
    v_s[96:224, :] = v_own[...]
    for w_s, out_s in ((wk_s, k_s), (wv_s, v_s)):
        @pl.loop(0, NC)
        def _(j, w_s=w_s, out_s=out_s):
            cols = lanes(j, COL)
            new = dot(n_s[...], w_s[:, cols]).astype(BF)
            out_s[0:96, cols] = new[0:96]
            out_s[224:320, cols] = new[96:192]

    queried = jnp.concatenate([n_s[64:96, :], n_own[...], n_s[96:128, :]], axis=0)
    load_q.wait()
    load_o.start()
    q_s[...] = dot(queried, wq_s[...]).astype(BF)

    fc_copy.wait()
    limit = fc[llm]

    def bias_of(rows, q_first, k_first):
        qe = lax.broadcasted_iota(jnp.int32, (rows, 256), 0) + q_first
        ke = lax.broadcasted_iota(jnp.int32, (rows, 256), 1) + k_first
        kt = ke + (first - HALO)
        ok = (ke >= qe - REACH) & (ke < qe + REACH) & (kt >= 0) & (kt < total) & ((kt < limit) | (ke == qe))
        return jnp.where(ok, 0.0, -1e30)

    bias_s[0:32, :] = bias_of(32, 64, 0)
    bias_s[32:160, :] = bias_of(FR, HALO, 32)
    bias_s[160:192, :] = bias_of(32, 224, 64)

    for base in range(0, HEADS, 16):
        some = [(h, h // 4, WINDOWS[h % 4]) for h in range(base, base + 16)]
        heads = []
        for h, g, (lo, hi) in some:
            q = q_s[:, window(g, lo, hi)] * head_mask(h % 4, lo, hi)
            k = k_s[:, window(g, lo, hi)]
            heads.append(
                jnp.concatenate(
                    [dot_t(q[0:32], k[0:256]), dot_t(q[32:160], k[32:288]), dot_t(q[160:192], k[64:320])], axis=0
                )
            )
        heads = [scores * SCALE + bias_s[...] for scores in heads]
        highest = [jnp.max(scores, axis=-1, keepdims=True) for scores in heads]
        heads = [jnp.exp(scores - top) for scores, top in zip(heads, highest)]
        inverse = [1.0 / jnp.sum(powers, axis=-1, keepdims=True) for powers in heads]
        heads = [(powers * inv).astype(BF) for powers, inv in zip(heads, inverse)]
        for g in range(base // 4, (base + 16) // 4):
            parts = [[None] * 3 for _ in range(3)]
            for (h, of, (lo, hi)), p in zip(some, heads):
                if of != g:
                    continue
                v = v_s[:, window(g, lo, hi)] * head_mask(h % 4, lo, hi)
                p_s[h] = p[32:160]
                add_tiles(parts[0], lo, dot(p[0:32], v[0:256]))
                add_tiles(parts[1], lo, dot(p[32:160], v[32:288]))
                add_tiles(parts[2], lo, dot(p[160:192], v[64:320]))
            for t in range(3):
                at = window(g, t, t + 1)
                att_s[0:32, at] = parts[0][t].astype(BF)
                att_s[32:160, at] = parts[1][t].astype(BF)
                att_s[160:192, at] = parts[2][t].astype(BF)

    load_o.wait()


def spoken_rows(fc, tm, llm):
    frame = lax.broadcasted_iota(jnp.int32, (QR, 1), 0) + (tm * FR - 32)
    return jnp.where((frame >= 0) & (frame < fc[llm]), 1.0, 0.0)


def convolve(
    fc_in, xq, att_s, wo_s, cg_in, lg_in, taps_in,
    lat_o, h_s, dsilu_s, pool_s, inv_o, cg_s, lg_s, tap_s, wot_s, fc, ci_s, up_s, norm_t, sems,
):
    copies = [
        pltpu.make_async_copy(source, into, sems.at[i])
        for i, (source, into) in enumerate(((fc_in, fc), (cg_in, cg_s), (lg_in, lg_s), (taps_in, tap_s)))
    ]
    for copy in copies:
        copy.start()
    tm = lax.axis_index("tm")
    llm = lax.axis_index("llm")

    def hidden_step(j, squares):
        cols = lanes(j, COL)
        h = dot(att_s[...], wo_s[:, cols]) + xq[:, cols].astype(F32)
        h = h.astype(BF).astype(F32)
        for t in range(COL // LANE):
            part = h[:, t * LANE : (t + 1) * LANE]
            h_s[j * (COL // LANE) + t] = part
            squares = squares + part * part
        return squares

    squares = lax.fori_loop(0, NC, hidden_step, jnp.zeros((QR, LANE), F32))
    inv_h = lax.rsqrt(jnp.sum(squares, axis=-1, keepdims=True) * (1.0 / D) + EPSILON)
    inv_o[...] = jnp.broadcast_to(inv_h, (QR, LANE))
    for copy in copies:
        copy.wait()
    inv_spoken = inv_h * spoken_rows(fc, tm, llm)

    def conv_step(c, squares):
        cols = lanes(c)
        wot_s[cols, :] = wo_s[:, cols].T
        ci_s[...] = (h_s[c] * inv_spoken * cg_s[pl.ds(c, 1), :]).astype(BF).astype(F32)
        kern = tap_s[:, cols]
        part = SR // 4
        for at in range(0, SR, part):
            acc = jnp.zeros((part, LANE), F32)
            for s in range(8):
                xs = ci_s[at + s : at + s + part + 24, :]
                for u in range(4):
                    m = s + 8 * u
                    acc = acc + kern[m : m + 1, :] * xs[8 * u : 8 * u + part]
            sig = 0.5 * jnp.tanh(0.5 * acc) + 0.5
            silu = acc * sig
            dsilu_s[c, at : at + part, :] = sig + silu * (1.0 - sig)
            up_s[at : at + part, :] = h_s[c, 16 + at : 16 + at + part, :] + silu
        pooled = up_s[pl.ds(0, PR, 4), :]
        for u in range(1, 4):
            pooled = pooled + up_s[pl.ds(u, PR, 4), :]
        pooled = pooled * 0.25
        pool_s[c] = pooled
        return squares + pooled * pooled

    squares = lax.fori_loop(0, NB, conv_step, jnp.zeros((PR, LANE), F32))
    inv_p = lax.rsqrt(jnp.sum(squares, axis=-1, keepdims=True) * (1.0 / D) + EPSILON)
    for c in range(NB):
        norm_t[...] = pool_s[c] * inv_p * lg_s[c : c + 1, :]
        lat_o[:, c * LANE : (c + 1) * LANE] = norm_t[4:36, :].astype(BF)


def convolve_back(
    fc_in, own, got_pair, got_mate, recv_a, recv_b, h_s, dsilu_s, pool_s, inv_s, cg_s, lg_s, tap_s, wot_s,
    dhid_s, datt_s, fc, g_s, up_s, ds_s, us_s, dnc_s, sems,
):
    copy = pltpu.make_async_copy(fc_in, fc, sems.at[0])
    copy.start()
    tm = lax.axis_index("tm")
    llm = lax.axis_index("llm")
    even = tm % 2 == 0

    row = lax.broadcasted_iota(jnp.int32, (PR, LR + 80), 0)
    col = lax.broadcasted_iota(jnp.int32, (PR, LR + 80), 1)
    is_left = row < 4
    is_right = row >= PR - 4
    r = jnp.where(is_left, row, row - (PR - 4))
    label = jnp.where(is_left, 1 - tm % 2, tm % 2)
    side = (
        (col == 44 + 16 * label + r) | (col == 64 + 8 * label + r)
        | (col == 80 + 8 * label + r) | (col == 100 + 8 * label + r)
    ) & (is_left | is_right)
    middle = (col < LR) & (col == row - 4)
    at = tm * LR + row - 4
    chosen = (side | middle) & (at >= 0) & (at < lax.axis_size("tm") * LR)
    chosen = jnp.where(chosen, 1.0, 0.0).astype(BF)
    stacked = jnp.concatenate(
        [
            own[...] + got_pair[:LR, :] + got_mate[:LR, :],
            recv_a[HALO:, :],
            recv_b[HALO:, :],
            got_pair[2 * LR :, :],
            got_mate[LR:, :],
        ],
        axis=0,
    )
    g_s[...] = dot(chosen, stacked)

    def sums(c, carry):
        squares, along = carry
        pooled = pool_s[c]
        return squares + pooled * pooled, along + g_s[:, lanes(c)] * lg_s[pl.ds(c, 1), :] * pooled

    zero = jnp.zeros((PR, LANE), F32)
    squares, along = lax.fori_loop(0, NB, sums, (zero, zero))
    inv_p = lax.rsqrt(jnp.sum(squares, axis=-1, keepdims=True) * (1.0 / D) + EPSILON)
    back_p = inv_p * inv_p * inv_p * (jnp.sum(along, axis=-1, keepdims=True) * (1.0 / D))
    inv_own = inv_s[32:160, :]
    copy.wait()
    spoken_own = spoken_rows(fc, tm, llm)[32:160]

    def conv_back(c, along):
        cols = lanes(c)
        gain = lg_s[pl.ds(c, 1), :]
        dpool = (g_s[:, cols] * gain * inv_p - pool_s[c] * back_p) * 0.25
        for u in range(4):
            up_s[pl.ds(u, PR, 4), :] = dpool
        ds_s[...] = up_s[...] * dsilu_s[c]
        us_s[c] = up_s[16 : 16 + FR, :]
        kern = tap_s[:, cols]
        part = FR // 4
        sums = []
        for at in range(0, FR, part):
            acc = jnp.zeros((part, LANE), F32)
            for s in range(8):
                base = 8 if s == 0 else s
                xs = ds_s[at + base : at + base + part + 24, :]
                for u in range(4):
                    m = 32 - base - 8 * u
                    acc = acc + kern[m : m + 1, :] * xs[8 * u : 8 * u + part]
            dn = acc.astype(BF).astype(F32) * spoken_own[at : at + part] * cg_s[pl.ds(c, 1), :]
            dnc_s[c, at : at + part, :] = dn
            sums.append(along[at : at + part] + dn * h_s[c, 32 + at : 32 + at + part, :])
        return jnp.concatenate(sums, axis=0)

    along = lax.fori_loop(0, NB, conv_back, jnp.zeros((FR, LANE), F32), unroll=2)
    back_h = inv_own * inv_own * inv_own * (jnp.sum(along, axis=-1, keepdims=True) * (1.0 / D))

    @pl.loop(0, NB)
    def _(c):
        dhid_s[:, lanes(c)] = (us_s[c] + dnc_s[c] * inv_own - h_s[c, 32:160, :] * back_h).astype(BF)

    @pl.loop(0, NC)
    def _(j):
        datt_s[:, lanes(j, COL)] = dot(dhid_s[...], wot_s[:, lanes(j, COL)]).astype(BF)


def attend_back(after, q_s, v_s, p_s, datt_s, wkt_s, wvt_s, send_a, send_b, ds_o, dk_s, dv_s, ek_s, ev_s):
    for base in range(0, HEADS, 16):
        some = [(h, h // 4, WINDOWS[h % 4]) for h in range(base, base + 16)]
        heads = []
        for h, g, (lo, hi) in some:
            win = window(g, lo, hi)
            heads.append(dot_t(datt_s[:, win] * head_mask(h % 4, lo, hi), v_s[32:288, win]))
        weights = [p_s[h].astype(F32) for h, _, _ in some]
        heads = [w * dp for w, dp in zip(weights, heads)]
        sums = [jnp.sum(pd, axis=-1, keepdims=True) for pd in heads]
        heads = [((pd - w * total) * SCALE).astype(BF) for pd, w, total in zip(heads, weights, sums)]
        for g in range(base // 4, (base + 16) // 4):
            dk, dv = [None] * 3, [None] * 3
            for (h, of, (lo, hi)), ds in zip(some, heads):
                if of != g:
                    continue
                win = window(g, lo, hi)
                mask = head_mask(h % 4, lo, hi)
                ds_o[h] = ds
                add_tiles(dk, lo, t_dot(ds, q_s[32:160, win] * mask))
                add_tiles(dv, lo, t_dot(p_s[h], datt_s[:, win] * mask))
            for t in range(3):
                at = window(g, t, t + 1)
                for out, edge, tiles in ((dk_s, ek_s, dk), (dv_s, ev_s, dv)):
                    new = tiles[t].astype(BF)
                    edge[0:64, at] = new[0:64]
                    out[:, at] = new[64:192]
                    edge[64:128, at] = new[192:256]

    even = lax.axis_index("tm") % 2 == 0

    @pl.loop(0, NC)
    def _(j):
        cols = lanes(j, COL)
        both = (dot(ek_s[...], wkt_s[:, cols]) + dot(ev_s[...], wvt_s[:, cols])).astype(BF)

        @pl.when(even)
        def _():
            send_a[:, cols] = both[64:128]
            send_b[:, cols] = both[0:64]

        @pl.when(jnp.logical_not(even))
        def _():
            send_a[:, cols] = both[0:64]
            send_b[:, cols] = both[64:128]


def project_back(
    after, ds_s, k_s, dk, dv, wq_s, wkt_s, wvt_s, x_s, gains, g_o, along_o, inv_o, dq_s,
):
    for g in range(4):
        dq = [None] * 3
        for j, (lo, hi) in enumerate(WINDOWS):
            add_tiles(dq, lo, dot(ds_s[g * 4 + j], k_s[32:288, window(g, lo, hi)] * head_mask(j, lo, hi)))
        for t in range(3):
            dq_s[:, window(g, t, t + 1)] = dq[t].astype(BF)
    dn = dot(dk[...], wkt_s[...]) + dot(dv[...], wvt_s[...]) + dot_t(dq_s[...], wq_s[...])
    squares = jnp.zeros((FR, LANE), F32)
    along = jnp.zeros((FR, LANE), F32)
    for c in range(NB):
        cols = slice(c * LANE, (c + 1) * LANE)
        x = x_s[:, cols].astype(F32)
        g = dn[:, cols] * gains[c : c + 1, :]
        g_o[:, cols] = g
        squares = squares + x * x
        along = along + g * x
    along_o[...] = along
    inv = lax.rsqrt(jnp.sum(squares, axis=-1, keepdims=True) * (1.0 / D) + EPSILON)
    inv_o[...] = jnp.broadcast_to(inv, (FR, LANE))


def place_rows(after, chosen, l0, l1, l23, rows_o):
    latents = jnp.concatenate([l0[...], l1[...], l23[...]], axis=0)
    rows_o[...] = dot(chosen[...], latents).astype(BF)


def finish(
    rows, x_s, dh_s, g_own, along_own, inv_s, recv_a, recv_b, gains, rows_out, grad_out, g_s, out_s, sems
):
    rows_copy = pltpu.make_async_copy(rows, rows_out, sems.at[2])
    rows_copy.start()
    tm = lax.axis_index("tm")
    odd = tm % 2
    one, none = jnp.float32(1.0), jnp.float32(0.0)
    copies = []
    for half in range(2):
        at = slice(half * 64, half * 64 + 64)
        keep_a = jnp.where(odd == 1 - half, one, none)
        inside = (tm > 0) & (tm < lax.axis_size("tm") - 1)
        keep_b = jnp.where((odd == half) & inside, one, none)
        along = along_own[at, :]
        for c in range(NB):
            cols = slice(c * LANE, (c + 1) * LANE)
            new = recv_a[:, cols].astype(F32) * keep_a + recv_b[:, cols].astype(F32) * keep_b
            new = new * gains[c : c + 1, :]
            g_s[at, cols] = g_own[at, cols] + new
            along = along + new * x_s[at, cols].astype(F32)
        inv = inv_s[at, :]
        back = inv * inv * inv * (jnp.sum(along, axis=-1, keepdims=True) * (1.0 / D))
        for c in range(NB):
            cols = slice(c * LANE, (c + 1) * LANE)
            x = x_s[at, cols].astype(F32)
            out_s[at, cols] = (dh_s[at, cols].astype(F32) + g_s[at, cols] * inv - x * back).astype(BF)
        copy = pltpu.make_async_copy(out_s.at[at], grad_out.at[at], sems.at[half])
        copy.start()
        copies.append(copy)
    for copy in copies + [rows_copy]:
        copy.wait()


def swap(count, cells_a, cells_b):
    pairs_a = [(i, i ^ 1) for i in range(count)]
    n = lax.axis_size("llm")
    full_b = []
    for i in range(count):
        partner = ((i + 1) ^ 1) - 1
        end = partner < 0 or partner >= count
        full_b += [(i * n + y, i * n + (y ^ 1) if end else partner * n + y) for y in range(n)]
    return lax.ppermute(cells_a, "tm", pairs_a), lax.ppermute(cells_b, ("tm", "llm"), full_b)


def trade(cells, apart):
    n = lax.axis_size("llm")
    return lax.ppermute(cells, "llm", [(i, i ^ apart) for i in range(n)])


def hbm(array):
    return pltpu.with_memory_space_constraint(array, pltpu.HBM)


def vmem(array):
    return pltpu.with_memory_space_constraint(array, pltpu.VMEM)


def call(kernel, ins, outs, scratch, flops, outs_in_hbm=False):
    place = {"h": hbm, "v": vmem, "n": lambda array: array}
    spec = {"h": ANY, "v": VMEM, "n": ANY}
    if outs_in_hbm:
        shapes = [jax.ShapeDtypeStruct(s, d) for s, d in outs]
    else:
        shapes = [pltpu.VMEM(s, d) for s, d in outs]
    return pl.pallas_call(
        kernel,
        out_shape=shapes,
        in_specs=[spec[kind] for kind, _ in ins],
        out_specs=[ANY if outs_in_hbm else VMEM] * len(outs),
        scratch_shapes=scratch,
        compiler_params=pltpu.CompilerParams(vmem_limit_bytes=12 * 1024 * 1024),
        cost_estimate=pl.CostEstimate(flops=flops, bytes_accessed=1_000_000, transcendentals=0),
        name=kernel.__name__,
    )(*[place[kind](array) for kind, array in ins])


def mark(kind, *arrays):
    return [(kind, array) for array in arrays]


def on_device(
    audio, frame_counts, text_lengths, norm_gain, w_query, w_key, w_value, w_out,
    conv_gain, conv_kernel, latent_gain, llm_grads,
):
    signal = audio[0]
    n_tm = lax.axis_size("tm")
    norm_row, conv_row, latent_row = (g.reshape(NB, LANE) for g in (norm_gain, conv_gain, latent_gain))
    tl_in = text_lengths.T
    V = pltpu.VMEM
    fc = pltpu.SMEM((NREC,), jnp.int32)
    tl = pltpu.SMEM((NREC, n_tm), jnp.int32)
    gain = ((NB, LANE), F32)
    weight = ((D, D), BF)

    def rows(n, dtype=BF):
        return ((n, D), dtype)

    def sems(*dims):
        return pltpu.SemaphoreType.DMA(dims)

    send_a, send_b, own, pair, mate, placing = call(
        prepare,
        mark("h", frame_counts, tl_in, signal, llm_grads[0]),
        [rows(HALO + 16), rows(HALO + 16), rows(LR), rows(2 * LR), rows(LR), ((SLOTS, NREC * LR), BF)],
        [fc, tl, V((SLOTS, D), BF), sems(5)],
        100_000_000,
    )
    recv_a, recv_b = swap(n_tm, send_a, send_b)
    x, gains, normed, k_own, v_own, wk, wv, wkt, wvt = call(
        project_own,
        mark("v", own) + mark("h", signal, norm_row, w_key, w_value),
        [rows(FR), gain, rows(FR), rows(FR), rows(FR), weight, weight, weight, weight],
        [sems(4)],
        6_000_000_000,
    )
    (pairs,) = call(stack_pair, mark("v", gains, pair, recv_a, recv_b), [rows(2 * LR + 16)], [], 1_000_000)
    got_pair = trade(pairs, 1)
    xq, q, k, v, p, att, wq, wo = call(
        attend,
        mark("h", frame_counts, w_query, w_out)
        + mark("v", recv_a, recv_b, x, normed, gains, k_own, v_own, wk, wv),
        [rows(QR), rows(QR), rows(EXT), rows(EXT), ((16, FR, 256), BF), rows(QR), weight, weight],
        [fc, V((2 * HALO, D), BF), V((QR, 256), F32), sems(3)],
        8_000_000_000,
    )
    (mates,) = call(stack_mate, mark("v", xq, mate, got_pair, recv_a, recv_b), [rows(LR + 32)], [], 1_000_000)
    got_mate = trade(mates, 3)
    latent, h, dsilu, pool, inv, cgain, lgain, taps, wot = call(
        convolve,
        mark("h", frame_counts) + mark("v", xq, att, wo) + mark("h", conv_row, latent_row, conv_kernel),
        [
            rows(LR), ((NB, QR, LANE), F32), ((NB, SR, LANE), F32), ((NB, PR, LANE), F32), ((QR, LANE), F32),
            gain, gain, rows(KERN, F32), weight,
        ],
        [fc, V((QR, LANE), F32), V((SR, LANE), F32), V((PR, LANE), F32), sems(4)],
        5_000_000_000,
    )
    latent_1 = trade(latent, 1)
    dhid, datt = call(
        convolve_back,
        mark("h", frame_counts)
        + mark("v", own, got_pair, got_mate, recv_a, recv_b, h, dsilu, pool, inv, cgain, lgain, taps, wot),
        [rows(FR), rows(FR)],
        [
            fc, V((PR, D), F32), V((SR, LANE), F32), V((SR, LANE), F32), V((NB, FR, LANE), F32),
            V((NB, FR, LANE), F32), sems(1),
        ],
        5_000_000_000,
    )
    (latents,) = call(stack_latents, mark("v", dhid, latent, latent_1), [rows(2 * LR)], [], 1_000_000)
    latent_23 = trade(latents, 3)
    back_a, back_b, ds, dk, dv = call(
        attend_back,
        mark("v", latents, q, v, p, datt, wkt, wvt),
        [rows(64), rows(64), ((16, FR, 256), BF), rows(FR), rows(FR)],
        [V((FR, D), BF), V((FR, D), BF)],
        6_000_000_000,
    )
    ret_a, ret_b = swap(n_tm, back_a, back_b)
    g_own, along, inv_x = call(
        project_back,
        mark("v", back_a, ds, k, dk, dv, wq, wkt, wvt, x, gains),
        [rows(FR, F32), ((FR, LANE), F32), ((FR, LANE), F32)],
        [V((FR, D), BF)],
        3_000_000_000,
    )
    (placed,) = call(
        place_rows,
        mark("v", along, placing, latent, latent_1, latent_23),
        [rows(SLOTS)],
        [],
        50_000_000,
    )
    out_rows, grad = call(
        finish,
        mark("v", placed, x, dhid, g_own, along, inv_x, ret_a, ret_b, gains),
        [rows(SLOTS), rows(FR)],
        [V((FR, D), F32), V((FR, D), BF), sems(3)],
        1_000_000_000,
        outs_in_hbm=True,
    )
    return (out_rows[None], grad[None])


def solution(mesh):
    placed = (P("llm", "tm", None),) + (P(),) * 10 + (P("tm", "llm", None),)
    return jax.shard_map(
        on_device,
        mesh=mesh,
        in_specs=placed,
        out_specs=(P("tm", "llm", None), P("llm", "tm", None)),
        check_vma=False,
    )
```
